32 devices in a mesh: fsdp: 32 (over z, y, x, core).
Axes of the slice: x: 2, y: 2, z: 4, core: 2. Of those that a mesh axis runs over, the one named last changes fastest.
Arguments:
- images: bfloat16 [96, 197, 384], P('fsdp'), may hold values from -6 to 6
- live_counts: int32 [96], P('fsdp'), may hold values from 0 to 1, as said below
- qkv_weight: bfloat16 [2, 442368], P(None, 'fsdp'), may hold values from -0.3125 to 0.3125
- out_weight: bfloat16 [2, 147456], P(None, 'fsdp'), may hold values from -2.5 to 2.5
- fc1_weight: bfloat16 [2, 589824], P(None, 'fsdp'), may hold values from -0.3125 to 0.3125
- fc2_weight: bfloat16 [2, 589824], P(None, 'fsdp'), may hold values from -0.21875 to 0.21875
- norm_gains: bfloat16 [2, 768], P(None, 'fsdp'), may hold values from 0.099609375 to 1.8984375
- biases: bfloat16 [2, 3840], P(None, 'fsdp'), may hold values from -3 to 3
- cotangent: bfloat16 [96, 197, 384], P('fsdp'), may hold values from -6 to 6
Outputs:
- activations: bfloat16 [96, 197, 384], P('fsdp')
- input_grad: bfloat16 [96, 197, 384], P('fsdp')
- qkv_grad: float32 [2, 442368], P(None, 'fsdp')
- out_grad: float32 [2, 147456], P(None, 'fsdp')
- fc1_grad: float32 [2, 589824], P(None, 'fsdp')
- fc2_grad: float32 [2, 589824], P(None, 'fsdp')
- gain_grad: float32 [2, 768], P(None, 'fsdp')
- bias_grad: float32 [2, 3840], P(None, 'fsdp')
The draws below stay inside these ranges and needn't reach their ends.
Inputs may be any that keep to these rules, and one draw needn't show every extreme that they name: Slot s of micro-batch b on device d is live when s < live_counts[d * 3 + b]; dead slots give zero outputs and no gradient. Some micro-batch is full in every draw.
All inputs are finite; a program needn't handle non-finite values.
Results may differ from the reference program's by a relative error of at most 0.015.
Values may be sent and summed in bfloat16 or wider, within the bound.
No kernel may reach another device: no remote copies, remote signals or barrier semaphores. Data moves between devices by JAX's collectives and lax.ppermute only.
A program may use at most 128 MiB of HBM per device.

```python
import jax
import jax.numpy as jnp
from jax import lax

D = 384
HEADS = 6
FF = 1536
SEQ = 197
HEAD = 64
LAYERS = 2
SLOTS = 1
IMAGES = 96


def draw_live_counts(key, part):
    key = jax.random.fold_in(key, 7)
    key_counts, key_place = jax.random.split(key)
    entries = IMAGES // SLOTS
    counts = jnp.minimum(jax.random.randint(key_counts, (entries,), 0, SLOTS + 2), SLOTS)
    full_index = jax.random.randint(key_place, (), 0, entries)
    return counts.at[full_index].set(SLOTS).astype(jnp.int32)


def shard_levels(stream_key, shape, cuts, least, top_value):
    loudness, own = 1.0, jax.random.fold_in(stream_key, 6)
    for dim, shards_of in cuts:
        heights = jnp.exp(jax.random.uniform(jax.random.fold_in(own, dim), (shards_of,), jnp.float32, least / len(cuts), top_value / len(cuts)))
        loudness = loudness * jnp.repeat(heights, shape[dim] // shards_of).reshape([-1 if axis == dim else 1 for axis in range(len(shape))])
    return loudness


def gaussian(rng, extent, scale, bound, cuts=(), kind=jnp.bfloat16):
    values = scale * jax.random.normal(rng, extent, jnp.float32)
    if cuts:
        values = values * shard_levels(rng, extent, cuts, -0.22, 0.18)
    return jnp.clip(values, -bound, bound).astype(kind)


def setup_inputs(seed: int = 0) -> dict:
    streams_of = jax.random.split(jax.random.key(seed), 10)
    images = gaussian(streams_of[0], (IMAGES, SEQ, D), 1.0, 6.0, ((0, 32),))
    live_counts = draw_live_counts(jax.random.fold_in(streams_of[9], 71), 0)
    qkv_weight = gaussian(streams_of[2], (LAYERS, 3 * D * D), D ** -0.5, 0.3125, ((1, 32),))
    out_weight = gaussian(streams_of[3], (LAYERS, D * D), (D // 64) ** -0.5, 2.5, ((1, 32),))
    fc1_weight = gaussian(streams_of[4], (LAYERS, D * FF), D ** -0.5, 0.3125, ((1, 32),))
    fc2_weight = gaussian(streams_of[5], (LAYERS, FF * D), (FF // 2) ** -0.5, 0.21875, ((1, 32),))
    norm_gains = jnp.clip(1.0 + 0.18 * jax.random.normal(streams_of[6], (LAYERS, 2 * D), jnp.float32), 0.099609375, 1.8984375).astype(jnp.bfloat16)
    biases = gaussian(streams_of[7], (LAYERS, 6 * D + FF), 0.5, 3.0, ((1, 32),))
    cotangent = gaussian(streams_of[8], (IMAGES, SEQ, D), 1.0, 6.0, ((0, 32),))
    return {"images": images, "live_counts": live_counts, "qkv_weight": qkv_weight, "out_weight": out_weight, "fc1_weight": fc1_weight, "fc2_weight": fc2_weight, "norm_gains": norm_gains, "biases": biases, "cotangent": cotangent}


@jax.custom_vjp
def low(v):
    return lax.optimization_barrier(v.astype(jnp.bfloat16)).astype(jnp.float32)

@jax.custom_vjp
def low_back(v):
    return v

def low_keep(v):
    return (low(v), None)

def low_pass(kept, grad):
    return (grad,)

def back_keep(v):
    return (v, None)

def back_low(kept, grad):
    return (low(grad),)
low.defvjp(low_keep, low_pass)
low_back.defvjp(back_keep, back_low)

def layer_norm(values, gain_row, shift_row):
    centre = lax.optimization_barrier(jnp.mean(values, axis=-1, keepdims=True))
    centred = values - centre
    spread = lax.optimization_barrier(jnp.mean(centred * centred, axis=-1, keepdims=True))
    return centred * lax.rsqrt(spread + 1e-06) * gain_row + shift_row

def project(values, matrix):
    return jnp.einsum('bsi,ij->bsj', values, matrix, precision=lax.Precision.HIGHEST)

def gelu_value(values):
    return 0.5 * values * (1.0 + lax.erf(values * 0.7071067811865476))

def vit_block(stream, qkv_mat, out_mat, fc1_mat, fc2_mat, gain_vec, shifts):
    image_count, seq_len = (stream.shape[0], stream.shape[1])
    normed = low(layer_norm(stream, gain_vec[:D], shifts[:D]))
    zeros_k = jnp.zeros((D,), jnp.float32)
    qkv_bias = jnp.concatenate([shifts[D:2 * D], zeros_k, shifts[2 * D:3 * D]])
    qkv_all = low_back(low(project(normed, qkv_mat) + qkv_bias))
    queries = qkv_all[..., :D].reshape(image_count, seq_len, HEADS, HEAD)
    keys_all = qkv_all[..., D:2 * D].reshape(image_count, seq_len, HEADS, HEAD)
    values_all = qkv_all[..., 2 * D:].reshape(image_count, seq_len, HEADS, HEAD)
    scores = low_back(jnp.einsum('bqhe,bkhe->bhqk', queries, keys_all, precision=lax.Precision.HIGHEST) * HEAD ** (-0.5))
    row_peak = lax.optimization_barrier(jnp.max(scores, axis=-1, keepdims=True))
    raised = jnp.exp(scores - row_peak)
    weights = low(raised / lax.optimization_barrier(jnp.sum(raised, axis=-1, keepdims=True)))
    mixed_heads = jnp.einsum('bhqk,bkhe->bqhe', weights, values_all, precision=lax.Precision.HIGHEST)
    mixed_heads = low_back(low(mixed_heads.reshape(image_count, seq_len, D)))
    branch = low_back(project(mixed_heads, out_mat) + shifts[3 * D:4 * D])
    middle = stream + branch
    normed_two = low(layer_norm(middle, gain_vec[D:], shifts[4 * D:5 * D]))
    hidden_pre = low_back(project(normed_two, fc1_mat) + shifts[6 * D:])
    hidden_act = low(gelu_value(hidden_pre))
    branch_two = low_back(project(hidden_act, fc2_mat) + shifts[5 * D:6 * D])
    return middle + branch_two

def forward(stream, params):
    qkv_all, out_all, fc1_all, fc2_all, gains_all, shifts_all = params
    for layer_idx in range(LAYERS):
        stream = vit_block(stream, qkv_all[layer_idx].reshape(D, 3 * D), out_all[layer_idx].reshape(D, D), fc1_all[layer_idx].reshape(D, FF), fc2_all[layer_idx].reshape(FF, D), gains_all[layer_idx], shifts_all[layer_idx])
    return stream

def reference(images, live_counts, qkv_weight, out_weight, fc1_weight, fc2_weight, norm_gains, biases, cotangent):
    params = (qkv_weight.astype(jnp.float32), out_weight.astype(jnp.float32), fc1_weight.astype(jnp.float32), fc2_weight.astype(jnp.float32), norm_gains.astype(jnp.float32), biases.astype(jnp.float32))
    slot_index = jnp.arange(IMAGES, dtype=jnp.int32) % SLOTS
    slot_live = slot_index < jnp.repeat(live_counts.astype(jnp.int32), SLOTS)
    live_mask = slot_live.astype(jnp.float32)
    per_group = 16
    group_total = IMAGES // per_group
    image_groups = images.reshape(group_total, per_group, SEQ, D)
    cot_groups = cotangent.reshape(group_total, per_group, SEQ, D)
    mask_groups = live_mask.reshape(group_total, per_group, 1, 1)

    def group_step(totals, pieces):
        image_part, cot_part, mask_part = pieces
        stream_in = image_part.astype(jnp.float32)
        result, pullback = jax.vjp(forward, stream_in, params)
        input_part, param_grads = pullback(cot_part.astype(jnp.float32) * mask_part)
        totals = jax.tree.map(jnp.add, totals, param_grads)
        outputs = ((result * mask_part).astype(jnp.bfloat16), input_part.astype(jnp.bfloat16))
        return (totals, outputs)
    zero_totals = jax.tree.map(jnp.zeros_like, params)
    totals, outputs = lax.scan(group_step, zero_totals, (image_groups, cot_groups, mask_groups))
    activations = outputs[0].reshape(IMAGES, SEQ, D)
    input_grad = outputs[1].reshape(IMAGES, SEQ, D)
    return (activations, input_grad, totals[0], totals[1], totals[2], totals[3], totals[4], totals[5])
```

```python
import jax
import jax.numpy as jnp
from jax import lax
from jax.experimental import pallas as pl
from jax.experimental.pallas import tpu as pltpu
from jax.sharding import PartitionSpec as P

D = 384
FF = 1536
SEQ = 197
HEAD = 64
LAYERS = 2
NORM_EPS = 1e-06
ROOT_HALF = 0.7071067811865476
INV_ROOT_TAU = 0.3989422804014327

IMGS = 3
ROWS = 208
R = IMGS * ROWS
CHUNK = 48
CHUNKS = R // CHUNK
PAIRS = 3

SLABS = 32
SLAB = 448
THIRD = 144
SMALL = 432
BLOCKS = 8
QUAD = 4 * SLAB
SHARD_BIAS = 120
SHARD_GAIN = 24
BIAS = 6 * D + FF
GAIN = 2 * D

F32 = jnp.float32
BF16 = jnp.bfloat16
VMEM_LIMIT = 56 * 1024 * 1024


def dot_nn(a, b):
    return lax.dot_general(a, b, (((1,), (0,)), ((), ())), preferred_element_type=F32)


def dot_nt(a, b):
    return lax.dot_general(a, b, (((1,), (1,)), ((), ())), preferred_element_type=F32)


def dot_tn(a, b):
    return lax.dot_general(a, b, (((0,), (0,)), ((), ())), preferred_element_type=F32)


def chunk_rows(i):
    return pl.ds(pl.multiple_of(i * CHUNK, CHUNK), CHUNK)


def block_rows(j):
    return pl.ds(pl.multiple_of(j * D, D), D)


def image_rows(i):
    return pl.ds(pl.multiple_of(i * ROWS, 16), ROWS)


def pair_lanes(p):
    return pl.ds(pl.multiple_of(p * 128, 128), 128)


def normalize(x):
    centred = x - jnp.mean(x, axis=-1, keepdims=True)
    inv_std = lax.rsqrt(jnp.mean(centred * centred, axis=-1, keepdims=True) + NORM_EPS)
    return centred * inv_std, inv_std


def digits(index, size):
    whole = jnp.floor((index.astype(F32) + 0.5) * (1.0 / size)).astype(jnp.int32)
    return whole, index - whole * size


def order_codes(shape, axis, low):
    index = lax.broadcasted_iota(jnp.int32, shape, axis)
    block, rest = digits(index, 48)
    dev, row = digits(rest, 12)
    return (block * 4 + dev) * 12 + row


def slab_codes(shape, axis, low):
    index = lax.broadcasted_iota(jnp.int32, shape, axis)
    rel, rest = digits(index, 96)
    block, row = digits(rest, 12)
    dev = jnp.bitwise_xor(rel, low)
    return (block * 4 + dev) * 12 + row


def owner_mask(size, per_owner):
    lane = lax.broadcasted_iota(jnp.int32, (1, size), 1)
    owner, place = digits(lane, per_owner)
    rows = lax.broadcasted_iota(jnp.int32, (SLABS, size), 0)
    return rows == owner, place


def place_matrix(place, size):
    rows = lax.broadcasted_iota(jnp.int32, (128, size), 0)
    return jnp.where(rows == place, 1.0, 0.0).astype(BF16)


def assemble(me, pieces, w, w2, bias_row, gain_row, rhs, small):
    low = jnp.bitwise_and(me, 3)
    order = jnp.where(
        order_codes((D, 1), 0, low) == slab_codes((1, D), 1, low), 1.0, 0.0
    ).astype(BF16)

    def group(zr, carry):
        for yr in range(2):
            g = jnp.bitwise_xor(lax.shift_right_logical(me, 2), yr + 2 * zr)
            for xr in range(2):
                for cr in range(2):
                    piece = pieces[cr * 4 + xr + 2 * yr]
                    d = jnp.bitwise_xor(me, cr + 2 * xr + 4 * yr + 8 * zr)
                    base = pl.multiple_of(zr * SLAB, 16)
                    s = xr * 2 + cr
                    for c in range(3):
                        lanes = slice(128 * c, 128 * c + 128)
                        rhs[96 * s : 96 * s + 96, lanes] = piece[pl.ds(base + c * THIRD, 96), :]
                        w2[pl.ds(pl.multiple_of(48 * d, 16), 48), lanes] = piece[
                            pl.ds(base + c * THIRD + 96, 48), :
                        ]
                    tail = piece[pl.ds(base + SMALL, 16), :].astype(F32)
                    small[0, pl.ds(d, 1), :] = tail[0:1, :]
                    small[1, pl.ds(d, 1), :] = tail[1:2, :]
            sorted_rows = dot_nn(order, rhs[...]).astype(BF16)
            for b in range(BLOCKS):
                w[b, pl.ds(pl.multiple_of(48 * g, 16), 48), :] = sorted_rows[48 * b : 48 * b + 48]
        return carry

    lax.fori_loop(0, 4, group, 0)
    for slot, size, per_owner, row in ((0, BIAS, SHARD_BIAS, bias_row), (1, GAIN, SHARD_GAIN, gain_row)):
        mine, place = owner_mask(size, per_owner)
        spread = dot_nn(small[slot].astype(BF16), place_matrix(place, size))
        row[...] = jnp.sum(jnp.where(mine, spread, 0.0), axis=0, keepdims=True)


def disperse(me, dw, dw2, bias_row, gain_row, keep, send, rhs, small):
    low = jnp.bitwise_and(me, 3)
    order = jnp.where(
        slab_codes((D, 1), 0, low) == order_codes((1, D), 1, low), 1.0, 0.0
    ).astype(BF16)
    for slot, size, per_owner, row in ((0, BIAS, SHARD_BIAS, bias_row), (1, GAIN, SHARD_GAIN, gain_row)):
        mine, place = owner_mask(size, per_owner)
        spread = jnp.where(mine, row[...], 0.0).astype(BF16)
        small[slot] = dot_nt(spread, place_matrix(place, size))
    head_row = lax.broadcasted_iota(jnp.int32, (16, 128), 0)

    def group(zr, carry):
        for yr in range(2):
            g = jnp.bitwise_xor(lax.shift_right_logical(me, 2), yr + 2 * zr)
            for b in range(BLOCKS):
                rhs[48 * b : 48 * b + 48, :] = dw[b, pl.ds(pl.multiple_of(48 * g, 16), 48), :]
            slabs = dot_nn(order, rhs[...]).astype(BF16)
            for xr in range(2):
                for cr in range(2):
                    out = send if cr else keep
                    d = jnp.bitwise_xor(me, cr + 2 * xr + 4 * yr + 8 * zr)
                    base = pl.multiple_of((xr + 2 * yr) * QUAD + zr * SLAB, 16)
                    s = xr * 2 + cr
                    for c in range(3):
                        lanes = slice(128 * c, 128 * c + 128)
                        out[pl.ds(base + c * THIRD, 96), :] = slabs[96 * s : 96 * s + 96, lanes]
                        out[pl.ds(base + c * THIRD + 96, 48), :] = dw2[
                            pl.ds(pl.multiple_of(48 * d, 16), 48), lanes
                        ]
                    tail = jnp.where(
                        head_row == 0,
                        small[0, pl.ds(d, 1), :],
                        jnp.where(head_row == 1, small[1, pl.ds(d, 1), :], 0.0),
                    )
                    out[pl.ds(base + SMALL, 16), :] = tail.astype(BF16)
        return carry

    lax.fori_loop(0, 4, group, 0)


def forward(x, w, w2, bias_row, gain_row, xna, qkv, probs, mixed, middle, xnb, act, slope, tmp):
    def norm_a(i, carry):
        rows = chunk_rows(i)
        normal, _ = normalize(x[rows, :])
        xna[rows, :] = (normal * gain_row[:, :D] + bias_row[:, :D]).astype(BF16)
        return carry

    lax.fori_loop(0, CHUNKS, norm_a, 0)
    for b in range(3):
        part = dot_nn(xna[...], w[b])
        if b == 0:
            part = part + bias_row[:, D : 2 * D]
        if b == 2:
            part = part + bias_row[:, 2 * D : 3 * D]
        qkv[b] = part.astype(BF16)

    lane = lax.broadcasted_iota(jnp.int32, (1, 128), 1)
    first = lane < HEAD
    halves = (first.astype(F32).astype(BF16), 1 - first.astype(F32).astype(BF16))
    real_key = lax.broadcasted_iota(jnp.int32, (1, ROWS), 1) < SEQ

    def image_attention(img, carry):
        rows = image_rows(img)

        def pair_attention(pair, inner):
            lanes = pair_lanes(pair)
            q, k, v = qkv[0, rows, lanes], qkv[1, rows, lanes], qkv[2, rows, lanes]
            outs = []
            for h in range(2):
                scores = dot_nt(q * halves[h], k) * (HEAD**-0.5)
                scores = jnp.where(real_key, scores, -1e30)
                raised = jnp.exp(scores - jnp.max(scores, axis=-1, keepdims=True))
                share = raised * (1.0 / jnp.sum(raised, axis=-1, keepdims=True))
                share = share.astype(BF16)
                probs[(img * PAIRS + pair) * 2 + h] = share
                outs.append(dot_nn(share, v))
            mixed[rows, lanes] = jnp.where(first, outs[0], outs[1]).astype(BF16)
            return inner

        return lax.fori_loop(0, PAIRS, pair_attention, carry)

    lax.fori_loop(0, IMGS, image_attention, 0)
    middle[...] = x[...] + (dot_nn(mixed[...], w[3]) + bias_row[:, 3 * D : 4 * D])

    def norm_b(i, carry):
        rows = chunk_rows(i)
        normal, _ = normalize(middle[rows, :])
        xnb[rows, :] = (normal * gain_row[:, D:] + bias_row[:, 4 * D : 5 * D]).astype(BF16)
        return carry

    lax.fori_loop(0, CHUNKS, norm_b, 0)

    def hidden(j, carry):
        tmp[...] = dot_nn(xnb[...], w[4 + j])
        shift = bias_row[:, pl.ds(pl.multiple_of(6 * D + j * D, 128), D)]

        def gelu(i, inner):
            rows = chunk_rows(i)
            pre = tmp[rows, :] + shift
            half = 0.5 * (1.0 + lax.erf(pre * ROOT_HALF))
            act[j, rows, :] = (pre * half).astype(BF16)
            slope[j, rows, :] = (half + pre * jnp.exp(-0.5 * pre * pre) * INV_ROOT_TAU).astype(BF16)
            return inner

        return lax.fori_loop(0, CHUNKS, gelu, carry)

    lax.fori_loop(0, 4, hidden, 0)
    tmp[...] = middle[...] + bias_row[:, 5 * D : 6 * D]
    for j in range(4):
        tmp[...] += dot_nn(act[j], w2[D * j : D * j + D, :])


def column_total(values):
    return jnp.sum(values.astype(F32), axis=0, keepdims=True)


def backward(
    x, w, w2, gain_row, xna, qkv, probs, mixed, middle, xnb, act, slope, grad, low, gpre, gqkv, gmix, tmp, dw, dw2, dbias, dgain
):
    low[...] = grad[...].astype(BF16)
    dbias[:, 5 * D : 6 * D] = column_total(low[...])

    def hidden(j, carry):
        dw2[block_rows(j), :] = dot_tn(act[j], low[...]).astype(BF16)
        pre = (dot_nt(low[...], w2[block_rows(j), :]) * slope[j].astype(F32)).astype(BF16)
        gpre[...] = pre
        dbias[:, pl.ds(pl.multiple_of(6 * D + j * D, 128), D)] = column_total(gpre[...])
        dw[4 + j] = dot_tn(xnb[...], gpre[...]).astype(BF16)
        part = dot_nt(gpre[...], w[4 + j])
        tmp[...] = jnp.where(j == 0, part, tmp[...] + part)
        return carry

    lax.fori_loop(0, 4, hidden, 0)

    def norm_back(source, gain, also_low):
        def step(i, totals):
            rows = chunk_rows(i)
            back = tmp[rows, :]
            normal, inv_std = normalize(source[rows, :])
            scaled = back * gain
            first_mean = jnp.mean(scaled, axis=-1, keepdims=True)
            cross_mean = jnp.mean(scaled * normal, axis=-1, keepdims=True)
            result = grad[rows, :] + inv_std * (scaled - first_mean - normal * cross_mean)
            grad[rows, :] = result
            result_low = result.astype(BF16)
            if also_low:
                low[rows, :] = result_low
            return (
                totals[0] + jnp.sum(back * normal, axis=0, keepdims=True),
                totals[1] + jnp.sum(back, axis=0, keepdims=True),
                totals[2] + jnp.sum(result_low.astype(F32), axis=0, keepdims=True),
            )

        zero = jnp.zeros((1, D), F32)
        return lax.fori_loop(0, CHUNKS, step, (zero, zero, zero))

    gain_two, shift_two, bias_out = norm_back(middle, gain_row[:, D:], True)
    dgain[:, D:] = gain_two
    dbias[:, 4 * D : 5 * D] = shift_two
    dbias[:, 3 * D : 4 * D] = bias_out
    dw[3] = dot_tn(mixed[...], low[...]).astype(BF16)
    gmix[...] = dot_nt(low[...], w[3]).astype(BF16)

    lane = lax.broadcasted_iota(jnp.int32, (1, 128), 1)
    first = lane < HEAD
    halves = (first.astype(F32).astype(BF16), 1 - first.astype(F32).astype(BF16))

    def image_attention(img, carry):
        rows = image_rows(img)

        def pair_attention(pair, inner):
            lanes = pair_lanes(pair)
            q, k, v = qkv[0, rows, lanes], qkv[1, rows, lanes], qkv[2, rows, lanes]
            gm = gmix[rows, lanes]
            grads = ([], [], [])
            for h in range(2):
                share = probs[(img * PAIRS + pair) * 2 + h]
                grad_share = dot_nt(gm * halves[h], v)
                full = share.astype(F32)
                row_dot = jnp.sum(full * grad_share, axis=-1, keepdims=True)
                grad_scores = (full * (grad_share - row_dot)).astype(BF16)
                grads[0].append(dot_nn(grad_scores, k) * (HEAD**-0.5))
                grads[1].append(dot_tn(grad_scores, q) * (HEAD**-0.5))
                grads[2].append(dot_tn(share, gm))
            for b in range(3):
                gqkv[b, rows, lanes] = jnp.where(first, grads[b][0], grads[b][1]).astype(BF16)
            return inner

        return lax.fori_loop(0, PAIRS, pair_attention, carry)

    lax.fori_loop(0, IMGS, image_attention, 0)
    for b in range(3):
        dw[b] = dot_tn(xna[...], gqkv[b]).astype(BF16)
        part = dot_nt(gqkv[b], w[b])
        tmp[...] = part if b == 0 else tmp[...] + part
    dbias[:, D : 2 * D] = column_total(gqkv[0])
    dbias[:, 2 * D : 3 * D] = column_total(gqkv[2])
    gain_one, shift_one, _ = norm_back(x, gain_row[:, :D], False)
    dgain[:, :D] = gain_one
    dbias[:, :D] = shift_one


def load_images(images, x):
    x[...] = jnp.zeros_like(x)
    for i in range(IMGS):
        x[ROWS * i : ROWS * i + SEQ, :] = images[i].astype(F32)


STATE = (
    ((R, D), BF16),
    ((3, R, D), BF16),
    ((IMGS * PAIRS * 2, ROWS, ROWS), BF16),
    ((R, D), BF16),
    ((R, D), F32),
    ((R, D), BF16),
    ((4, R, D), BF16),
    ((4, R, D), BF16),
)
WEIGHTS = (
    ((BLOCKS, D, D), BF16),
    ((FF, D), BF16),
    ((1, BIAS), F32),
    ((1, GAIN), F32),
)
GRAD_SCRATCH = (
    ((R, D), BF16),
    ((R, D), BF16),
    ((3, R, D), BF16),
    ((R, D), BF16),
    ((R, D), F32),
    ((BLOCKS, D, D), BF16),
    ((FF, D), BF16),
    ((1, BIAS), F32),
    ((1, GAIN), F32),
)
MOVE_SCRATCH = (((D, D), BF16), ((2, SLABS, 128), F32))
WIRE = jax.ShapeDtypeStruct((4 * QUAD, 128), BF16)


def shapes(specs):
    return [jax.ShapeDtypeStruct(*spec) for spec in specs]


def scratch(specs):
    return [pltpu.VMEM(*spec) for spec in specs]


def first_forward_kernel(*refs):
    me, images, pieces, refs = refs[0][0], refs[1], refs[2:10], refs[10:]
    stream, weights, state = refs[0], refs[1:5], refs[5:13]
    x, rhs, small = refs[13:]
    assemble(me, pieces, *weights, rhs, small)
    load_images(images, x)
    forward(x, *weights, *state, stream)


def second_layer_kernel(*refs):
    me, live, stream, cotangent, pieces, refs = refs[0][0], refs[1], refs[2], refs[3], refs[4:12], refs[12:]
    activations, grad, keep, send = refs[:4]
    weights, state, back, (rhs, small) = refs[4:8], refs[8:16], refs[16:25], refs[25:]
    assemble(me, pieces, *weights, rhs, small)
    forward(stream, *weights, *state, grad)
    for i in range(IMGS):
        alive = jnp.where(live[i] > 0, 1.0, 0.0)
        activations[i] = (grad[ROWS * i : ROWS * i + SEQ, :] * alive).astype(BF16)
    load_images(cotangent, grad)
    for i in range(IMGS):
        alive = jnp.where(live[i] > 0, 1.0, 0.0)
        grad[ROWS * i : ROWS * i + ROWS, :] = grad[ROWS * i : ROWS * i + ROWS, :] * alive
    w, w2, _, gain_row = weights
    backward(stream, w, w2, gain_row, *state, grad, *back)
    disperse(me, *back[5:], keep, send, rhs, small)


def first_backward_kernel(*refs):
    me, images, grad_in, refs = refs[0][0], refs[1], refs[2], refs[3:]
    weights, state, refs = refs[:3], refs[3:11], refs[11:]
    input_grad, keep, send = refs[:3]
    x, grad, back, (rhs, small) = refs[3], refs[4], refs[5:14], refs[14:]
    load_images(images, x)
    grad[...] = grad_in[...]
    backward(x, *weights, *state, grad, *back)
    for i in range(IMGS):
        input_grad[i] = grad[ROWS * i : ROWS * i + SEQ, :].astype(BF16)
    disperse(me, *back[5:], keep, send, rhs, small)


def whole(count):
    return [pl.BlockSpec(memory_space=pltpu.VMEM)] * count


def scalar(count):
    return [pl.BlockSpec(memory_space=pltpu.SMEM)] * count


def params():
    return pltpu.CompilerParams(vmem_limit_bytes=VMEM_LIMIT)


def cost(flops):
    return pl.CostEstimate(flops=flops, bytes_accessed=20_000_000, transcendentals=0)


def run_first_forward(me, images, pieces):
    outs = [jax.ShapeDtypeStruct((R, D), F32)] + shapes(WEIGHTS) + shapes(STATE)
    out = pl.pallas_call(
        first_forward_kernel,
        out_shape=outs,
        in_specs=scalar(1) + whole(9),
        out_specs=whole(len(outs)),
        scratch_shapes=scratch((((R, D), F32),) + MOVE_SCRATCH),
        compiler_params=params(),
        cost_estimate=cost(8_000_000_000),
        name="first_forward",
    )(me, images, *pieces)
    return out[0], out[1:5], out[5:]


def run_second_layer(me, live, stream, cotangent, pieces):
    outs = [jax.ShapeDtypeStruct(cotangent.shape, BF16), jax.ShapeDtypeStruct((R, D), F32), WIRE, WIRE]
    return pl.pallas_call(
        second_layer_kernel,
        out_shape=outs,
        in_specs=scalar(2) + whole(10),
        out_specs=whole(len(outs)),
        scratch_shapes=scratch(WEIGHTS + STATE + GRAD_SCRATCH + MOVE_SCRATCH),
        compiler_params=params(),
        cost_estimate=cost(24_000_000_000),
        name="second_layer",
    )(me, live, stream, cotangent, *pieces)


def run_first_backward(me, images, grad, weights, state):
    w, w2, _, gain_row = weights
    outs = [jax.ShapeDtypeStruct(images.shape, BF16), WIRE, WIRE]
    return pl.pallas_call(
        first_backward_kernel,
        out_shape=outs,
        in_specs=scalar(1) + whole(13),
        out_specs=whole(len(outs)),
        scratch_shapes=scratch((((R, D), F32), ((R, D), F32)) + GRAD_SCRATCH + MOVE_SCRATCH),
        compiler_params=params(),
        cost_estimate=cost(16_000_000_000),
        name="first_backward",
    )(me, images, grad, w, w2, gain_row, *state)


def chunk_table():
    table = []
    for c in range(3):
        for i in range(12):
            for b in range(3):
                table.append((0, i * 9 + b * 3 + c, c * THIRD + b * 12 + i))
            table.append((1, i * 3 + c, c * THIRD + 36 + i))
            for b in range(4):
                table.append((2, i * 12 + b * 3 + c, c * THIRD + 48 + b * 12 + i))
        for i in range(48):
            table.append((3, i * 3 + c, c * THIRD + 96 + i))
    return table


def pack_kernel(qkv, out, fc1, fc2, gains, biases, slab_a, slab_b, stage):
    flats = (qkv, out, fc1, fc2)
    stage[...] = jnp.zeros_like(stage)
    for which, piece, row in chunk_table():
        both = flats[which][:, 128 * piece : 128 * piece + 128].astype(F32)
        stage[0, row : row + 1, :] = both[0:1]
        stage[1, row : row + 1, :] = both[1:2]
    for layer in range(LAYERS):
        stage[layer, SMALL : SMALL + 1, 0:SHARD_BIAS] = biases[...].astype(F32)[layer : layer + 1]
        stage[layer, SMALL + 1 : SMALL + 2, 0:SHARD_GAIN] = gains[...].astype(F32)[layer : layer + 1]
    slab_a[...] = stage[0].astype(BF16)
    slab_b[...] = stage[1].astype(BF16)


def run_pack(qkv, out, fc1, fc2, gains, biases):
    return pl.pallas_call(
        pack_kernel,
        out_shape=[jax.ShapeDtypeStruct((SLAB, 128), BF16)] * 2,
        in_specs=whole(6),
        out_specs=whole(2),
        scratch_shapes=[pltpu.VMEM((2, SLAB, 128), F32)],
        name="pack",
    )(qkv, out, fc1, fc2, gains, biases)


def unpack_kernel(slab_a, slab_b, qkv, out, fc1, fc2, gains, biases):
    flats = (qkv, out, fc1, fc2)
    for which, piece, row in chunk_table():
        lanes = slice(128 * piece, 128 * piece + 128)
        flats[which][0:1, lanes] = slab_a[row : row + 1, :]
        flats[which][1:2, lanes] = slab_b[row : row + 1, :]
    for layer, slab in enumerate((slab_a, slab_b)):
        biases[layer : layer + 1, :] = slab[SMALL : SMALL + 1, 0:SHARD_BIAS]
        gains[layer : layer + 1, :] = slab[SMALL + 1 : SMALL + 2, 0:SHARD_GAIN]


def run_unpack(slab_a, slab_b, widths):
    return pl.pallas_call(
        unpack_kernel,
        out_shape=[jax.ShapeDtypeStruct((LAYERS, width), F32) for width in widths],
        in_specs=whole(2),
        out_specs=whole(6),
        name="unpack",
    )(slab_a, slab_b)


def swap(value, bits):
    return lax.ppermute(value, "fsdp", [(i, i ^ bits) for i in range(SLABS)])


def gather_tree(slab):
    quad = jnp.concatenate([slab] + [swap(slab, 8 * z) for z in (1, 2, 3)], axis=0)
    near = [quad] + [swap(quad, 2 * xy) for xy in (1, 2, 3)]
    return near + [swap(part, 1) for part in near]


def scatter_tree(keep, send):
    got = swap(send, 1)
    total = keep.astype(F32) + got.astype(F32)
    parts = [total[QUAD * xy : QUAD * xy + QUAD] for xy in range(4)]
    mine = parts[0]
    for xy in (1, 2, 3):
        mine = mine + swap(parts[xy].astype(BF16), 2 * xy).astype(F32)
    slabs = [mine[SLAB * z : SLAB * z + SLAB] for z in range(4)]
    total = slabs[0]
    for z in (1, 2, 3):
        total = total + swap(slabs[z].astype(BF16), 8 * z).astype(F32)
    return total


def to_slabs(qkv, out, fc1, fc2, gains, biases):
    blocks = jnp.concatenate(
        [
            qkv.reshape(SLABS, 12, 3, D).transpose(0, 2, 1, 3).reshape(SLABS, 36, D),
            out.reshape(SLABS, 12, D),
            fc1.reshape(SLABS, 12, 4, D).transpose(0, 2, 1, 3).reshape(SLABS, 48, D),
            fc2.reshape(SLABS, 48, D),
        ],
        axis=1,
    )
    thirds = blocks.reshape(SLABS, THIRD, 3, 128).transpose(0, 2, 1, 3).reshape(SLABS, SMALL, 128)
    tail = jnp.zeros((SLABS, SLAB - SMALL, 128), blocks.dtype)
    tail = tail.at[:, 0, :SHARD_BIAS].set(biases.reshape(SLABS, SHARD_BIAS))
    tail = tail.at[:, 1, :SHARD_GAIN].set(gains.reshape(SLABS, SHARD_GAIN))
    return jnp.concatenate([thirds, tail], axis=1)


def from_slabs(slabs):
    blocks = slabs[:, :SMALL].reshape(SLABS, 3, THIRD, 128).transpose(0, 2, 1, 3).reshape(SLABS, THIRD, D)
    return (
        blocks[:, :36].reshape(SLABS, 3, 12, D).transpose(0, 2, 1, 3).reshape(-1),
        blocks[:, 36:48].reshape(-1),
        blocks[:, 48:96].reshape(SLABS, 4, 12, D).transpose(0, 2, 1, 3).reshape(-1),
        blocks[:, 96:].reshape(-1),
        slabs[:, SMALL + 1, :SHARD_GAIN].reshape(-1),
        slabs[:, SMALL, :SHARD_BIAS].reshape(-1),
    )


def slab_number(core, xy, z):
    return core + 2 * xy + 8 * z


def plain_pieces(flats, layer):
    slabs = to_slabs(*(lax.all_gather(flat[layer], "fsdp", axis=0, tiled=True) for flat in flats))
    return [
        jnp.concatenate([slabs[slab_number(core, xy, z)] for z in range(4)], axis=0)
        for core in range(2)
        for xy in range(4)
    ]


def plain_totals(keep, send):
    halves = [half.reshape(4, 4, SLAB, 128).astype(F32) for half in (keep, send)]
    slabs = jnp.stack([halves[d & 1][(d >> 1) & 3, d >> 3] for d in range(SLABS)])
    return [lax.psum_scatter(flat, "fsdp", scatter_dimension=0, tiled=True) for flat in from_slabs(slabs)]


def local(images, live_counts, qkv_weight, out_weight, fc1_weight, fc2_weight, norm_gains, biases, cotangent):
    flats = (qkv_weight, out_weight, fc1_weight, fc2_weight, norm_gains, biases)
    tree = lax.axis_size("fsdp") == SLABS
    if tree:
        me = lax.axis_index("fsdp").astype(jnp.int32).reshape(1)
        slab_a, slab_b = run_pack(*flats)
        pieces_a, pieces_b = gather_tree(slab_a), gather_tree(slab_b)
    else:
        me = jnp.zeros((1,), jnp.int32)
        pieces_a, pieces_b = plain_pieces(flats, 0), plain_pieces(flats, 1)
    stream, weights, state = run_first_forward(me, images, pieces_a)
    activations, grad, keep_b, send_b = run_second_layer(me, live_counts, stream, cotangent, pieces_b)
    input_grad, keep_a, send_a = run_first_backward(me, images, grad, weights, state)
    if tree:
        total_b, total_a = scatter_tree(keep_b, send_b), scatter_tree(keep_a, send_a)
        results = run_unpack(total_a, total_b, [flat.shape[1] for flat in flats])
    else:
        results = [jnp.stack(both) for both in zip(plain_totals(keep_a, send_a), plain_totals(keep_b, send_b))]
    return (activations, input_grad, *results)


def solution(mesh):
    flat = P(None, "fsdp")
    image = P("fsdp", None, None)
    return jax.shard_map(
        local,
        mesh=mesh,
        in_specs=(image, P("fsdp")) + (flat,) * 6 + (image,),
        out_specs=(image, image) + (flat,) * 6,
        check_vma=False,
    )
```

```python
import jax
import jax.numpy as jnp
from jax import lax
from jax.experimental import pallas as pl
from jax.experimental.pallas import tpu as pltpu
from jax.sharding import PartitionSpec as P

D = 384
FF = 1536
SEQ = 197
HEAD = 64
LAYERS = 2
NORM_EPS = 1e-06
ROOT_HALF = 0.7071067811865476
INV_ROOT_TAU = 0.3989422804014327

IMGS = 3
ROWS = 208
R = IMGS * ROWS
CHUNK = 48
CHUNKS = R // CHUNK
PAIRS = 3

SLABS = 32
THIRD = 144
SMALL = 2 * THIRD
MAIN = SMALL + 16
SIDE = THIRD
BLOCKS = 8
SHARD_BIAS = 120
SHARD_GAIN = 24
BIAS = 6 * D + FF
GAIN = 2 * D

F32 = jnp.float32
BF16 = jnp.bfloat16
VMEM_LIMIT = 56 * 1024 * 1024


def dot_nn(a, b):
    return lax.dot_general(a, b, (((1,), (0,)), ((), ())), preferred_element_type=F32)


def dot_nt(a, b):
    return lax.dot_general(a, b, (((1,), (1,)), ((), ())), preferred_element_type=F32)


def dot_tn(a, b):
    return lax.dot_general(a, b, (((0,), (0,)), ((), ())), preferred_element_type=F32)


def chunk_rows(i):
    return pl.ds(pl.multiple_of(i * CHUNK, CHUNK), CHUNK)


def block_rows(j):
    return pl.ds(pl.multiple_of(j * D, D), D)


def image_rows(i):
    return pl.ds(pl.multiple_of(i * ROWS, 16), ROWS)


def pair_lanes(p):
    return pl.ds(pl.multiple_of(p * 128, 128), 128)


def normalize(x):
    centred = x - jnp.mean(x, axis=-1, keepdims=True)
    inv_std = lax.rsqrt(jnp.mean(centred * centred, axis=-1, keepdims=True) + NORM_EPS)
    return centred * inv_std, inv_std


def digits(index, size):
    whole = jnp.floor((index.astype(F32) + 0.5) * (1.0 / size)).astype(jnp.int32)
    return whole, index - whole * size


def order_codes(shape, axis):
    index = lax.broadcasted_iota(jnp.int32, shape, axis)
    block, rest = digits(index, 48)
    dev, row = digits(rest, 12)
    return (block * 4 + dev) * 12 + row


def slab_codes(shape, axis, low, blocks):
    index = lax.broadcasted_iota(jnp.int32, shape, axis)
    rel, rest = digits(index, 12 * blocks)
    block, row = digits(rest, 12)
    dev = jnp.bitwise_xor(rel, low)
    return (block * 4 + dev) * 12 + row


def owner_mask(size, per_owner):
    lane = lax.broadcasted_iota(jnp.int32, (1, size), 1)
    owner, place = digits(lane, per_owner)
    rows = lax.broadcasted_iota(jnp.int32, (SLABS, size), 0)
    return rows == owner, place


def place_matrix(place, size):
    rows = lax.broadcasted_iota(jnp.int32, (128, size), 0)
    return jnp.where(rows == place, 1.0, 0.0).astype(BF16)


def assemble(me, pieces, w, w2, bias_row, gain_row, rhs, small):
    low = jnp.bitwise_and(me, 3)
    order = jnp.where(
        order_codes((D, 1), 0) == slab_codes((1, D), 1, low, BLOCKS), 1.0, 0.0
    ).astype(BF16)

    for zr in range(4):
        for yr in range(2):
            g = jnp.bitwise_xor(lax.shift_right_logical(me, 2), yr + 2 * zr)
            for xr in range(2):
                for cr in range(2):
                    xy = xr + 2 * yr
                    main, side = pieces[4 * cr + xy], pieces[8 + 4 * cr + zr]
                    d = jnp.bitwise_xor(me, cr + 2 * xy + 8 * zr)
                    s = xr * 2 + cr
                    for c in range(3):
                        lanes = slice(128 * c, 128 * c + 128)
                        piece = main if c else side
                        base = zr * MAIN + (c - 1) * THIRD if c else xy * SIDE
                        rhs[96 * s : 96 * s + 96, lanes] = piece[base : base + 96, :]
                        w2[pl.ds(pl.multiple_of(48 * d, 16), 48), lanes] = piece[base + 96 : base + THIRD, :]
                    tail = main[zr * MAIN + SMALL : zr * MAIN + MAIN, :].astype(F32)
                    small[0, pl.ds(d, 1), :] = tail[0:1, :]
                    small[1, pl.ds(d, 1), :] = tail[1:2, :]
            sorted_rows = dot_nn(order, rhs[...]).astype(BF16)
            for b in range(BLOCKS):
                w[b, pl.ds(pl.multiple_of(48 * g, 16), 48), :] = sorted_rows[48 * b : 48 * b + 48]
    for slot, size, per_owner, row in ((0, BIAS, SHARD_BIAS, bias_row), (1, GAIN, SHARD_GAIN, gain_row)):
        mine, place = owner_mask(size, per_owner)
        spread = dot_nn(small[slot].astype(BF16), place_matrix(place, size))
        row[...] = jnp.sum(jnp.where(mine, spread, 0.0), axis=0, keepdims=True)


def main_rows(blocks, with_w2, with_small):
    return 2 * side_rows(blocks, with_w2) + 16 * with_small


def side_rows(blocks, with_w2):
    return 12 * blocks + 48 * with_w2


def disperse(me, dw, dw2, bias_row, gain_row, wires, rhs, small):
    blocks = dw.shape[0]
    size = 48 * blocks
    third = side_rows(blocks, dw2 is not None)
    stride = main_rows(blocks, dw2 is not None, bias_row is not None)
    low = jnp.bitwise_and(me, 3)
    order = jnp.where(
        slab_codes((size, 1), 0, low, blocks) == order_codes((1, size), 1), 1.0, 0.0
    ).astype(BF16)
    if bias_row is not None:
        for slot, width, per_owner, row in ((0, BIAS, SHARD_BIAS, bias_row), (1, GAIN, SHARD_GAIN, gain_row)):
            mine, place = owner_mask(width, per_owner)
            spread = jnp.where(mine, row[...], 0.0).astype(BF16)
            small[slot] = dot_nt(spread, place_matrix(place, width))
    head_row = lax.broadcasted_iota(jnp.int32, (16, 128), 0)

    def group(zr, carry):
        for yr in range(2):
            g = jnp.bitwise_xor(lax.shift_right_logical(me, 2), yr + 2 * zr)
            for b in range(blocks):
                rhs[48 * b : 48 * b + 48, :] = dw[b, pl.ds(pl.multiple_of(48 * g, 16), 48), :]
            slabs = dot_nn(order, rhs[0:size, :]).astype(BF16)
            for xr in range(2):
                for cr in range(2):
                    main, side = wires[2 * cr : 2 * cr + 2]
                    xy = xr + 2 * yr
                    d = jnp.bitwise_xor(me, cr + 2 * xy + 8 * zr)
                    s = xr * 2 + cr
                    base = pl.multiple_of(xy * (4 * stride) + zr * stride, 16)
                    for c in range(3):
                        lanes = slice(128 * c, 128 * c + 128)
                        if c:
                            out, start = main, base + (c - 1) * third
                        else:
                            out, start = side, pl.multiple_of(zr * (4 * third) + xy * third, 16)
                        rows = 12 * blocks
                        out[pl.ds(start, rows), :] = slabs[rows * s : rows * s + rows, lanes]
                        if dw2 is not None:
                            out[pl.ds(start + rows, 48), :] = dw2[pl.ds(pl.multiple_of(48 * d, 16), 48), lanes]
                    if bias_row is not None:
                        tail = jnp.where(
                            head_row == 0,
                            small[0, pl.ds(d, 1), :],
                            jnp.where(head_row == 1, small[1, pl.ds(d, 1), :], 0.0),
                        )
                        main[pl.ds(base + 2 * third, 16), :] = tail.astype(BF16)
        return carry

    lax.fori_loop(0, 4, group, 0)


def forward(x, w, w2, bias_row, gain_row, xna, qkv, probs, mixed, middle, xnb, act, slope, tmp):
    def norm_a(i, carry):
        rows = chunk_rows(i)
        normal, _ = normalize(x[rows, :])
        xna[rows, :] = (normal * gain_row[:, :D] + bias_row[:, :D]).astype(BF16)
        return carry

    lax.fori_loop(0, CHUNKS, norm_a, 0)
    for b in range(3):
        part = dot_nn(xna[...], w[b])
        if b == 0:
            part = part + bias_row[:, D : 2 * D]
        if b == 2:
            part = part + bias_row[:, 2 * D : 3 * D]
        qkv[b] = part.astype(BF16)

    lane = lax.broadcasted_iota(jnp.int32, (1, 128), 1)
    first = lane < HEAD
    halves = (first.astype(F32).astype(BF16), 1 - first.astype(F32).astype(BF16))
    real_key = lax.broadcasted_iota(jnp.int32, (1, ROWS), 1) < SEQ

    def image_attention(img, carry):
        rows = image_rows(img)

        def pair_attention(pair, inner):
            lanes = pair_lanes(pair)
            q, k, v = qkv[0, rows, lanes], qkv[1, rows, lanes], qkv[2, rows, lanes]
            outs = []
            for h in range(2):
                scores = dot_nt(q * halves[h], k) * (HEAD**-0.5)
                scores = jnp.where(real_key, scores, -1e30)
                raised = jnp.exp(scores - jnp.max(scores, axis=-1, keepdims=True))
                share = raised * (1.0 / jnp.sum(raised, axis=-1, keepdims=True))
                share = share.astype(BF16)
                probs[(img * PAIRS + pair) * 2 + h] = share
                outs.append(dot_nn(share, v))
            mixed[rows, lanes] = jnp.where(first, outs[0], outs[1]).astype(BF16)
            return inner

        return lax.fori_loop(0, PAIRS, pair_attention, carry)

    lax.fori_loop(0, IMGS, image_attention, 0)
    middle[...] = x[...] + (dot_nn(mixed[...], w[3]) + bias_row[:, 3 * D : 4 * D])

    def norm_b(i, carry):
        rows = chunk_rows(i)
        normal, _ = normalize(middle[rows, :])
        xnb[rows, :] = (normal * gain_row[:, D:] + bias_row[:, 4 * D : 5 * D]).astype(BF16)
        return carry

    lax.fori_loop(0, CHUNKS, norm_b, 0)

    def hidden(j, carry):
        tmp[...] = dot_nn(xnb[...], w[4 + j])
        shift = bias_row[:, pl.ds(pl.multiple_of(6 * D + j * D, 128), D)]

        def gelu(i, inner):
            rows = chunk_rows(i)
            pre = tmp[rows, :] + shift
            half = 0.5 * (1.0 + lax.erf(pre * ROOT_HALF))
            act[j, rows, :] = (pre * half).astype(BF16)
            slope[j, rows, :] = (half + pre * jnp.exp(-0.5 * pre * pre) * INV_ROOT_TAU).astype(BF16)
            return inner

        return lax.fori_loop(0, CHUNKS, gelu, carry)

    lax.fori_loop(0, 4, hidden, 0)
    tmp[...] = middle[...] + bias_row[:, 5 * D : 6 * D]
    for j in range(4):
        tmp[...] += dot_nn(act[j], w2[D * j : D * j + D, :])


def column_total(values):
    return jnp.sum(values.astype(F32), axis=0, keepdims=True)


def norm_back(source, gain, grad, tmp, low):
    def step(i, totals):
        rows = chunk_rows(i)
        back = tmp[rows, :]
        normal, inv_std = normalize(source[rows, :])
        scaled = back * gain
        first_mean = jnp.mean(scaled, axis=-1, keepdims=True)
        cross_mean = jnp.mean(scaled * normal, axis=-1, keepdims=True)
        result = grad[rows, :] + inv_std * (scaled - first_mean - normal * cross_mean)
        grad[rows, :] = result
        result_low = result.astype(BF16)
        if low is not None:
            low[rows, :] = result_low
        return (
            totals[0] + jnp.sum(back * normal, axis=0, keepdims=True),
            totals[1] + jnp.sum(back, axis=0, keepdims=True),
            totals[2] + jnp.sum(result_low.astype(F32), axis=0, keepdims=True),
        )

    zero = jnp.zeros((1, D), F32)
    return lax.fori_loop(0, CHUNKS, step, (zero, zero, zero))


def mlp_backward(w, w2, gain_row, mixed, middle, xnb, act, slope, grad, low, gpre, gmix, tmp, dw, dw_out, dw2, dbias, dgain):
    low[...] = grad[...].astype(BF16)
    dbias[:, 5 * D : 6 * D] = column_total(low[...])

    def hidden(j, carry):
        dw2[block_rows(j), :] = dot_tn(act[j], low[...]).astype(BF16)
        pre = (dot_nt(low[...], w2[block_rows(j), :]) * slope[j].astype(F32)).astype(BF16)
        gpre[...] = pre
        dbias[:, pl.ds(pl.multiple_of(6 * D + j * D, 128), D)] = column_total(gpre[...])
        dw[j] = dot_tn(xnb[...], gpre[...]).astype(BF16)
        part = dot_nt(gpre[...], w[4 + j])
        tmp[...] = jnp.where(j == 0, part, tmp[...] + part)
        return carry

    lax.fori_loop(0, 4, hidden, 0)
    gain_two, shift_two, bias_out = norm_back(middle, gain_row[:, D:], grad, tmp, low)
    dgain[:, D:] = gain_two
    dbias[:, 4 * D : 5 * D] = shift_two
    dbias[:, 3 * D : 4 * D] = bias_out
    dw_out[...] = dot_tn(mixed[...], low[...]).astype(BF16)
    gmix[...] = dot_nt(low[...], w[3]).astype(BF16)


def attention_backward(x, w, gain_row, xna, qkv, probs, grad, gqkv, gmix, tmp, dw, dbias, dgain):
    lane = lax.broadcasted_iota(jnp.int32, (1, 128), 1)
    first = lane < HEAD
    halves = (first.astype(F32).astype(BF16), 1 - first.astype(F32).astype(BF16))

    def image_attention(img, carry):
        rows = image_rows(img)

        def pair_attention(pair, inner):
            lanes = pair_lanes(pair)
            q, k, v = qkv[0, rows, lanes], qkv[1, rows, lanes], qkv[2, rows, lanes]
            gm = gmix[rows, lanes]
            grads = ([], [], [])
            for h in range(2):
                share = probs[(img * PAIRS + pair) * 2 + h]
                grad_share = dot_nt(gm * halves[h], v)
                full = share.astype(F32)
                row_dot = jnp.sum(full * grad_share, axis=-1, keepdims=True)
                grad_scores = (full * (grad_share - row_dot)).astype(BF16)
                grads[0].append(dot_nn(grad_scores, k) * (HEAD**-0.5))
                grads[1].append(dot_tn(grad_scores, q) * (HEAD**-0.5))
                grads[2].append(dot_tn(share, gm))
            for b in range(3):
                gqkv[b, rows, lanes] = jnp.where(first, grads[b][0], grads[b][1]).astype(BF16)
            return inner

        return lax.fori_loop(0, PAIRS, pair_attention, carry)

    lax.fori_loop(0, IMGS, image_attention, 0)
    for b in range(3):
        dw[b] = dot_tn(xna[...], gqkv[b]).astype(BF16)
        part = dot_nt(gqkv[b], w[b])
        tmp[...] = part if b == 0 else tmp[...] + part
    dbias[:, D : 2 * D] = column_total(gqkv[0])
    dbias[:, 2 * D : 3 * D] = column_total(gqkv[2])
    gain_one, shift_one, _ = norm_back(x, gain_row[:, :D], grad, tmp, None)
    dgain[:, :D] = gain_one
    dbias[:, :D] = shift_one


def load_images(images, x):
    x[...] = jnp.zeros_like(x)
    for i in range(IMGS):
        x[ROWS * i : ROWS * i + SEQ, :] = images[i].astype(F32)


STATE = (
    ((R, D), BF16),
    ((3, R, D), BF16),
    ((IMGS * PAIRS * 2, ROWS, ROWS), BF16),
    ((R, D), BF16),
    ((R, D), F32),
    ((R, D), BF16),
    ((4, R, D), BF16),
    ((4, R, D), BF16),
)
WEIGHTS = (
    ((BLOCKS, D, D), BF16),
    ((FF, D), BF16),
    ((1, BIAS), F32),
    ((1, GAIN), F32),
)
BIAS_ROW = ((1, BIAS), F32)
GAIN_ROW = ((1, GAIN), F32)
HALF_BLOCKS = ((BLOCKS // 2, D, D), BF16)
MOVE_SCRATCH = (((D, D), BF16), ((2, SLABS, 128), F32))


def wires(blocks, with_w2, with_small):
    rows = (main_rows(blocks, with_w2, with_small), side_rows(blocks, with_w2))
    return [jax.ShapeDtypeStruct((16 * count, 128), BF16) for count in rows] * 2


def shapes(specs):
    return [jax.ShapeDtypeStruct(*spec) for spec in specs]


def scratch(specs):
    return [pltpu.VMEM(*spec) for spec in specs]


def first_forward_kernel(*refs):
    me, images, pieces, refs = refs[0][0], refs[1], refs[2:18], refs[18:]
    stream, weights, state = refs[0], refs[1:5], refs[5:13]
    x, rhs, small = refs[13:]
    assemble(me, pieces, *weights, rhs, small)
    load_images(images, x)
    forward(x, *weights, *state, stream)


def second_layer_kernel(*refs):
    me, live, stream, cotangent, pieces, refs = refs[0][0], refs[1], refs[2], refs[3], refs[4:20], refs[20:]
    activations, grad, sent, refs = refs[0], refs[1], refs[2:6], refs[6:]
    weights, state, refs = refs[:4], refs[4:12], refs[12:]
    low, gpre, gqkv, gmix, tmp, dw, dw2, dbias, dgain, rhs, small = refs
    assemble(me, pieces, *weights, rhs, small)
    forward(stream, *weights, *state, grad)
    for i in range(IMGS):
        alive = jnp.where(live[i] > 0, 1.0, 0.0)
        activations[i] = (grad[ROWS * i : ROWS * i + SEQ, :] * alive).astype(BF16)
    load_images(cotangent, grad)
    for i in range(IMGS):
        alive = jnp.where(live[i] > 0, 1.0, 0.0)
        grad[ROWS * i : ROWS * i + ROWS, :] = grad[ROWS * i : ROWS * i + ROWS, :] * alive
    w, w2, _, gain_row = weights
    xna, qkv, probs, mixed, middle, xnb, act, slope = state
    mlp_backward(
        w, w2, gain_row, mixed, middle, xnb, act, slope, grad, low, gpre, gmix, tmp, dw.at[4:8], dw.at[3], dw2, dbias, dgain
    )
    attention_backward(stream, w, gain_row, xna, qkv, probs, grad, gqkv, gmix, tmp, dw, dbias, dgain)
    disperse(me, dw, dw2, dbias, dgain, sent, rhs, small)


def first_mlp_backward_kernel(
    me, grad_in, w, w2, gain_row, mixed, middle, xnb, act, slope, grad, gmix, dw_out, dbias, dgain, *refs
):
    sent, (low, gpre, tmp, dw, dw2, rhs) = refs[:4], refs[4:]
    grad[...] = grad_in[...]
    dbias[...] = jnp.zeros_like(dbias)
    dgain[...] = jnp.zeros_like(dgain)
    mlp_backward(
        w, w2, gain_row, mixed, middle, xnb, act, slope, grad, low, gpre, gmix, tmp, dw, dw_out, dw2, dbias, dgain
    )
    disperse(me[0], dw, dw2, None, None, sent, rhs, None)


def first_attention_backward_kernel(
    me, images, grad_in, gmix, dw_out, dbias_in, dgain_in, w, gain_row, xna, qkv, probs, input_grad, *refs
):
    sent, (x, grad, gqkv, tmp, dw, dbias, dgain, rhs, small) = refs[:4], refs[4:]
    load_images(images, x)
    grad[...] = grad_in[...]
    dbias[...] = dbias_in[...]
    dgain[...] = dgain_in[...]
    dw[3] = dw_out[...]
    attention_backward(x, w, gain_row, xna, qkv, probs, grad, gqkv, gmix, tmp, dw, dbias, dgain)
    for i in range(IMGS):
        input_grad[i] = grad[ROWS * i : ROWS * i + SEQ, :].astype(BF16)
    disperse(me[0], dw, None, dbias, dgain, sent, rhs, small)


def whole(count):
    return [pl.BlockSpec(memory_space=pltpu.VMEM)] * count


def scalar(count):
    return [pl.BlockSpec(memory_space=pltpu.SMEM)] * count


def params():
    return pltpu.CompilerParams(vmem_limit_bytes=VMEM_LIMIT)


def cost(flops):
    return pl.CostEstimate(flops=flops, bytes_accessed=20_000_000, transcendentals=0)


def run_first_forward(me, images, pieces):
    outs = [jax.ShapeDtypeStruct((R, D), F32)] + shapes(WEIGHTS) + shapes(STATE)
    out = pl.pallas_call(
        first_forward_kernel,
        out_shape=outs,
        in_specs=scalar(1) + whole(17),
        out_specs=whole(len(outs)),
        scratch_shapes=scratch((((R, D), F32),) + MOVE_SCRATCH),
        compiler_params=params(),
        cost_estimate=cost(33_000_000_000),
        name="first_forward",
    )(me, images, *pieces)
    return out[0], out[1:5], out[5:]


def run_second_layer(me, live, stream, cotangent, pieces):
    outs = [jax.ShapeDtypeStruct(cotangent.shape, BF16), jax.ShapeDtypeStruct((R, D), F32)]
    outs += wires(BLOCKS, True, True)
    low, full = ((R, D), BF16), ((R, D), F32)
    back = (low, low, ((3, R, D), BF16), low, full, ((BLOCKS, D, D), BF16), ((FF, D), BF16), BIAS_ROW, GAIN_ROW)
    return pl.pallas_call(
        second_layer_kernel,
        out_shape=outs,
        in_specs=scalar(2) + whole(18),
        out_specs=whole(len(outs)),
        scratch_shapes=scratch(WEIGHTS + STATE + back + MOVE_SCRATCH),
        compiler_params=params(),
        cost_estimate=cost(65_000_000_000),
        name="second_layer",
    )(me, live, stream, cotangent, *pieces)


def run_first_mlp_backward(me, grad, weights, state):
    w, w2, _, gain_row = weights
    low, full = ((R, D), BF16), ((R, D), F32)
    outs = shapes((full, low, ((D, D), BF16), BIAS_ROW, GAIN_ROW)) + wires(BLOCKS // 2, True, False)
    return pl.pallas_call(
        first_mlp_backward_kernel,
        out_shape=outs,
        in_specs=scalar(1) + whole(9),
        out_specs=whole(len(outs)),
        scratch_shapes=scratch((low, low, full, HALF_BLOCKS, ((FF, D), BF16), MOVE_SCRATCH[0])),
        compiler_params=params(),
        cost_estimate=cost(20_000_000_000),
        name="first_mlp_backward",
    )(me, grad, w, w2, gain_row, *state[3:])


def run_first_attention_backward(me, images, grads, weights, state):
    w, _, _, gain_row = weights
    low, full = ((R, D), BF16), ((R, D), F32)
    outs = [jax.ShapeDtypeStruct(images.shape, BF16)] + wires(BLOCKS // 2, False, True)
    back = (full, full, ((3, R, D), BF16), full, HALF_BLOCKS, BIAS_ROW, GAIN_ROW)
    return pl.pallas_call(
        first_attention_backward_kernel,
        out_shape=outs,
        in_specs=scalar(1) + whole(11),
        out_specs=whole(len(outs)),
        scratch_shapes=scratch(back + MOVE_SCRATCH),
        compiler_params=params(),
        cost_estimate=cost(20_000_000_000),
        name="first_attention_backward",
    )(me, images, *grads, w, gain_row, *state[:3])


def chunk_table():
    table = []
    for c in range(3):
        for i in range(12):
            for b in range(3):
                table.append((0, i * 9 + b * 3 + c, c, b * 12 + i))
            table.append((1, i * 3 + c, c, 36 + i))
            for b in range(4):
                table.append((2, i * 12 + b * 3 + c, c, 48 + b * 12 + i))
        for i in range(48):
            table.append((3, i * 3 + c, c, 96 + i))
    return table


def pack_kernel(qkv, out, fc1, fc2, gains, biases, *refs):
    flats, slabs, stages = (qkv, out, fc1, fc2), refs[:4], refs[4:]
    for stage in stages:
        stage[...] = jnp.zeros_like(stage)
    for which, piece, c, row in chunk_table():
        both = flats[which][:, 128 * piece : 128 * piece + 128].astype(F32)
        row += max(c - 1, 0) * THIRD
        for layer in range(LAYERS):
            stages[2 * layer + (c == 0)][row : row + 1, :] = both[layer : layer + 1]
    for layer in range(LAYERS):
        main = stages[2 * layer]
        main[SMALL : SMALL + 1, 0:SHARD_BIAS] = biases[...].astype(F32)[layer : layer + 1]
        main[SMALL + 1 : SMALL + 2, 0:SHARD_GAIN] = gains[...].astype(F32)[layer : layer + 1]
    for slab, stage in zip(slabs, stages):
        slab[...] = stage[...].astype(BF16)


def run_pack(qkv, out, fc1, fc2, gains, biases):
    sizes = [(MAIN, 128), (SIDE, 128)] * LAYERS
    return pl.pallas_call(
        pack_kernel,
        out_shape=[jax.ShapeDtypeStruct(size, BF16) for size in sizes],
        in_specs=whole(6),
        out_specs=whole(4),
        scratch_shapes=[pltpu.VMEM(size, F32) for size in sizes],
        name="pack",
    )(qkv, out, fc1, fc2, gains, biases)


def unpack_kernel(*refs):
    attention, mlp, second, flats, (gains, biases) = refs[:2], refs[2:4], refs[4:6], refs[6:10], refs[10:]
    for which, piece, c, row in chunk_table():
        lanes = slice(128 * piece, 128 * piece + 128)
        place = max(c - 1, 0)
        source, at = (attention, place * 48 + row) if which < 2 else (mlp, place * 96 + row - 48)
        flats[which][0:1, lanes] = source[c == 0][at : at + 1, :]
        at = place * THIRD + row
        flats[which][1:2, lanes] = second[c == 0][at : at + 1, :]
    for layer, (main, row) in enumerate(((attention[0], 96), (second[0], SMALL))):
        biases[layer : layer + 1, :] = main[row : row + 1, 0:SHARD_BIAS]
        gains[layer : layer + 1, :] = main[row + 1 : row + 2, 0:SHARD_GAIN]


def run_unpack(slabs, widths):
    return pl.pallas_call(
        unpack_kernel,
        out_shape=[jax.ShapeDtypeStruct((LAYERS, width), F32) for width in widths],
        in_specs=whole(6),
        out_specs=whole(6),
        name="unpack",
    )(*slabs)


def swap(value, bits):
    return lax.ppermute(value, "fsdp", [(i, i ^ bits) for i in range(SLABS)])


XY_STEPS = (2, 4, 6)
Z_STEPS = (8, 16, 24)


def spread(value, steps):
    return [value] + [swap(value, bits) for bits in steps]


def gather_first(main, side):
    return (
        jnp.concatenate(spread(main, Z_STEPS), axis=0),
        jnp.concatenate(spread(side, XY_STEPS), axis=0),
    )


def gather_second(main, side):
    return spread(main, XY_STEPS) + spread(side, Z_STEPS)


def gather_cores(near):
    far = [swap(part, 1) for part in near]
    return near[:4] + far[:4] + near[4:] + far[4:]


def collect(total, steps):
    rows = total.shape[0] // 4
    mine = total[:rows]
    for place, bits in enumerate(steps):
        part = total[rows * (place + 1) : rows * (place + 2)]
        mine = mine + swap(part.astype(BF16), bits).astype(F32)
    return mine


def scatter_cores(wires):
    return [keep.astype(F32) + swap(send, 1).astype(F32) for keep, send in zip(wires[:2], wires[2:])]


def scatter_first(main, side):
    return [collect(main, XY_STEPS), collect(side, Z_STEPS)]


def scatter_second(main, side):
    return [collect(main, Z_STEPS), collect(side, XY_STEPS)]


def to_slabs(qkv, out, fc1, fc2, gains, biases):
    blocks = jnp.concatenate(
        [
            qkv.reshape(SLABS, 12, 3, D).transpose(0, 2, 1, 3).reshape(SLABS, 36, D),
            out.reshape(SLABS, 12, D),
            fc1.reshape(SLABS, 12, 4, D).transpose(0, 2, 1, 3).reshape(SLABS, 48, D),
            fc2.reshape(SLABS, 48, D),
        ],
        axis=1,
    )
    thirds = blocks.reshape(SLABS, THIRD, 3, 128).transpose(0, 2, 1, 3).reshape(SLABS, 3 * THIRD, 128)
    tail = jnp.zeros((SLABS, MAIN - SMALL, 128), blocks.dtype)
    tail = tail.at[:, 0, :SHARD_BIAS].set(biases.reshape(SLABS, SHARD_BIAS))
    tail = tail.at[:, 1, :SHARD_GAIN].set(gains.reshape(SLABS, SHARD_GAIN))
    return jnp.concatenate([thirds[:, THIRD:], tail], axis=1), thirds[:, :THIRD]


def from_slabs(main, side):
    blocks = jnp.concatenate([side, main[:, :SMALL]], axis=1).reshape(SLABS, 3, THIRD, 128).transpose(0, 2, 1, 3).reshape(SLABS, THIRD, D)
    return (
        blocks[:, :36].reshape(SLABS, 3, 12, D).transpose(0, 2, 1, 3).reshape(-1),
        blocks[:, 36:48].reshape(-1),
        blocks[:, 48:96].reshape(SLABS, 4, 12, D).transpose(0, 2, 1, 3).reshape(-1),
        blocks[:, 96:].reshape(-1),
        main[:, SMALL + 1, :SHARD_GAIN].reshape(-1),
        main[:, SMALL, :SHARD_BIAS].reshape(-1),
    )


def plain_pieces(flats, layer):
    main, side = to_slabs(*(lax.all_gather(flat[layer], "fsdp", axis=0, tiled=True) for flat in flats))
    mains, sides = [], []
    for core in range(2):
        for xy in range(4):
            mains.append(jnp.concatenate([main[core + 2 * xy + 8 * z] for z in range(4)], axis=0))
        for z in range(4):
            sides.append(jnp.concatenate([side[core + 2 * xy + 8 * z] for xy in range(4)], axis=0))
    return mains + sides


def plain_slabs(sent):
    mains, sides = ([wire.reshape(4, 4, -1, 128).astype(F32) for wire in sent[part::2]] for part in range(2))
    main = jnp.stack([mains[d & 1][(d >> 1) & 3, d >> 3] for d in range(SLABS)])
    side = jnp.stack([sides[d & 1][d >> 3, (d >> 1) & 3] for d in range(SLABS)])
    return main, side


def plain_totals(main, side):
    return [lax.psum_scatter(flat, "fsdp", scatter_dimension=0, tiled=True) for flat in from_slabs(main, side)]


def joined_slabs(attention, mlp):
    (main, side), (mlp_main, mlp_side) = plain_slabs(attention), plain_slabs(mlp)
    parts = [main[:, :48], mlp_main[:, :96], main[:, 48:96], mlp_main[:, 96:], main[:, 96:]]
    return jnp.concatenate(parts, axis=1), jnp.concatenate([side, mlp_side], axis=1)


def local(images, live_counts, qkv_weight, out_weight, fc1_weight, fc2_weight, norm_gains, biases, cotangent):
    flats = (qkv_weight, out_weight, fc1_weight, fc2_weight, norm_gains, biases)
    tree = lax.axis_size("fsdp") == SLABS
    if tree:
        me = lax.axis_index("fsdp").astype(jnp.int32).reshape(1)
        main_a, side_a, main_b, side_b = run_pack(*flats)
        first_a = gather_first(main_a, side_a)
        first_a, main_b, side_b = lax.optimization_barrier((first_a, main_b, side_b))
        second_a = gather_second(*first_a)
        first_b = gather_first(main_b, side_b)
        second_a, first_b = lax.optimization_barrier((second_a, first_b))
        pieces_a = gather_cores(second_a)
    else:
        me = jnp.zeros((1,), jnp.int32)
        pieces_a, pieces_b = plain_pieces(flats, 0), plain_pieces(flats, 1)
    stream, weights, state = run_first_forward(me, images, pieces_a)
    if tree:
        second_b, stream = lax.optimization_barrier((gather_second(*first_b), stream))
        pieces_b = gather_cores(second_b)
    activations, grad, *wires_b = run_second_layer(me, live_counts, stream, cotangent, pieces_b)
    if not tree:
        *grads, m0, m1, m2, m3 = run_first_mlp_backward(me, grad, weights, state)
        input_grad, *wires_a = run_first_attention_backward(me, images, grads, weights, state)
        totals_a = plain_totals(*joined_slabs(wires_a, (m0, m1, m2, m3)))
        results = [jnp.stack(both) for both in zip(totals_a, plain_totals(*plain_slabs(wires_b)))]
    else:
        sums_b = scatter_cores(wires_b)
        *grads, m0, m1, m2, m3 = run_first_mlp_backward(me, grad, weights, state)
        sums_b, grads, wires_m = lax.optimization_barrier((sums_b, grads, (m0, m1, m2, m3)))
        halves_b, sums_m = scatter_first(*sums_b), scatter_cores(wires_m)
        input_grad, *wires_a = run_first_attention_backward(me, images, grads, weights, state)
        halves_b, sums_m, wires_a = lax.optimization_barrier((halves_b, sums_m, wires_a))
        slabs_b, halves_m, sums_a = scatter_second(*halves_b), scatter_first(*sums_m), scatter_cores(wires_a)
        slabs_a, slabs_m = scatter_second(*scatter_first(*sums_a)), scatter_second(*halves_m)
        results = run_unpack(slabs_a + slabs_m + slabs_b, [flat.shape[1] for flat in flats])
    return (activations, input_grad, *results)


def solution(mesh):
    flat = P(None, "fsdp")
    image = P("fsdp", None, None)
    return jax.shard_map(
        local,
        mesh=mesh,
        in_specs=(image, P("fsdp")) + (flat,) * 6 + (image,),
        out_specs=(image, image) + (flat,) * 6,
        check_vma=False,
    )
```

```python
import jax
import jax.numpy as jnp
from jax import lax
from jax.experimental import pallas as pl
from jax.experimental.pallas import tpu as pltpu
from jax.sharding import PartitionSpec as P

D = 384
FF = 1536
SEQ = 197
HEAD = 64
LAYERS = 2
NORM_EPS = 1e-06
ROOT_HALF = 0.7071067811865476
INV_ROOT_TAU = 0.3989422804014327

IMGS = 3
ROWS = 208
R = IMGS * ROWS
CHUNK = 48
CHUNKS = R // CHUNK
PAIRS = 3

SLABS = 32
THIRD = 144
SMALL = 3 * THIRD
SLAB = SMALL + 16
BLOCKS = 8
SHARD_BIAS = 120
SHARD_GAIN = 24
BIAS = 6 * D + FF
GAIN = 2 * D

F32 = jnp.float32
BF16 = jnp.bfloat16
VMEM_LIMIT = 56 * 1024 * 1024


def dot_nn(a, b):
    return lax.dot_general(a, b, (((1,), (0,)), ((), ())), preferred_element_type=F32)


def dot_nt(a, b):
    return lax.dot_general(a, b, (((1,), (1,)), ((), ())), preferred_element_type=F32)


def dot_tn(a, b):
    return lax.dot_general(a, b, (((0,), (0,)), ((), ())), preferred_element_type=F32)


def chunk_rows(i):
    return pl.ds(pl.multiple_of(i * CHUNK, CHUNK), CHUNK)


def block_rows(j):
    return pl.ds(pl.multiple_of(j * D, D), D)


def image_rows(i):
    return pl.ds(pl.multiple_of(i * ROWS, 16), ROWS)


def pair_lanes(p):
    return pl.ds(pl.multiple_of(p * 128, 128), 128)


def normalize(x):
    centred = x - jnp.mean(x, axis=-1, keepdims=True)
    inv_std = lax.rsqrt(jnp.mean(centred * centred, axis=-1, keepdims=True) + NORM_EPS)
    return centred * inv_std, inv_std


def digits(index, size):
    whole = jnp.floor((index.astype(F32) + 0.5) * (1.0 / size)).astype(jnp.int32)
    return whole, index - whole * size


def order_codes(shape, axis):
    index = lax.broadcasted_iota(jnp.int32, shape, axis)
    block, rest = digits(index, 48)
    dev, row = digits(rest, 12)
    return (block * 4 + dev) * 12 + row


def slab_codes(shape, axis, low, blocks):
    index = lax.broadcasted_iota(jnp.int32, shape, axis)
    rel, rest = digits(index, 12 * blocks)
    block, row = digits(rest, 12)
    dev = jnp.bitwise_xor(rel, low)
    return (block * 4 + dev) * 12 + row


def owner_mask(size, per_owner):
    lane = lax.broadcasted_iota(jnp.int32, (1, size), 1)
    owner, place = digits(lane, per_owner)
    rows = lax.broadcasted_iota(jnp.int32, (SLABS, size), 0)
    return rows == owner, place


def place_matrix(place, size):
    rows = lax.broadcasted_iota(jnp.int32, (128, size), 0)
    return jnp.where(rows == place, 1.0, 0.0).astype(BF16)


def assemble(me, place, w, w2, bias_row, gain_row, rhs, small):
    low = jnp.bitwise_and(me, 3)
    order = jnp.where(
        order_codes((D, 1), 0) == slab_codes((1, D), 1, low, BLOCKS), 1.0, 0.0
    ).astype(BF16)

    for zr in range(4):
        for yr in range(2):
            g = jnp.bitwise_xor(lax.shift_right_logical(me, 2), yr + 2 * zr)
            for xr in range(2):
                for cr in range(2):
                    xy = xr + 2 * yr
                    piece, base = place(cr, xy, zr)
                    d = jnp.bitwise_xor(me, cr + 2 * xy + 8 * zr)
                    s = xr * 2 + cr
                    for c in range(3):
                        lanes = slice(128 * c, 128 * c + 128)
                        start = base + c * THIRD
                        rhs[96 * s : 96 * s + 96, lanes] = piece[start : start + 96, :]
                        w2[pl.ds(pl.multiple_of(48 * d, 16), 48), lanes] = piece[start + 96 : start + THIRD, :]
                    tail = piece[base + SMALL : base + SLAB, :].astype(F32)
                    small[0, pl.ds(d, 1), :] = tail[0:1, :]
                    small[1, pl.ds(d, 1), :] = tail[1:2, :]
            sorted_rows = dot_nn(order, rhs[...]).astype(BF16)
            for b in range(BLOCKS):
                w[b, pl.ds(pl.multiple_of(48 * g, 16), 48), :] = sorted_rows[48 * b : 48 * b + 48]
    for slot, size, per_owner, row in ((0, BIAS, SHARD_BIAS, bias_row), (1, GAIN, SHARD_GAIN, gain_row)):
        mine, place = owner_mask(size, per_owner)
        spread = dot_nn(small[slot].astype(BF16), place_matrix(place, size))
        row[...] = jnp.sum(jnp.where(mine, spread, 0.0), axis=0, keepdims=True)


def slab_rows(blocks, with_w2, with_small):
    return 3 * (12 * blocks + 48 * with_w2) + 16 * with_small


def disperse(me, dw, dw2, bias_row, gain_row, wires, rhs, small):
    blocks = dw.shape[0]
    size = 48 * blocks
    third = slab_rows(blocks, dw2 is not None, False) // 3
    stride = slab_rows(blocks, dw2 is not None, bias_row is not None)
    low = jnp.bitwise_and(me, 3)
    order = jnp.where(
        slab_codes((size, 1), 0, low, blocks) == order_codes((1, size), 1), 1.0, 0.0
    ).astype(BF16)
    if bias_row is not None:
        for slot, width, per_owner, row in ((0, BIAS, SHARD_BIAS, bias_row), (1, GAIN, SHARD_GAIN, gain_row)):
            mine, place = owner_mask(width, per_owner)
            spread = jnp.where(mine, row[...], 0.0).astype(BF16)
            small[slot] = dot_nt(spread, place_matrix(place, width))
    head_row = lax.broadcasted_iota(jnp.int32, (16, 128), 0)

    def group(zr, carry):
        for yr in range(2):
            g = jnp.bitwise_xor(lax.shift_right_logical(me, 2), yr + 2 * zr)
            for b in range(blocks):
                rhs[48 * b : 48 * b + 48, :] = dw[b, pl.ds(pl.multiple_of(48 * g, 16), 48), :]
            slabs = dot_nn(order, rhs[0:size, :]).astype(BF16)
            for xr in range(2):
                for cr in range(2):
                    out = wires[cr]
                    xy = xr + 2 * yr
                    d = jnp.bitwise_xor(me, cr + 2 * xy + 8 * zr)
                    s = xr * 2 + cr
                    base = pl.multiple_of(xy * (4 * stride) + zr * stride, 16)
                    for c in range(3):
                        lanes = slice(128 * c, 128 * c + 128)
                        start = base + c * third
                        rows = 12 * blocks
                        out[pl.ds(start, rows), :] = slabs[rows * s : rows * s + rows, lanes]
                        if dw2 is not None:
                            out[pl.ds(start + rows, 48), :] = dw2[pl.ds(pl.multiple_of(48 * d, 16), 48), lanes]
                    if bias_row is not None:
                        tail = jnp.where(
                            head_row == 0,
                            small[0, pl.ds(d, 1), :],
                            jnp.where(head_row == 1, small[1, pl.ds(d, 1), :], 0.0),
                        )
                        out[pl.ds(base + 3 * third, 16), :] = tail.astype(BF16)
        return carry

    lax.fori_loop(0, 4, group, 0)


def forward(x, w, w2, bias_row, gain_row, xna, qkv, probs, mixed, middle, xnb, act, slope, tmp):
    def norm_a(i, carry):
        rows = chunk_rows(i)
        normal, _ = normalize(x[rows, :])
        xna[rows, :] = (normal * gain_row[:, :D] + bias_row[:, :D]).astype(BF16)
        return carry

    lax.fori_loop(0, CHUNKS, norm_a, 0)
    for b in range(3):
        part = dot_nn(xna[...], w[b])
        if b == 0:
            part = part + bias_row[:, D : 2 * D]
        if b == 2:
            part = part + bias_row[:, 2 * D : 3 * D]
        qkv[b] = part.astype(BF16)

    lane = lax.broadcasted_iota(jnp.int32, (1, 128), 1)
    first = lane < HEAD
    halves = (first.astype(F32).astype(BF16), 1 - first.astype(F32).astype(BF16))
    real_key = lax.broadcasted_iota(jnp.int32, (1, ROWS), 1) < SEQ

    def image_attention(img, carry):
        rows = image_rows(img)

        def pair_attention(pair, inner):
            lanes = pair_lanes(pair)
            q, k, v = qkv[0, rows, lanes], qkv[1, rows, lanes], qkv[2, rows, lanes]
            outs = []
            for h in range(2):
                scores = dot_nt(q * halves[h], k) * (HEAD**-0.5)
                scores = jnp.where(real_key, scores, -1e30)
                raised = jnp.exp(scores - jnp.max(scores, axis=-1, keepdims=True))
                share = raised * (1.0 / jnp.sum(raised, axis=-1, keepdims=True))
                share = share.astype(BF16)
                probs[(img * PAIRS + pair) * 2 + h] = share
                outs.append(dot_nn(share, v))
            mixed[rows, lanes] = jnp.where(first, outs[0], outs[1]).astype(BF16)
            return inner

        return lax.fori_loop(0, PAIRS, pair_attention, carry)

    lax.fori_loop(0, IMGS, image_attention, 0)
    middle[...] = x[...] + (dot_nn(mixed[...], w[3]) + bias_row[:, 3 * D : 4 * D])

    def norm_b(i, carry):
        rows = chunk_rows(i)
        normal, _ = normalize(middle[rows, :])
        xnb[rows, :] = (normal * gain_row[:, D:] + bias_row[:, 4 * D : 5 * D]).astype(BF16)
        return carry

    lax.fori_loop(0, CHUNKS, norm_b, 0)

    def hidden(j, carry):
        tmp[...] = dot_nn(xnb[...], w[4 + j])
        shift = bias_row[:, pl.ds(pl.multiple_of(6 * D + j * D, 128), D)]

        def gelu(i, inner):
            rows = chunk_rows(i)
            pre = tmp[rows, :] + shift
            half = 0.5 * (1.0 + lax.erf(pre * ROOT_HALF))
            act[j, rows, :] = (pre * half).astype(BF16)
            slope[j, rows, :] = (half + pre * jnp.exp(-0.5 * pre * pre) * INV_ROOT_TAU).astype(BF16)
            return inner

        return lax.fori_loop(0, CHUNKS, gelu, carry)

    lax.fori_loop(0, 4, hidden, 0)
    tmp[...] = middle[...] + bias_row[:, 5 * D : 6 * D]
    for j in range(4):
        tmp[...] += dot_nn(act[j], w2[D * j : D * j + D, :])


def column_total(values):
    return jnp.sum(values.astype(F32), axis=0, keepdims=True)


def norm_back(source, gain, grad, tmp, low):
    def step(i, totals):
        rows = chunk_rows(i)
        back = tmp[rows, :]
        normal, inv_std = normalize(source[rows, :])
        scaled = back * gain
        first_mean = jnp.mean(scaled, axis=-1, keepdims=True)
        cross_mean = jnp.mean(scaled * normal, axis=-1, keepdims=True)
        result = grad[rows, :] + inv_std * (scaled - first_mean - normal * cross_mean)
        grad[rows, :] = result
        result_low = result.astype(BF16)
        if low is not None:
            low[rows, :] = result_low
        return (
            totals[0] + jnp.sum(back * normal, axis=0, keepdims=True),
            totals[1] + jnp.sum(back, axis=0, keepdims=True),
            totals[2] + jnp.sum(result_low.astype(F32), axis=0, keepdims=True),
        )

    zero = jnp.zeros((1, D), F32)
    return lax.fori_loop(0, CHUNKS, step, (zero, zero, zero))


def mlp_backward(w, w2, gain_row, mixed, middle, xnb, act, slope, grad, low, gpre, gmix, tmp, dw, dw_out, dw2, dbias, dgain):
    low[...] = grad[...].astype(BF16)
    dbias[:, 5 * D : 6 * D] = column_total(low[...])

    def hidden(j, carry):
        dw2[block_rows(j), :] = dot_tn(act[j], low[...]).astype(BF16)
        pre = (dot_nt(low[...], w2[block_rows(j), :]) * slope[j].astype(F32)).astype(BF16)
        gpre[...] = pre
        dbias[:, pl.ds(pl.multiple_of(6 * D + j * D, 128), D)] = column_total(gpre[...])
        dw[j] = dot_tn(xnb[...], gpre[...]).astype(BF16)
        part = dot_nt(gpre[...], w[4 + j])
        tmp[...] = jnp.where(j == 0, part, tmp[...] + part)
        return carry

    lax.fori_loop(0, 4, hidden, 0)
    gain_two, shift_two, bias_out = norm_back(middle, gain_row[:, D:], grad, tmp, low)
    dgain[:, D:] = gain_two
    dbias[:, 4 * D : 5 * D] = shift_two
    dbias[:, 3 * D : 4 * D] = bias_out
    dw_out[...] = dot_tn(mixed[...], low[...]).astype(BF16)
    gmix[...] = dot_nt(low[...], w[3]).astype(BF16)


def attention_backward(qkv, probs, gmix, gqkv):
    lane = lax.broadcasted_iota(jnp.int32, (1, 128), 1)
    first = lane < HEAD
    halves = (first.astype(F32).astype(BF16), 1 - first.astype(F32).astype(BF16))

    def image_attention(img, carry):
        rows = image_rows(img)

        def pair_attention(pair, inner):
            lanes = pair_lanes(pair)
            q, k, v = qkv[0, rows, lanes], qkv[1, rows, lanes], qkv[2, rows, lanes]
            gm = gmix[rows, lanes]
            grads = ([], [], [])
            for h in range(2):
                share = probs[(img * PAIRS + pair) * 2 + h]
                grad_share = dot_nt(gm * halves[h], v)
                full = share.astype(F32)
                row_dot = jnp.sum(full * grad_share, axis=-1, keepdims=True)
                grad_scores = (full * (grad_share - row_dot)).astype(BF16)
                grads[0].append(dot_nn(grad_scores, k) * (HEAD**-0.5))
                grads[1].append(dot_tn(grad_scores, q) * (HEAD**-0.5))
                grads[2].append(dot_tn(share, gm))
            for b in range(3):
                gqkv[b, rows, lanes] = jnp.where(first, grads[b][0], grads[b][1]).astype(BF16)
            return inner

        return lax.fori_loop(0, PAIRS, pair_attention, carry)

    lax.fori_loop(0, IMGS, image_attention, 0)


def projection_backward(x, w, gain_row, xna, gqkv, grad, tmp, dw, dbias, dgain):
    for b in range(3):
        dw[b] = dot_tn(xna[...], gqkv[b]).astype(BF16)
        part = dot_nt(gqkv[b], w[b])
        tmp[...] = part if b == 0 else tmp[...] + part
    dbias[:, D : 2 * D] = column_total(gqkv[0])
    dbias[:, 2 * D : 3 * D] = column_total(gqkv[2])
    gain_one, shift_one, _ = norm_back(x, gain_row[:, :D], grad, tmp, None)
    dgain[:, :D] = gain_one
    dbias[:, :D] = shift_one


def load_images(images, x):
    x[...] = jnp.zeros_like(x)
    for i in range(IMGS):
        x[ROWS * i : ROWS * i + SEQ, :] = images[i].astype(F32)


STATE = (
    ((R, D), BF16),
    ((3, R, D), BF16),
    ((IMGS * PAIRS * 2, ROWS, ROWS), BF16),
    ((R, D), BF16),
    ((R, D), F32),
    ((R, D), BF16),
    ((4, R, D), BF16),
    ((4, R, D), BF16),
)
WEIGHTS = (
    ((BLOCKS, D, D), BF16),
    ((FF, D), BF16),
    ((1, BIAS), F32),
    ((1, GAIN), F32),
)
BIAS_ROW = ((1, BIAS), F32)
GAIN_ROW = ((1, GAIN), F32)
HALF_BLOCKS = ((BLOCKS // 2, D, D), BF16)
MOVE_SCRATCH = (((D, D), BF16), ((2, SLABS, 128), F32))


def wires(*part):
    return [jax.ShapeDtypeStruct((16 * slab_rows(*part), 128), BF16)] * 2


def shapes(specs):
    return [jax.ShapeDtypeStruct(*spec) for spec in specs]


def scratch(specs):
    return [pltpu.VMEM(*spec) for spec in specs]


def first_forward_kernel(*refs):
    me, images, pieces, refs = refs[0][0], refs[1], refs[2:10], refs[10:]
    stream, weights, state = refs[0], refs[1:5], refs[5:13]
    x, rhs, small = refs[13:]
    assemble(me, lambda core, xy, z: (pieces[4 * core + xy], z * SLAB), *weights, rhs, small)
    load_images(images, x)
    forward(x, *weights, *state, stream)


def second_layer_kernel(*refs):
    me, live, stream, cotangent, slabs, refs = refs[0][0], refs[1], refs[2], refs[3], refs[4], refs[5:]
    activations, grad, sent, refs = refs[0], refs[1], refs[2:4], refs[4:]
    weights, state, refs = refs[:4], refs[4:12], refs[12:]
    low, gpre, gqkv, gmix, tmp, dw, dw2, dbias, dgain, rhs, small = refs
    assemble(jnp.int32(0), lambda core, xy, z: (slabs, (core + 2 * xy + 8 * z) * SLAB), *weights, rhs, small)
    forward(stream, *weights, *state, grad)
    for i in range(IMGS):
        alive = jnp.where(live[i] > 0, 1.0, 0.0)
        activations[i] = (grad[ROWS * i : ROWS * i + SEQ, :] * alive).astype(BF16)
    load_images(cotangent, grad)
    for i in range(IMGS):
        alive = jnp.where(live[i] > 0, 1.0, 0.0)
        grad[ROWS * i : ROWS * i + ROWS, :] = grad[ROWS * i : ROWS * i + ROWS, :] * alive
    w, w2, _, gain_row = weights
    xna, qkv, probs, mixed, middle, xnb, act, slope = state
    mlp_backward(
        w, w2, gain_row, mixed, middle, xnb, act, slope, grad, low, gpre, gmix, tmp, dw.at[4:8], dw.at[3], dw2, dbias, dgain
    )
    attention_backward(qkv, probs, gmix, gqkv)
    projection_backward(stream, w, gain_row, xna, gqkv, grad, tmp, dw, dbias, dgain)
    disperse(me, dw, dw2, dbias, dgain, sent, rhs, small)


def first_mlp_backward_kernel(
    me, grad_in, w, w2, gain_row, mixed, middle, xnb, act, slope, grad, gmix, dw_out, dbias, dgain, *refs
):
    sent, (low, gpre, tmp, dw, dw2, rhs) = refs[:2], refs[2:]
    grad[...] = grad_in[...]
    dbias[...] = jnp.zeros_like(dbias)
    dgain[...] = jnp.zeros_like(dgain)
    mlp_backward(
        w, w2, gain_row, mixed, middle, xnb, act, slope, grad, low, gpre, gmix, tmp, dw, dw_out, dw2, dbias, dgain
    )
    disperse(me[0], dw, dw2, None, None, sent, rhs, None)


def first_attention_backward_kernel(qkv, probs, gmix, gqkv):
    attention_backward(qkv, probs, gmix, gqkv)


def first_projection_backward_kernel(
    me, images, grad_in, gqkv, dw_out, dbias_in, dgain_in, w, gain_row, xna, input_grad, *refs
):
    sent, (x, grad, tmp, dw, dbias, dgain, rhs, small) = refs[:2], refs[2:]
    load_images(images, x)
    grad[...] = grad_in[...]
    dbias[...] = dbias_in[...]
    dgain[...] = dgain_in[...]
    dw[3] = dw_out[...]
    projection_backward(x, w, gain_row, xna, gqkv, grad, tmp, dw, dbias, dgain)
    for i in range(IMGS):
        input_grad[i] = grad[ROWS * i : ROWS * i + SEQ, :].astype(BF16)
    disperse(me[0], dw, None, dbias, dgain, sent, rhs, small)


def whole(count):
    return [pl.BlockSpec(memory_space=pltpu.VMEM)] * count


def scalar(count):
    return [pl.BlockSpec(memory_space=pltpu.SMEM)] * count


def params():
    return pltpu.CompilerParams(vmem_limit_bytes=VMEM_LIMIT)


def cost(flops):
    return pl.CostEstimate(flops=flops, bytes_accessed=20_000_000, transcendentals=0)


def run_first_forward(me, images, pieces):
    outs = [jax.ShapeDtypeStruct((R, D), F32)] + shapes(WEIGHTS) + shapes(STATE)
    out = pl.pallas_call(
        first_forward_kernel,
        out_shape=outs,
        in_specs=scalar(1) + whole(9),
        out_specs=whole(len(outs)),
        scratch_shapes=scratch((((R, D), F32),) + MOVE_SCRATCH),
        compiler_params=params(),
        cost_estimate=cost(33_000_000_000),
        name="first_forward",
    )(me, images, *pieces)
    return out[0], out[1:5], out[5:]


def run_second_layer(me, live, stream, cotangent, slabs):
    outs = [jax.ShapeDtypeStruct(cotangent.shape, BF16), jax.ShapeDtypeStruct((R, D), F32)]
    outs += wires(BLOCKS, True, True)
    low, full = ((R, D), BF16), ((R, D), F32)
    back = (low, low, ((3, R, D), BF16), low, full, ((BLOCKS, D, D), BF16), ((FF, D), BF16), BIAS_ROW, GAIN_ROW)
    return pl.pallas_call(
        second_layer_kernel,
        out_shape=outs,
        in_specs=scalar(2) + whole(3),
        out_specs=whole(len(outs)),
        scratch_shapes=scratch(WEIGHTS + STATE + back + MOVE_SCRATCH),
        compiler_params=params(),
        cost_estimate=cost(65_000_000_000),
        name="second_layer",
    )(me, live, stream, cotangent, slabs)


def run_first_mlp_backward(me, grad, weights, state):
    w, w2, _, gain_row = weights
    low, full = ((R, D), BF16), ((R, D), F32)
    outs = shapes((full, low, ((D, D), BF16), BIAS_ROW, GAIN_ROW)) + wires(BLOCKS // 2, True, False)
    return pl.pallas_call(
        first_mlp_backward_kernel,
        out_shape=outs,
        in_specs=scalar(1) + whole(9),
        out_specs=whole(len(outs)),
        scratch_shapes=scratch((low, low, full, HALF_BLOCKS, ((FF, D), BF16), MOVE_SCRATCH[0])),
        compiler_params=params(),
        cost_estimate=cost(20_000_000_000),
        name="first_mlp_backward",
    )(me, grad, w, w2, gain_row, *state[3:])


def run_first_attention_backward(gmix, state):
    return pl.pallas_call(
        first_attention_backward_kernel,
        out_shape=jax.ShapeDtypeStruct((3, R, D), BF16),
        in_specs=whole(3),
        out_specs=whole(1)[0],
        compiler_params=params(),
        cost_estimate=cost(12_000_000_000),
        name="first_attention_backward",
    )(state[1], state[2], gmix)


def run_first_projection_backward(me, images, grad, gqkv, rest, weights, state):
    w, _, _, gain_row = weights
    full = ((R, D), F32)
    outs = [jax.ShapeDtypeStruct(images.shape, BF16)] + wires(BLOCKS // 2, False, True)
    return pl.pallas_call(
        first_projection_backward_kernel,
        out_shape=outs,
        in_specs=scalar(1) + whole(9),
        out_specs=whole(len(outs)),
        scratch_shapes=scratch((full, full, full, HALF_BLOCKS, BIAS_ROW, GAIN_ROW) + MOVE_SCRATCH),
        compiler_params=params(),
        cost_estimate=cost(10_000_000_000),
        name="first_projection_backward",
    )(me, images, grad, gqkv, *rest, w, gain_row, state[0])


def chunk_table():
    table = []
    for c in range(3):
        for i in range(12):
            for b in range(3):
                table.append((0, i * 9 + b * 3 + c, c, b * 12 + i))
            table.append((1, i * 3 + c, c, 36 + i))
            for b in range(4):
                table.append((2, i * 12 + b * 3 + c, c, 48 + b * 12 + i))
        for i in range(48):
            table.append((3, i * 3 + c, c, 96 + i))
    return table


def pack_kernel(qkv, out, fc1, fc2, gains, biases, slab_a, slab_b, stage_a, stage_b):
    flats, stages = (qkv, out, fc1, fc2), (stage_a, stage_b)
    for stage in stages:
        stage[SMALL:SLAB, :] = jnp.zeros((SLAB - SMALL, 128), F32)
    for which, piece, c, row in chunk_table():
        both = flats[which][:, 128 * piece : 128 * piece + 128].astype(F32)
        row += c * THIRD
        for layer in range(LAYERS):
            stages[layer][row : row + 1, :] = both[layer : layer + 1]
    for layer in range(LAYERS):
        stages[layer][SMALL : SMALL + 1, 0:SHARD_BIAS] = biases[...].astype(F32)[layer : layer + 1]
        stages[layer][SMALL + 1 : SMALL + 2, 0:SHARD_GAIN] = gains[...].astype(F32)[layer : layer + 1]
    slab_a[...] = stage_a[...].astype(BF16)
    slab_b[...] = stage_b[...].astype(BF16)


def run_pack(qkv, out, fc1, fc2, gains, biases):
    return pl.pallas_call(
        pack_kernel,
        out_shape=[jax.ShapeDtypeStruct((SLAB, 128), BF16)] * 2,
        in_specs=whole(6),
        out_specs=whole(2),
        scratch_shapes=[pltpu.VMEM((SLAB, 128), F32)] * 2,
        name="pack",
    )(qkv, out, fc1, fc2, gains, biases)


def unpack_kernel(first, second, *refs):
    flats, (gains, biases) = refs[:4], refs[4:]
    start = slab_rows(BLOCKS // 2, True, False)
    for which, piece, c, row in chunk_table():
        lanes = slice(128 * piece, 128 * piece + 128)
        at = start + c * 48 + row if which < 2 else c * 96 + row - 48
        flats[which][0:1, lanes] = first[at : at + 1, :]
        at = c * THIRD + row
        flats[which][1:2, lanes] = second[at : at + 1, :]
    for layer, slab in enumerate((first, second)):
        biases[layer : layer + 1, :] = slab[SMALL : SMALL + 1, 0:SHARD_BIAS]
        gains[layer : layer + 1, :] = slab[SMALL + 1 : SMALL + 2, 0:SHARD_GAIN]


def run_unpack(first, second, widths):
    return pl.pallas_call(
        unpack_kernel,
        out_shape=[jax.ShapeDtypeStruct((LAYERS, width), F32) for width in widths],
        in_specs=whole(2),
        out_specs=whole(6),
        name="unpack",
    )(first, second)


def swap(value, bits):
    return lax.ppermute(value, "fsdp", [(i, i ^ bits) for i in range(SLABS)])


XY_STEPS = (2, 4, 6)
Z_STEPS = (8, 16, 24)


def spread(value, steps):
    return [value] + [swap(value, bits) for bits in steps]


def gather_tree(slab):
    near = spread(jnp.concatenate(spread(slab, Z_STEPS), axis=0), XY_STEPS)
    return near + [swap(part, 1) for part in near]


def across_cores(keep, send):
    return keep.astype(F32) + swap(send, 1).astype(F32)


def collect(total, steps):
    rows = total.shape[0] // 4
    mine = total[:rows]
    for place, bits in enumerate(steps):
        part = total[rows * (place + 1) : rows * (place + 2)]
        mine = mine + swap(part.astype(BF16), bits).astype(F32)
    return mine


def join(first, second):
    return jnp.concatenate([first.reshape(4, -1, 128), second.reshape(4, -1, 128)], axis=1).reshape(-1, 128)


def to_slabs(qkv, out, fc1, fc2, gains, biases):
    blocks = jnp.concatenate(
        [
            qkv.reshape(SLABS, 12, 3, D).transpose(0, 2, 1, 3).reshape(SLABS, 36, D),
            out.reshape(SLABS, 12, D),
            fc1.reshape(SLABS, 12, 4, D).transpose(0, 2, 1, 3).reshape(SLABS, 48, D),
            fc2.reshape(SLABS, 48, D),
        ],
        axis=1,
    )
    thirds = blocks.reshape(SLABS, THIRD, 3, 128).transpose(0, 2, 1, 3).reshape(SLABS, 3 * THIRD, 128)
    tail = jnp.zeros((SLABS, SLAB - SMALL, 128), blocks.dtype)
    tail = tail.at[:, 0, :SHARD_BIAS].set(biases.reshape(SLABS, SHARD_BIAS))
    tail = tail.at[:, 1, :SHARD_GAIN].set(gains.reshape(SLABS, SHARD_GAIN))
    return jnp.concatenate([thirds, tail], axis=1)


def from_slabs(slabs):
    blocks = slabs[:, :SMALL].reshape(SLABS, 3, THIRD, 128).transpose(0, 2, 1, 3).reshape(SLABS, THIRD, D)
    return (
        blocks[:, :36].reshape(SLABS, 3, 12, D).transpose(0, 2, 1, 3).reshape(-1),
        blocks[:, 36:48].reshape(-1),
        blocks[:, 48:96].reshape(SLABS, 4, 12, D).transpose(0, 2, 1, 3).reshape(-1),
        blocks[:, 96:].reshape(-1),
        slabs[:, SMALL + 1, :SHARD_GAIN].reshape(-1),
        slabs[:, SMALL, :SHARD_BIAS].reshape(-1),
    )


def plain_gather(flats, layer):
    return to_slabs(*(lax.all_gather(flat[layer], "fsdp", axis=0, tiled=True) for flat in flats))


def plain_pieces(slabs):
    return [
        jnp.concatenate([slabs[core + 2 * xy + 8 * z] for z in range(4)], axis=0)
        for core in range(2)
        for xy in range(4)
    ]


def plain_slabs(keep, send):
    halves = [half.reshape(4, 4, -1, 128).astype(F32) for half in (keep, send)]
    return jnp.stack([halves[d & 1][(d >> 1) & 3, d >> 3] for d in range(SLABS)])


def plain_totals(slabs):
    return [lax.psum_scatter(flat, "fsdp", scatter_dimension=0, tiled=True) for flat in from_slabs(slabs)]


def joined_slabs(mlp, attention):
    parts = []
    for c in range(3):
        parts += [attention[:, 48 * c : 48 * c + 48], mlp[:, 96 * c : 96 * c + 96]]
    return jnp.concatenate(parts + [attention[:, THIRD:]], axis=1)


def local(images, live_counts, qkv_weight, out_weight, fc1_weight, fc2_weight, norm_gains, biases, cotangent):
    flats = (qkv_weight, out_weight, fc1_weight, fc2_weight, norm_gains, biases)
    if lax.axis_size("fsdp") == SLABS:
        return local_tree(images, live_counts, flats, cotangent)
    me = jnp.zeros((1,), jnp.int32)
    slabs_b = plain_gather(flats, 1).reshape(-1, 128)
    stream, weights, state = run_first_forward(me, images, plain_pieces(plain_gather(flats, 0)))
    activations, grad, *second = run_second_layer(me, live_counts, stream, cotangent, slabs_b)
    grad, gmix, *rest, mlp_keep, mlp_send = run_first_mlp_backward(me, grad, weights, state)
    gqkv = run_first_attention_backward(gmix, state)
    input_grad, *attention = run_first_projection_backward(me, images, grad, gqkv, rest, weights, state)
    first = joined_slabs(plain_slabs(mlp_keep, mlp_send), plain_slabs(*attention))
    results = [jnp.stack(both) for both in zip(plain_totals(first), plain_totals(plain_slabs(*second)))]
    return (activations, input_grad, *results)


def local_tree(images, live_counts, flats, cotangent):
    me = lax.axis_index("fsdp").astype(jnp.int32).reshape(1)
    slab_a, slab_b = run_pack(*flats)
    slabs_b = lax.all_gather(slab_b, "fsdp", axis=0, tiled=True)
    stream, weights, state = run_first_forward(me, images, gather_tree(slab_a))
    slabs_b, stream = lax.optimization_barrier((slabs_b, stream))
    activations, grad, *second = run_second_layer(me, live_counts, stream, cotangent, slabs_b)

    second = across_cores(*second)
    grad, gmix, *rest, mlp_keep, mlp_send = run_first_mlp_backward(me, grad, weights, state)
    second, gmix, mlp_keep, mlp_send = lax.optimization_barrier((second, gmix, mlp_keep, mlp_send))

    second, mlp = collect(second, XY_STEPS), across_cores(mlp_keep, mlp_send)
    gqkv = run_first_attention_backward(gmix, state)
    second, mlp, gqkv = lax.optimization_barrier((second, mlp, gqkv))

    second, mlp = collect(second, Z_STEPS), collect(mlp, XY_STEPS)
    input_grad, *attention = run_first_projection_backward(me, images, grad, gqkv, rest, weights, state)
    second, mlp, attention = lax.optimization_barrier((second, mlp, attention))

    attention = collect(across_cores(*attention), XY_STEPS)
    first = collect(join(mlp, attention), Z_STEPS)
    results = run_unpack(first, second, [flat.shape[1] for flat in flats])
    return (activations, input_grad, *results)


def solution(mesh):
    flat = P(None, "fsdp")
    image = P("fsdp", None, None)
    return jax.shard_map(
        local,
        mesh=mesh,
        in_specs=(image, P("fsdp")) + (flat,) * 6 + (image,),
        out_specs=(image, image) + (flat,) * 6,
        check_vma=False,
    )
```

```python
import jax
import jax.numpy as jnp
from jax import lax
from jax.experimental import pallas as pl
from jax.experimental.pallas import tpu as pltpu
from jax.sharding import PartitionSpec as P

D = 384
FF = 1536
SEQ = 197
HEAD = 64
LAYERS = 2
NORM_EPS = 1e-06
ROOT_HALF = 0.7071067811865476
INV_ROOT_TAU = 0.3989422804014327

IMGS = 3
ROWS = 208
R = IMGS * ROWS
CHUNK = 48
CHUNKS = R // CHUNK
PAIRS = 3

SLABS = 32
THIRD = 144
SMALL = 3 * THIRD
SLAB = SMALL + 16
BLOCKS = 8
SHARD_BIAS = 120
SHARD_GAIN = 24
BIAS = 6 * D + FF
GAIN = 2 * D

F32 = jnp.float32
BF16 = jnp.bfloat16
VMEM_LIMIT = 56 * 1024 * 1024


def dot_nn(a, b):
    return lax.dot_general(a, b, (((1,), (0,)), ((), ())), preferred_element_type=F32)


def dot_nt(a, b):
    return lax.dot_general(a, b, (((1,), (1,)), ((), ())), preferred_element_type=F32)


def dot_tn(a, b):
    return lax.dot_general(a, b, (((0,), (0,)), ((), ())), preferred_element_type=F32)


def chunk_rows(i):
    return pl.ds(pl.multiple_of(i * CHUNK, CHUNK), CHUNK)


def block_rows(j):
    return pl.ds(pl.multiple_of(j * D, D), D)


def image_rows(i):
    return pl.ds(pl.multiple_of(i * ROWS, 16), ROWS)


def pair_lanes(p):
    return pl.ds(pl.multiple_of(p * 128, 128), 128)


def normalize(x):
    centred = x - jnp.mean(x, axis=-1, keepdims=True)
    inv_std = lax.rsqrt(jnp.mean(centred * centred, axis=-1, keepdims=True) + NORM_EPS)
    return centred * inv_std, inv_std


def digits(index, size):
    whole = jnp.floor((index.astype(F32) + 0.5) * (1.0 / size)).astype(jnp.int32)
    return whole, index - whole * size


def order_codes(shape, axis):
    index = lax.broadcasted_iota(jnp.int32, shape, axis)
    block, rest = digits(index, 48)
    dev, row = digits(rest, 12)
    return (block * 4 + dev) * 12 + row


def slab_codes(shape, axis, low, blocks):
    index = lax.broadcasted_iota(jnp.int32, shape, axis)
    rel, rest = digits(index, 12 * blocks)
    block, row = digits(rest, 12)
    dev = jnp.bitwise_xor(rel, low)
    return (block * 4 + dev) * 12 + row


def owner_mask(size, per_owner):
    lane = lax.broadcasted_iota(jnp.int32, (1, size), 1)
    owner, place = digits(lane, per_owner)
    rows = lax.broadcasted_iota(jnp.int32, (SLABS, size), 0)
    return rows == owner, place


def place_matrix(place, size):
    rows = lax.broadcasted_iota(jnp.int32, (128, size), 0)
    return jnp.where(rows == place, 1.0, 0.0).astype(BF16)


def assemble(me, pieces, w, w2, bias_row, gain_row, rhs, small):
    low = jnp.bitwise_and(me, 3)
    order = jnp.where(
        order_codes((D, 1), 0) == slab_codes((1, D), 1, low, BLOCKS), 1.0, 0.0
    ).astype(BF16)

    for zr in range(4):
        for yr in range(2):
            g = jnp.bitwise_xor(lax.shift_right_logical(me, 2), yr + 2 * zr)
            for xr in range(2):
                for cr in range(2):
                    xy = xr + 2 * yr
                    piece, base = pieces[4 * cr + xy], zr * SLAB
                    d = jnp.bitwise_xor(me, cr + 2 * xy + 8 * zr)
                    s = xr * 2 + cr
                    for c in range(3):
                        lanes = slice(128 * c, 128 * c + 128)
                        start = base + c * THIRD
                        rhs[96 * s : 96 * s + 96, lanes] = piece[start : start + 96, :]
                        w2[pl.ds(pl.multiple_of(48 * d, 16), 48), lanes] = piece[start + 96 : start + THIRD, :]
                    tail = piece[base + SMALL : base + SLAB, :].astype(F32)
                    small[0, pl.ds(d, 1), :] = tail[0:1, :]
                    small[1, pl.ds(d, 1), :] = tail[1:2, :]
            sorted_rows = dot_nn(order, rhs[...]).astype(BF16)
            for b in range(BLOCKS):
                w[b, pl.ds(pl.multiple_of(48 * g, 16), 48), :] = sorted_rows[48 * b : 48 * b + 48]
    for slot, size, per_owner, row in ((0, BIAS, SHARD_BIAS, bias_row), (1, GAIN, SHARD_GAIN, gain_row)):
        mine, place = owner_mask(size, per_owner)
        spread = dot_nn(small[slot].astype(BF16), place_matrix(place, size))
        row[...] = jnp.sum(jnp.where(mine, spread, 0.0), axis=0, keepdims=True)


def slab_rows(blocks, with_w2, with_small):
    return 3 * (12 * blocks + 48 * with_w2) + 16 * with_small


def disperse(me, dw, dw2, bias_row, gain_row, wires, rhs, small):
    blocks = dw.shape[0]
    size = 48 * blocks
    third = slab_rows(blocks, dw2 is not None, False) // 3
    stride = slab_rows(blocks, dw2 is not None, bias_row is not None)
    low = jnp.bitwise_and(me, 3)
    order = jnp.where(
        slab_codes((size, 1), 0, low, blocks) == order_codes((1, size), 1), 1.0, 0.0
    ).astype(BF16)
    if bias_row is not None:
        for slot, width, per_owner, row in ((0, BIAS, SHARD_BIAS, bias_row), (1, GAIN, SHARD_GAIN, gain_row)):
            mine, place = owner_mask(width, per_owner)
            spread = jnp.where(mine, row[...], 0.0).astype(BF16)
            small[slot] = dot_nt(spread, place_matrix(place, width))
    head_row = lax.broadcasted_iota(jnp.int32, (16, 128), 0)

    def group(zr, carry):
        for yr in range(2):
            g = jnp.bitwise_xor(lax.shift_right_logical(me, 2), yr + 2 * zr)
            for b in range(blocks):
                rhs[48 * b : 48 * b + 48, :] = dw[b, pl.ds(pl.multiple_of(48 * g, 16), 48), :]
            slabs = dot_nn(order, rhs[0:size, :]).astype(BF16)
            for xr in range(2):
                for cr in range(2):
                    out = wires[cr]
                    xy = xr + 2 * yr
                    d = jnp.bitwise_xor(me, cr + 2 * xy + 8 * zr)
                    s = xr * 2 + cr
                    base = pl.multiple_of(xy * (4 * stride) + zr * stride, 16)
                    for c in range(3):
                        lanes = slice(128 * c, 128 * c + 128)
                        start = base + c * third
                        rows = 12 * blocks
                        out[pl.ds(start, rows), :] = slabs[rows * s : rows * s + rows, lanes]
                        if dw2 is not None:
                            out[pl.ds(start + rows, 48), :] = dw2[pl.ds(pl.multiple_of(48 * d, 16), 48), lanes]
                    if bias_row is not None:
                        tail = jnp.where(
                            head_row == 0,
                            small[0, pl.ds(d, 1), :],
                            jnp.where(head_row == 1, small[1, pl.ds(d, 1), :], 0.0),
                        )
                        out[pl.ds(base + 3 * third, 16), :] = tail.astype(BF16)
        return carry

    lax.fori_loop(0, 4, group, 0, unroll=True)


def forward(x, w, w2, bias_row, gain_row, xna, qkv, probs, mixed, middle, xnb, act, slope, tmp):
    def norm_a(i, carry):
        rows = chunk_rows(i)
        normal, _ = normalize(x[rows, :])
        xna[rows, :] = (normal * gain_row[:, :D] + bias_row[:, :D]).astype(BF16)
        return carry

    lax.fori_loop(0, CHUNKS, norm_a, 0, unroll=True)
    for b in range(3):
        part = dot_nn(xna[...], w[b])
        if b == 0:
            part = part + bias_row[:, D : 2 * D]
        if b == 2:
            part = part + bias_row[:, 2 * D : 3 * D]
        qkv[b] = part.astype(BF16)

    lane = lax.broadcasted_iota(jnp.int32, (1, 128), 1)
    first = lane < HEAD
    halves = (first.astype(F32).astype(BF16), 1 - first.astype(F32).astype(BF16))
    real_key = lax.broadcasted_iota(jnp.int32, (1, ROWS), 1) < SEQ

    def image_attention(img, carry):
        rows = image_rows(img)

        def pair_attention(pair, inner):
            lanes = pair_lanes(pair)
            q, k, v = qkv[0, rows, lanes], qkv[1, rows, lanes], qkv[2, rows, lanes]
            outs = []
            for h in range(2):
                scores = dot_nt(q * halves[h], k) * (HEAD**-0.5)
                scores = jnp.where(real_key, scores, -1e30)
                raised = jnp.exp(scores - jnp.max(scores, axis=-1, keepdims=True))
                share = raised * (1.0 / jnp.sum(raised, axis=-1, keepdims=True))
                share = share.astype(BF16)
                probs[(img * PAIRS + pair) * 2 + h] = share
                outs.append(dot_nn(share, v))
            mixed[rows, lanes] = jnp.where(first, outs[0], outs[1]).astype(BF16)
            return inner

        return lax.fori_loop(0, PAIRS, pair_attention, carry, unroll=True)

    lax.fori_loop(0, IMGS, image_attention, 0, unroll=True)
    middle[...] = x[...] + (dot_nn(mixed[...], w[3]) + bias_row[:, 3 * D : 4 * D])

    def norm_b(i, carry):
        rows = chunk_rows(i)
        normal, _ = normalize(middle[rows, :])
        xnb[rows, :] = (normal * gain_row[:, D:] + bias_row[:, 4 * D : 5 * D]).astype(BF16)
        return carry

    lax.fori_loop(0, CHUNKS, norm_b, 0, unroll=True)

    def hidden(j, carry):
        tmp[...] = dot_nn(xnb[...], w[4 + j])
        shift = bias_row[:, pl.ds(pl.multiple_of(6 * D + j * D, 128), D)]

        def gelu(i, inner):
            rows = chunk_rows(i)
            pre = tmp[rows, :] + shift
            half = 0.5 * (1.0 + lax.erf(pre * ROOT_HALF))
            act[j, rows, :] = (pre * half).astype(BF16)
            slope[j, rows, :] = (half + pre * jnp.exp(-0.5 * pre * pre) * INV_ROOT_TAU).astype(BF16)
            return inner

        return lax.fori_loop(0, CHUNKS, gelu, carry, unroll=True)

    lax.fori_loop(0, 4, hidden, 0, unroll=True)
    tmp[...] = middle[...] + bias_row[:, 5 * D : 6 * D]
    for j in range(4):
        tmp[...] += dot_nn(act[j], w2[D * j : D * j + D, :])


def column_total(values):
    return jnp.sum(values.astype(F32), axis=0, keepdims=True)


def norm_back(source, gain, grad, tmp, low):
    def step(i, totals):
        rows = chunk_rows(i)
        back = tmp[rows, :]
        normal, inv_std = normalize(source[rows, :])
        scaled = back * gain
        first_mean = jnp.mean(scaled, axis=-1, keepdims=True)
        cross_mean = jnp.mean(scaled * normal, axis=-1, keepdims=True)
        result = grad[rows, :] + inv_std * (scaled - first_mean - normal * cross_mean)
        grad[rows, :] = result
        result_low = result.astype(BF16)
        if low is not None:
            low[rows, :] = result_low
        return (
            totals[0] + jnp.sum(back * normal, axis=0, keepdims=True),
            totals[1] + jnp.sum(back, axis=0, keepdims=True),
            totals[2] + jnp.sum(result_low.astype(F32), axis=0, keepdims=True),
        )

    zero = jnp.zeros((1, D), F32)
    return lax.fori_loop(0, CHUNKS, step, (zero, zero, zero), unroll=True)


def mlp_backward(w, w2, gain_row, mixed, middle, xnb, act, slope, grad, low, gpre, gmix, tmp, dw, dw_out, dw2, dbias, dgain):
    low[...] = grad[...].astype(BF16)
    dbias[:, 5 * D : 6 * D] = column_total(low[...])

    def hidden(j, carry):
        dw2[block_rows(j), :] = dot_tn(act[j], low[...]).astype(BF16)
        pre = (dot_nt(low[...], w2[block_rows(j), :]) * slope[j].astype(F32)).astype(BF16)
        gpre[...] = pre
        dbias[:, pl.ds(pl.multiple_of(6 * D + j * D, 128), D)] = column_total(gpre[...])
        dw[j] = dot_tn(xnb[...], gpre[...]).astype(BF16)
        part = dot_nt(gpre[...], w[4 + j])
        tmp[...] = jnp.where(j == 0, part, tmp[...] + part)
        return carry

    lax.fori_loop(0, 4, hidden, 0, unroll=True)
    gain_two, shift_two, bias_out = norm_back(middle, gain_row[:, D:], grad, tmp, low)
    dgain[:, D:] = gain_two
    dbias[:, 4 * D : 5 * D] = shift_two
    dbias[:, 3 * D : 4 * D] = bias_out
    dw_out[...] = dot_tn(mixed[...], low[...]).astype(BF16)
    gmix[...] = dot_nt(low[...], w[3]).astype(BF16)


def attention_backward(qkv, probs, gmix, gqkv):
    lane = lax.broadcasted_iota(jnp.int32, (1, 128), 1)
    first = lane < HEAD
    halves = (first.astype(F32).astype(BF16), 1 - first.astype(F32).astype(BF16))

    def image_attention(img, carry):
        rows = image_rows(img)

        def pair_attention(pair, inner):
            lanes = pair_lanes(pair)
            q, k, v = qkv[0, rows, lanes], qkv[1, rows, lanes], qkv[2, rows, lanes]
            gm = gmix[rows, lanes]
            grads = ([], [], [])
            for h in range(2):
                share = probs[(img * PAIRS + pair) * 2 + h]
                grad_share = dot_nt(gm * halves[h], v)
                full = share.astype(F32)
                row_dot = jnp.sum(full * grad_share, axis=-1, keepdims=True)
                grad_scores = (full * (grad_share - row_dot)).astype(BF16)
                grads[0].append(dot_nn(grad_scores, k) * (HEAD**-0.5))
                grads[1].append(dot_tn(grad_scores, q) * (HEAD**-0.5))
                grads[2].append(dot_tn(share, gm))
            for b in range(3):
                gqkv[b, rows, lanes] = jnp.where(first, grads[b][0], grads[b][1]).astype(BF16)
            return inner

        return lax.fori_loop(0, PAIRS, pair_attention, carry, unroll=True)

    lax.fori_loop(0, IMGS, image_attention, 0, unroll=True)


def projection_backward(x, w, gain_row, xna, gqkv, grad, tmp, dw, dbias, dgain):
    for b in range(3):
        dw[b] = dot_tn(xna[...], gqkv[b]).astype(BF16)
        part = dot_nt(gqkv[b], w[b])
        tmp[...] = part if b == 0 else tmp[...] + part
    dbias[:, D : 2 * D] = column_total(gqkv[0])
    dbias[:, 2 * D : 3 * D] = column_total(gqkv[2])
    gain_one, shift_one, _ = norm_back(x, gain_row[:, :D], grad, tmp, None)
    dgain[:, :D] = gain_one
    dbias[:, :D] = shift_one


def load_images(images, x):
    x[...] = jnp.zeros_like(x)
    for i in range(IMGS):
        x[ROWS * i : ROWS * i + SEQ, :] = images[i].astype(F32)


STATE = (
    ((R, D), BF16),
    ((3, R, D), BF16),
    ((IMGS * PAIRS * 2, ROWS, ROWS), BF16),
    ((R, D), BF16),
    ((R, D), F32),
    ((R, D), BF16),
    ((4, R, D), BF16),
    ((4, R, D), BF16),
)
WEIGHTS = (
    ((BLOCKS, D, D), BF16),
    ((FF, D), BF16),
    ((1, BIAS), F32),
    ((1, GAIN), F32),
)
BIAS_ROW = ((1, BIAS), F32)
GAIN_ROW = ((1, GAIN), F32)
HALF_BLOCKS = ((BLOCKS // 2, D, D), BF16)
MOVE_SCRATCH = (((D, D), BF16), ((2, SLABS, 128), F32))


def wires(*part):
    return [jax.ShapeDtypeStruct((16 * slab_rows(*part), 128), BF16)] * 2


def shapes(specs):
    return [jax.ShapeDtypeStruct(*spec) for spec in specs]


def scratch(specs):
    return [pltpu.VMEM(*spec) for spec in specs]


def first_forward_kernel(*refs):
    me, images, pieces, refs = refs[0][0], refs[1], refs[2:10], refs[10:]
    stream, weights, state = refs[0], refs[1:5], refs[5:13]
    x, rhs, small = refs[13:]
    assemble(me, pieces, *weights, rhs, small)
    load_images(images, x)
    forward(x, *weights, *state, stream)


def second_layer_kernel(*refs):
    me, live, stream, cotangent, pieces, refs = refs[0][0], refs[1], refs[2], refs[3], refs[4:12], refs[12:]
    activations, grad, sent, refs = refs[0], refs[1], refs[2:4], refs[4:]
    weights, state, refs = refs[:4], refs[4:12], refs[12:]
    low, gpre, gqkv, gmix, tmp, dw, dw2, dbias, dgain, rhs, small = refs
    assemble(me, pieces, *weights, rhs, small)
    forward(stream, *weights, *state, grad)
    for i in range(IMGS):
        alive = jnp.where(live[i] > 0, 1.0, 0.0)
        activations[i] = (grad[ROWS * i : ROWS * i + SEQ, :] * alive).astype(BF16)
    load_images(cotangent, grad)
    for i in range(IMGS):
        alive = jnp.where(live[i] > 0, 1.0, 0.0)
        grad[ROWS * i : ROWS * i + ROWS, :] = grad[ROWS * i : ROWS * i + ROWS, :] * alive
    w, w2, _, gain_row = weights
    xna, qkv, probs, mixed, middle, xnb, act, slope = state
    mlp_backward(
        w, w2, gain_row, mixed, middle, xnb, act, slope, grad, low, gpre, gmix, tmp, dw.at[4:8], dw.at[3], dw2, dbias, dgain
    )
    attention_backward(qkv, probs, gmix, gqkv)
    projection_backward(stream, w, gain_row, xna, gqkv, grad, tmp, dw, dbias, dgain)
    disperse(me, dw, dw2, dbias, dgain, sent, rhs, small)


def first_mlp_backward_kernel(
    me, grad_in, w, w2, gain_row, mixed, middle, xnb, act, slope, grad, gmix, dw_out, dbias, dgain, *refs
):
    sent, (low, gpre, tmp, dw, dw2, rhs) = refs[:2], refs[2:]
    grad[...] = grad_in[...]
    dbias[...] = jnp.zeros_like(dbias)
    dgain[...] = jnp.zeros_like(dgain)
    mlp_backward(
        w, w2, gain_row, mixed, middle, xnb, act, slope, grad, low, gpre, gmix, tmp, dw, dw_out, dw2, dbias, dgain
    )
    disperse(me[0], dw, dw2, None, None, sent, rhs, None)


def first_attention_backward_kernel(qkv, probs, gmix, gqkv):
    attention_backward(qkv, probs, gmix, gqkv)


def first_projection_backward_kernel(
    me, images, grad_in, gqkv, dw_out, dbias_in, dgain_in, w, gain_row, xna, input_grad, *refs
):
    sent, (x, grad, tmp, dw, dbias, dgain, rhs, small) = refs[:2], refs[2:]
    load_images(images, x)
    grad[...] = grad_in[...]
    dbias[...] = dbias_in[...]
    dgain[...] = dgain_in[...]
    dw[3] = dw_out[...]
    projection_backward(x, w, gain_row, xna, gqkv, grad, tmp, dw, dbias, dgain)
    for i in range(IMGS):
        input_grad[i] = grad[ROWS * i : ROWS * i + SEQ, :].astype(BF16)
    disperse(me[0], dw, None, dbias, dgain, sent, rhs, small)


def whole(count):
    return [pl.BlockSpec(memory_space=pltpu.VMEM)] * count


def scalar(count):
    return [pl.BlockSpec(memory_space=pltpu.SMEM)] * count


def params():
    return pltpu.CompilerParams(vmem_limit_bytes=VMEM_LIMIT)


def cost(flops):
    return pl.CostEstimate(flops=flops, bytes_accessed=20_000_000, transcendentals=0)


def run_first_forward(me, images, pieces):
    outs = [jax.ShapeDtypeStruct((R, D), F32)] + shapes(WEIGHTS) + shapes(STATE)
    out = pl.pallas_call(
        first_forward_kernel,
        out_shape=outs,
        in_specs=scalar(1) + whole(9),
        out_specs=whole(len(outs)),
        scratch_shapes=scratch((((R, D), F32),) + MOVE_SCRATCH),
        compiler_params=params(),
        cost_estimate=cost(33_000_000_000),
        name="first_forward",
    )(me, images, *pieces)
    return out[0], out[1:5], out[5:]


def run_second_layer(me, live, stream, cotangent, pieces):
    outs = [jax.ShapeDtypeStruct(cotangent.shape, BF16), jax.ShapeDtypeStruct((R, D), F32)]
    outs += wires(BLOCKS, True, True)
    low, full = ((R, D), BF16), ((R, D), F32)
    back = (low, low, ((3, R, D), BF16), low, full, ((BLOCKS, D, D), BF16), ((FF, D), BF16), BIAS_ROW, GAIN_ROW)
    return pl.pallas_call(
        second_layer_kernel,
        out_shape=outs,
        in_specs=scalar(2) + whole(10),
        out_specs=whole(len(outs)),
        scratch_shapes=scratch(WEIGHTS + STATE + back + MOVE_SCRATCH),
        compiler_params=params(),
        cost_estimate=cost(65_000_000_000),
        name="second_layer",
    )(me, live, stream, cotangent, *pieces)


def run_first_mlp_backward(me, grad, weights, state):
    w, w2, _, gain_row = weights
    low, full = ((R, D), BF16), ((R, D), F32)
    outs = shapes((full, low, ((D, D), BF16), BIAS_ROW, GAIN_ROW)) + wires(BLOCKS // 2, True, False)
    return pl.pallas_call(
        first_mlp_backward_kernel,
        out_shape=outs,
        in_specs=scalar(1) + whole(9),
        out_specs=whole(len(outs)),
        scratch_shapes=scratch((low, low, full, HALF_BLOCKS, ((FF, D), BF16), MOVE_SCRATCH[0])),
        compiler_params=params(),
        cost_estimate=cost(20_000_000_000),
        name="first_mlp_backward",
    )(me, grad, w, w2, gain_row, *state[3:])


def run_first_attention_backward(gmix, state):
    return pl.pallas_call(
        first_attention_backward_kernel,
        out_shape=jax.ShapeDtypeStruct((3, R, D), BF16),
        in_specs=whole(3),
        out_specs=whole(1)[0],
        compiler_params=params(),
        cost_estimate=cost(12_000_000_000),
        name="first_attention_backward",
    )(state[1], state[2], gmix)


def run_first_projection_backward(me, images, grad, gqkv, rest, weights, state):
    w, _, _, gain_row = weights
    full = ((R, D), F32)
    outs = [jax.ShapeDtypeStruct(images.shape, BF16)] + wires(BLOCKS // 2, False, True)
    return pl.pallas_call(
        first_projection_backward_kernel,
        out_shape=outs,
        in_specs=scalar(1) + whole(9),
        out_specs=whole(len(outs)),
        scratch_shapes=scratch((full, full, full, HALF_BLOCKS, BIAS_ROW, GAIN_ROW) + MOVE_SCRATCH),
        compiler_params=params(),
        cost_estimate=cost(10_000_000_000),
        name="first_projection_backward",
    )(me, images, grad, gqkv, *rest, w, gain_row, state[0])


def chunk_table():
    table = []
    for c in range(3):
        for i in range(12):
            for b in range(3):
                table.append((0, i * 9 + b * 3 + c, c, b * 12 + i))
            table.append((1, i * 3 + c, c, 36 + i))
            for b in range(4):
                table.append((2, i * 12 + b * 3 + c, c, 48 + b * 12 + i))
        for i in range(48):
            table.append((3, i * 3 + c, c, 96 + i))
    return table


def pack_kernel(qkv, out, fc1, fc2, gains, biases, slab_a, slab_b, stage_a, stage_b):
    flats, stages = (qkv, out, fc1, fc2), (stage_a, stage_b)
    for stage in stages:
        stage[SMALL:SLAB, :] = jnp.zeros((SLAB - SMALL, 128), F32)
    for which, piece, c, row in chunk_table():
        both = flats[which][:, 128 * piece : 128 * piece + 128].astype(F32)
        row += c * THIRD
        for layer in range(LAYERS):
            stages[layer][row : row + 1, :] = both[layer : layer + 1]
    for layer in range(LAYERS):
        stages[layer][SMALL : SMALL + 1, 0:SHARD_BIAS] = biases[...].astype(F32)[layer : layer + 1]
        stages[layer][SMALL + 1 : SMALL + 2, 0:SHARD_GAIN] = gains[...].astype(F32)[layer : layer + 1]
    slab_a[...] = stage_a[...].astype(BF16)
    slab_b[...] = stage_b[...].astype(BF16)


def run_pack(qkv, out, fc1, fc2, gains, biases):
    return pl.pallas_call(
        pack_kernel,
        out_shape=[jax.ShapeDtypeStruct((SLAB, 128), BF16)] * 2,
        in_specs=whole(6),
        out_specs=whole(2),
        scratch_shapes=[pltpu.VMEM((SLAB, 128), F32)] * 2,
        name="pack",
    )(qkv, out, fc1, fc2, gains, biases)


def unpack_kernel(first, second, *refs):
    flats, (gains, biases) = refs[:4], refs[4:]
    start = slab_rows(BLOCKS // 2, True, False)
    for which, piece, c, row in chunk_table():
        lanes = slice(128 * piece, 128 * piece + 128)
        at = start + c * 48 + row if which < 2 else c * 96 + row - 48
        flats[which][0:1, lanes] = first[at : at + 1, :]
        at = c * THIRD + row
        flats[which][1:2, lanes] = second[at : at + 1, :]
    for layer, slab in enumerate((first, second)):
        biases[layer : layer + 1, :] = slab[SMALL : SMALL + 1, 0:SHARD_BIAS]
        gains[layer : layer + 1, :] = slab[SMALL + 1 : SMALL + 2, 0:SHARD_GAIN]


def run_unpack(first, second, widths):
    return pl.pallas_call(
        unpack_kernel,
        out_shape=[jax.ShapeDtypeStruct((LAYERS, width), F32) for width in widths],
        in_specs=whole(2),
        out_specs=whole(6),
        name="unpack",
    )(first, second)


def swap(value, bits):
    return lax.ppermute(value, "fsdp", [(i, i ^ bits) for i in range(SLABS)])


XY_STEPS = (2, 4, 6)
Z_STEPS = (8, 16, 24)


def spread(value, steps):
    return [value] + [swap(value, bits) for bits in steps]


def gather_column(slab):
    return jnp.concatenate(spread(slab, Z_STEPS), axis=0)


def with_other_core(near):
    return near + [swap(part, 1) for part in near]


def across_cores(keep, send):
    return keep.astype(F32) + swap(send, 1).astype(F32)


def collect(total, steps):
    rows = total.shape[0] // 4
    mine = total[:rows]
    for place, bits in enumerate(steps):
        part = total[rows * (place + 1) : rows * (place + 2)]
        mine = mine + swap(part.astype(BF16), bits).astype(F32)
    return mine


def join(first, second):
    return jnp.concatenate([first.reshape(4, -1, 128), second.reshape(4, -1, 128)], axis=1).reshape(-1, 128)


def to_slabs(qkv, out, fc1, fc2, gains, biases):
    blocks = jnp.concatenate(
        [
            qkv.reshape(SLABS, 12, 3, D).transpose(0, 2, 1, 3).reshape(SLABS, 36, D),
            out.reshape(SLABS, 12, D),
            fc1.reshape(SLABS, 12, 4, D).transpose(0, 2, 1, 3).reshape(SLABS, 48, D),
            fc2.reshape(SLABS, 48, D),
        ],
        axis=1,
    )
    thirds = blocks.reshape(SLABS, THIRD, 3, 128).transpose(0, 2, 1, 3).reshape(SLABS, 3 * THIRD, 128)
    tail = jnp.zeros((SLABS, SLAB - SMALL, 128), blocks.dtype)
    tail = tail.at[:, 0, :SHARD_BIAS].set(biases.reshape(SLABS, SHARD_BIAS))
    tail = tail.at[:, 1, :SHARD_GAIN].set(gains.reshape(SLABS, SHARD_GAIN))
    return jnp.concatenate([thirds, tail], axis=1)


def from_slabs(slabs):
    blocks = slabs[:, :SMALL].reshape(SLABS, 3, THIRD, 128).transpose(0, 2, 1, 3).reshape(SLABS, THIRD, D)
    return (
        blocks[:, :36].reshape(SLABS, 3, 12, D).transpose(0, 2, 1, 3).reshape(-1),
        blocks[:, 36:48].reshape(-1),
        blocks[:, 48:96].reshape(SLABS, 4, 12, D).transpose(0, 2, 1, 3).reshape(-1),
        blocks[:, 96:].reshape(-1),
        slabs[:, SMALL + 1, :SHARD_GAIN].reshape(-1),
        slabs[:, SMALL, :SHARD_BIAS].reshape(-1),
    )


def plain_gather(flats, layer):
    return to_slabs(*(lax.all_gather(flat[layer], "fsdp", axis=0, tiled=True) for flat in flats))


def plain_pieces(slabs):
    return [
        jnp.concatenate([slabs[core + 2 * xy + 8 * z] for z in range(4)], axis=0)
        for core in range(2)
        for xy in range(4)
    ]


def plain_slabs(keep, send):
    halves = [half.reshape(4, 4, -1, 128).astype(F32) for half in (keep, send)]
    return jnp.stack([halves[d & 1][(d >> 1) & 3, d >> 3] for d in range(SLABS)])


def plain_totals(slabs):
    return [lax.psum_scatter(flat, "fsdp", scatter_dimension=0, tiled=True) for flat in from_slabs(slabs)]


def joined_slabs(mlp, attention):
    parts = []
    for c in range(3):
        parts += [attention[:, 48 * c : 48 * c + 48], mlp[:, 96 * c : 96 * c + 96]]
    return jnp.concatenate(parts + [attention[:, THIRD:]], axis=1)


def local(images, live_counts, qkv_weight, out_weight, fc1_weight, fc2_weight, norm_gains, biases, cotangent):
    flats = (qkv_weight, out_weight, fc1_weight, fc2_weight, norm_gains, biases)
    if lax.axis_size("fsdp") == SLABS:
        return local_tree(images, live_counts, flats, cotangent)
    me = jnp.zeros((1,), jnp.int32)
    pieces_b = plain_pieces(plain_gather(flats, 1))
    stream, weights, state = run_first_forward(me, images, plain_pieces(plain_gather(flats, 0)))
    activations, grad, *second = run_second_layer(me, live_counts, stream, cotangent, pieces_b)
    grad, gmix, *rest, mlp_keep, mlp_send = run_first_mlp_backward(me, grad, weights, state)
    gqkv = run_first_attention_backward(gmix, state)
    input_grad, *attention = run_first_projection_backward(me, images, grad, gqkv, rest, weights, state)
    first = joined_slabs(plain_slabs(mlp_keep, mlp_send), plain_slabs(*attention))
    results = [jnp.stack(both) for both in zip(plain_totals(first), plain_totals(plain_slabs(*second)))]
    return (activations, input_grad, *results)


def local_tree(images, live_counts, flats, cotangent):
    me = lax.axis_index("fsdp").astype(jnp.int32).reshape(1)
    slab_a, slab_b = run_pack(*flats)
    column_a, slab_b = lax.optimization_barrier((gather_column(slab_a), slab_b))
    own_a, *near_a = spread(column_a, XY_STEPS)
    near_a, column_b = lax.optimization_barrier((near_a, gather_column(slab_b)))
    stream, weights, state = run_first_forward(me, images, with_other_core([own_a] + near_a))
    near_b, stream = lax.optimization_barrier((spread(column_b, XY_STEPS), stream))
    pieces_b = with_other_core(near_b)
    activations, grad, *second = run_second_layer(me, live_counts, stream, cotangent, pieces_b)

    second = across_cores(*second)
    grad, gmix, *rest, mlp_keep, mlp_send = run_first_mlp_backward(me, grad, weights, state)
    second, gmix, mlp_keep, mlp_send = lax.optimization_barrier((second, gmix, mlp_keep, mlp_send))

    second, mlp = collect(second, XY_STEPS), across_cores(mlp_keep, mlp_send)
    gqkv = run_first_attention_backward(gmix, state)
    second, mlp, gqkv = lax.optimization_barrier((second, mlp, gqkv))

    second, mlp = collect(second, Z_STEPS), collect(mlp, XY_STEPS)
    input_grad, *attention = run_first_projection_backward(me, images, grad, gqkv, rest, weights, state)
    second, mlp, attention = lax.optimization_barrier((second, mlp, attention))

    attention = collect(across_cores(*attention), XY_STEPS)
    first = collect(join(mlp, attention), Z_STEPS)
    results = run_unpack(first, second, [flat.shape[1] for flat in flats])
    return (activations, input_grad, *results)


def solution(mesh):
    flat = P(None, "fsdp")
    image = P("fsdp", None, None)
    return jax.shard_map(
        local,
        mesh=mesh,
        in_specs=(image, P("fsdp")) + (flat,) * 6 + (image,),
        out_specs=(image, image) + (flat,) * 6,
        check_vma=False,
    )
```

```python
import jax
import jax.numpy as jnp
from jax import lax
from jax.experimental import pallas as pl
from jax.experimental.pallas import tpu as pltpu
from jax.sharding import PartitionSpec as P

D = 384
FF = 1536
SEQ = 197
HEAD = 64
LAYERS = 2
NORM_EPS = 1e-06
ROOT_HALF = 0.7071067811865476
INV_ROOT_TAU = 0.3989422804014327

IMGS = 3
ROWS = 208
R = IMGS * ROWS
CHUNK = 48
CHUNKS = R // CHUNK
PAIRS = 3

SLABS = 32
THIRD = 144
SMALL = 3 * THIRD
SLAB = SMALL + 16
BLOCKS = 8
SHARD_BIAS = 120
SHARD_GAIN = 24
BIAS = 6 * D + FF
GAIN = 2 * D

F32 = jnp.float32
BF16 = jnp.bfloat16
VMEM_LIMIT = 56 * 1024 * 1024


def dot_nn(a, b):
    return lax.dot_general(a, b, (((1,), (0,)), ((), ())), preferred_element_type=F32)


def dot_nt(a, b):
    return lax.dot_general(a, b, (((1,), (1,)), ((), ())), preferred_element_type=F32)


def dot_tn(a, b):
    return lax.dot_general(a, b, (((0,), (0,)), ((), ())), preferred_element_type=F32)


def chunk_rows(i):
    return pl.ds(pl.multiple_of(i * CHUNK, CHUNK), CHUNK)


def block_rows(j):
    return pl.ds(pl.multiple_of(j * D, D), D)


def image_rows(i):
    return pl.ds(pl.multiple_of(i * ROWS, 16), ROWS)


def pair_lanes(p):
    return pl.ds(pl.multiple_of(p * 128, 128), 128)


def normalize(x):
    centred = x - jnp.mean(x, axis=-1, keepdims=True)
    inv_std = lax.rsqrt(jnp.mean(centred * centred, axis=-1, keepdims=True) + NORM_EPS)
    return centred * inv_std, inv_std


def digits(index, size):
    whole = jnp.floor((index.astype(F32) + 0.5) * (1.0 / size)).astype(jnp.int32)
    return whole, index - whole * size


def order_codes(shape, axis):
    index = lax.broadcasted_iota(jnp.int32, shape, axis)
    block, rest = digits(index, 48)
    dev, row = digits(rest, 12)
    return (block * 4 + dev) * 12 + row


def slab_codes(shape, axis, low, blocks):
    index = lax.broadcasted_iota(jnp.int32, shape, axis)
    rel, rest = digits(index, 12 * blocks)
    block, row = digits(rest, 12)
    dev = jnp.bitwise_xor(rel, low)
    return (block * 4 + dev) * 12 + row


def owner_mask(size, per_owner):
    lane = lax.broadcasted_iota(jnp.int32, (1, size), 1)
    owner, place = digits(lane, per_owner)
    rows = lax.broadcasted_iota(jnp.int32, (SLABS, size), 0)
    return rows == owner, place


def place_matrix(place, size):
    rows = lax.broadcasted_iota(jnp.int32, (128, size), 0)
    return jnp.where(rows == place, 1.0, 0.0).astype(BF16)


def assemble(me, pieces, w, w2, bias_row, gain_row, rhs, small):
    low = jnp.bitwise_and(me, 3)
    order = jnp.where(
        order_codes((D, 1), 0) == slab_codes((1, D), 1, low, BLOCKS), 1.0, 0.0
    ).astype(BF16)

    for zr in range(4):
        for yr in range(2):
            g = jnp.bitwise_xor(lax.shift_right_logical(me, 2), yr + 2 * zr)
            for xr in range(2):
                for cr in range(2):
                    xy = xr + 2 * yr
                    piece, base = pieces[4 * cr + xy], zr * SLAB
                    d = jnp.bitwise_xor(me, cr + 2 * xy + 8 * zr)
                    s = xr * 2 + cr
                    for c in range(3):
                        lanes = slice(128 * c, 128 * c + 128)
                        start = base + c * THIRD
                        rhs[96 * s : 96 * s + 96, lanes] = piece[start : start + 96, :]
                        w2[pl.ds(pl.multiple_of(48 * d, 16), 48), lanes] = piece[start + 96 : start + THIRD, :]
                    tail = piece[base + SMALL : base + SLAB, :].astype(F32)
                    small[0, pl.ds(d, 1), :] = tail[0:1, :]
                    small[1, pl.ds(d, 1), :] = tail[1:2, :]
            sorted_rows = dot_nn(order, rhs[...]).astype(BF16)
            for b in range(BLOCKS):
                w[b, pl.ds(pl.multiple_of(48 * g, 16), 48), :] = sorted_rows[48 * b : 48 * b + 48]
    for slot, size, per_owner, row in ((0, BIAS, SHARD_BIAS, bias_row), (1, GAIN, SHARD_GAIN, gain_row)):
        mine, place = owner_mask(size, per_owner)
        spread = dot_nn(small[slot].astype(BF16), place_matrix(place, size))
        row[...] = jnp.sum(jnp.where(mine, spread, 0.0), axis=0, keepdims=True)


def slab_rows(blocks, with_w2, with_small):
    return 3 * (12 * blocks + 48 * with_w2) + 16 * with_small


def disperse(me, dw, dw2, bias_row, gain_row, wires, rhs, small):
    blocks = dw.shape[0]
    size = 48 * blocks
    third = slab_rows(blocks, dw2 is not None, False) // 3
    stride = slab_rows(blocks, dw2 is not None, bias_row is not None)
    low = jnp.bitwise_and(me, 3)
    order = jnp.where(
        slab_codes((size, 1), 0, low, blocks) == order_codes((1, size), 1), 1.0, 0.0
    ).astype(BF16)
    if bias_row is not None:
        for slot, width, per_owner, row in ((0, BIAS, SHARD_BIAS, bias_row), (1, GAIN, SHARD_GAIN, gain_row)):
            mine, place = owner_mask(width, per_owner)
            spread = jnp.where(mine, row[...], 0.0).astype(BF16)
            small[slot] = dot_nt(spread, place_matrix(place, width))
    head_row = lax.broadcasted_iota(jnp.int32, (16, 128), 0)

    def group(zr, carry):
        for yr in range(2):
            g = jnp.bitwise_xor(lax.shift_right_logical(me, 2), yr + 2 * zr)
            for b in range(blocks):
                rhs[48 * b : 48 * b + 48, :] = dw[b, pl.ds(pl.multiple_of(48 * g, 16), 48), :]
            slabs = dot_nn(order, rhs[0:size, :]).astype(BF16)
            for xr in range(2):
                for cr in range(2):
                    out = wires[cr]
                    xy = xr + 2 * yr
                    d = jnp.bitwise_xor(me, cr + 2 * xy + 8 * zr)
                    s = xr * 2 + cr
                    base = pl.multiple_of(xy * (4 * stride) + zr * stride, 16)
                    for c in range(3):
                        lanes = slice(128 * c, 128 * c + 128)
                        start = base + c * third
                        rows = 12 * blocks
                        out[pl.ds(start, rows), :] = slabs[rows * s : rows * s + rows, lanes]
                        if dw2 is not None:
                            out[pl.ds(start + rows, 48), :] = dw2[pl.ds(pl.multiple_of(48 * d, 16), 48), lanes]
                    if bias_row is not None:
                        tail = jnp.where(
                            head_row == 0,
                            small[0, pl.ds(d, 1), :],
                            jnp.where(head_row == 1, small[1, pl.ds(d, 1), :], 0.0),
                        )
                        out[pl.ds(base + 3 * third, 16), :] = tail.astype(BF16)
        return carry

    lax.fori_loop(0, 4, group, 0, unroll=True)


def forward(x, w, w2, bias_row, gain_row, xna, qkv, probs, mixed, middle, xnb, act, slope, tmp):
    def norm_a(i, carry):
        rows = chunk_rows(i)
        normal, _ = normalize(x[rows, :])
        xna[rows, :] = (normal * gain_row[:, :D] + bias_row[:, :D]).astype(BF16)
        return carry

    lax.fori_loop(0, CHUNKS, norm_a, 0, unroll=True)
    for b in range(3):
        part = dot_nn(xna[...], w[b])
        if b == 0:
            part = part + bias_row[:, D : 2 * D]
        if b == 2:
            part = part + bias_row[:, 2 * D : 3 * D]
        qkv[b] = part.astype(BF16)

    lane = lax.broadcasted_iota(jnp.int32, (1, 128), 1)
    first = lane < HEAD
    halves = (first.astype(F32).astype(BF16), 1 - first.astype(F32).astype(BF16))
    real_key = lax.broadcasted_iota(jnp.int32, (ROWS, 1), 0) < SEQ

    def image_attention(img, carry):
        rows = image_rows(img)

        def pair_attention(pair, inner):
            lanes = pair_lanes(pair)
            q, k, v = qkv[0, rows, lanes], qkv[1, rows, lanes], qkv[2, rows, lanes]
            outs = []
            for h in range(2):
                scores = dot_nt(k, q * halves[h]) * (HEAD**-0.5)
                scores = jnp.where(real_key, scores, -1e30)
                raised = jnp.exp(scores - jnp.max(scores, axis=0, keepdims=True))
                share = raised * (1.0 / jnp.sum(raised, axis=0, keepdims=True))
                share = share.astype(BF16)
                probs[(img * PAIRS + pair) * 2 + h] = share
                outs.append(dot_tn(share, v))
            mixed[rows, lanes] = jnp.where(first, outs[0], outs[1]).astype(BF16)
            return inner

        return lax.fori_loop(0, PAIRS, pair_attention, carry, unroll=True)

    lax.fori_loop(0, IMGS, image_attention, 0, unroll=True)
    middle[...] = x[...] + (dot_nn(mixed[...], w[3]) + bias_row[:, 3 * D : 4 * D])

    def norm_b(i, carry):
        rows = chunk_rows(i)
        normal, _ = normalize(middle[rows, :])
        xnb[rows, :] = (normal * gain_row[:, D:] + bias_row[:, 4 * D : 5 * D]).astype(BF16)
        return carry

    lax.fori_loop(0, CHUNKS, norm_b, 0, unroll=True)

    def hidden(j, carry):
        tmp[...] = dot_nn(xnb[...], w[4 + j])
        shift = bias_row[:, pl.ds(pl.multiple_of(6 * D + j * D, 128), D)]

        def gelu(i, inner):
            rows = chunk_rows(i)
            pre = tmp[rows, :] + shift
            half = 0.5 * (1.0 + lax.erf(pre * ROOT_HALF))
            act[j, rows, :] = (pre * half).astype(BF16)
            slope[j, rows, :] = (half + pre * jnp.exp(-0.5 * pre * pre) * INV_ROOT_TAU).astype(BF16)
            return inner

        return lax.fori_loop(0, CHUNKS, gelu, carry, unroll=True)

    lax.fori_loop(0, 4, hidden, 0, unroll=True)
    tmp[...] = middle[...] + bias_row[:, 5 * D : 6 * D]
    for j in range(4):
        tmp[...] += dot_nn(act[j], w2[D * j : D * j + D, :])


def column_total(values):
    return jnp.sum(values.astype(F32), axis=0, keepdims=True)


def norm_back(source, gain, grad, tmp, low):
    def step(i, totals):
        rows = chunk_rows(i)
        back = tmp[rows, :]
        normal, inv_std = normalize(source[rows, :])
        scaled = back * gain
        first_mean = jnp.mean(scaled, axis=-1, keepdims=True)
        cross_mean = jnp.mean(scaled * normal, axis=-1, keepdims=True)
        result = grad[rows, :] + inv_std * (scaled - first_mean - normal * cross_mean)
        grad[rows, :] = result
        result_low = result.astype(BF16)
        if low is not None:
            low[rows, :] = result_low
        return (
            totals[0] + jnp.sum(back * normal, axis=0, keepdims=True),
            totals[1] + jnp.sum(back, axis=0, keepdims=True),
            totals[2] + jnp.sum(result_low.astype(F32), axis=0, keepdims=True),
        )

    zero = jnp.zeros((1, D), F32)
    return lax.fori_loop(0, CHUNKS, step, (zero, zero, zero), unroll=True)


def mlp_backward(w, w2, gain_row, mixed, middle, xnb, act, slope, grad, low, gpre, gmix, tmp, dw, dw_out, dw2, dbias, dgain):
    low[...] = grad[...].astype(BF16)
    dbias[:, 5 * D : 6 * D] = column_total(low[...])

    def hidden(j, carry):
        dw2[block_rows(j), :] = dot_tn(act[j], low[...]).astype(BF16)
        pre = (dot_nt(low[...], w2[block_rows(j), :]) * slope[j].astype(F32)).astype(BF16)
        gpre[...] = pre
        dbias[:, pl.ds(pl.multiple_of(6 * D + j * D, 128), D)] = column_total(gpre[...])
        dw[j] = dot_tn(xnb[...], gpre[...]).astype(BF16)
        part = dot_nt(gpre[...], w[4 + j])
        tmp[...] = jnp.where(j == 0, part, tmp[...] + part)
        return carry

    lax.fori_loop(0, 4, hidden, 0, unroll=True)
    gain_two, shift_two, bias_out = norm_back(middle, gain_row[:, D:], grad, tmp, low)
    dgain[:, D:] = gain_two
    dbias[:, 4 * D : 5 * D] = shift_two
    dbias[:, 3 * D : 4 * D] = bias_out
    dw_out[...] = dot_tn(mixed[...], low[...]).astype(BF16)
    gmix[...] = dot_nt(low[...], w[3]).astype(BF16)


def attention_backward(qkv, probs, gmix, gqkv):
    lane = lax.broadcasted_iota(jnp.int32, (1, 128), 1)
    first = lane < HEAD
    halves = (first.astype(F32).astype(BF16), 1 - first.astype(F32).astype(BF16))

    def image_attention(img, carry):
        rows = image_rows(img)

        def pair_attention(pair, inner):
            lanes = pair_lanes(pair)
            q, k, v = qkv[0, rows, lanes], qkv[1, rows, lanes], qkv[2, rows, lanes]
            gm = gmix[rows, lanes]
            grads = ([], [], [])
            for h in range(2):
                share = probs[(img * PAIRS + pair) * 2 + h]
                grad_share = dot_nt(v, gm * halves[h])
                full = share.astype(F32)
                row_dot = jnp.sum(full * grad_share, axis=0, keepdims=True)
                grad_scores = (full * (grad_share - row_dot)).astype(BF16)
                grads[0].append(dot_tn(grad_scores, k) * (HEAD**-0.5))
                grads[1].append(dot_nn(grad_scores, q) * (HEAD**-0.5))
                grads[2].append(dot_nn(share, gm))
            for b in range(3):
                gqkv[b, rows, lanes] = jnp.where(first, grads[b][0], grads[b][1]).astype(BF16)
            return inner

        return lax.fori_loop(0, PAIRS, pair_attention, carry, unroll=True)

    lax.fori_loop(0, IMGS, image_attention, 0, unroll=True)


def projection_backward(x, w, gain_row, xna, gqkv, grad, tmp, dw, dbias, dgain):
    for b in range(3):
        dw[b] = dot_tn(xna[...], gqkv[b]).astype(BF16)
        part = dot_nt(gqkv[b], w[b])
        tmp[...] = part if b == 0 else tmp[...] + part
    dbias[:, D : 2 * D] = column_total(gqkv[0])
    dbias[:, 2 * D : 3 * D] = column_total(gqkv[2])
    gain_one, shift_one, _ = norm_back(x, gain_row[:, :D], grad, tmp, None)
    dgain[:, :D] = gain_one
    dbias[:, :D] = shift_one


def load_images(images, x):
    x[...] = jnp.zeros_like(x)
    for i in range(IMGS):
        x[ROWS * i : ROWS * i + SEQ, :] = images[i].astype(F32)


STATE = (
    ((R, D), BF16),
    ((3, R, D), BF16),
    ((IMGS * PAIRS * 2, ROWS, ROWS), BF16),
    ((R, D), BF16),
    ((R, D), F32),
    ((R, D), BF16),
    ((4, R, D), BF16),
    ((4, R, D), BF16),
)
WEIGHTS = (
    ((BLOCKS, D, D), BF16),
    ((FF, D), BF16),
    ((1, BIAS), F32),
    ((1, GAIN), F32),
)
BIAS_ROW = ((1, BIAS), F32)
GAIN_ROW = ((1, GAIN), F32)
HALF_BLOCKS = ((BLOCKS // 2, D, D), BF16)
MOVE_SCRATCH = (((D, D), BF16), ((2, SLABS, 128), F32))


def wires(*part):
    return [jax.ShapeDtypeStruct((16 * slab_rows(*part), 128), BF16)] * 2


def shapes(specs):
    return [jax.ShapeDtypeStruct(*spec) for spec in specs]


def scratch(specs):
    return [pltpu.VMEM(*spec) for spec in specs]


def first_forward_kernel(*refs):
    me, images, pieces, refs = refs[0][0], refs[1], refs[2:10], refs[10:]
    stream, weights, state = refs[0], refs[1:5], refs[5:13]
    x, rhs, small = refs[13:]
    assemble(me, pieces, *weights, rhs, small)
    load_images(images, x)
    forward(x, *weights, *state, stream)


def second_layer_kernel(*refs):
    me, live, stream, cotangent, pieces, refs = refs[0][0], refs[1], refs[2], refs[3], refs[4:12], refs[12:]
    activations, grad, sent, refs = refs[0], refs[1], refs[2:4], refs[4:]
    weights, state, refs = refs[:4], refs[4:12], refs[12:]
    low, gpre, gqkv, gmix, tmp, dw, dw2, dbias, dgain, rhs, small = refs
    assemble(me, pieces, *weights, rhs, small)
    forward(stream, *weights, *state, grad)
    for i in range(IMGS):
        alive = jnp.where(live[i] > 0, 1.0, 0.0)
        activations[i] = (grad[ROWS * i : ROWS * i + SEQ, :] * alive).astype(BF16)
    load_images(cotangent, grad)
    for i in range(IMGS):
        alive = jnp.where(live[i] > 0, 1.0, 0.0)
        grad[ROWS * i : ROWS * i + ROWS, :] = grad[ROWS * i : ROWS * i + ROWS, :] * alive
    w, w2, _, gain_row = weights
    xna, qkv, probs, mixed, middle, xnb, act, slope = state
    mlp_backward(
        w, w2, gain_row, mixed, middle, xnb, act, slope, grad, low, gpre, gmix, tmp, dw.at[4:8], dw.at[3], dw2, dbias, dgain
    )
    attention_backward(qkv, probs, gmix, gqkv)
    projection_backward(stream, w, gain_row, xna, gqkv, grad, tmp, dw, dbias, dgain)
    disperse(me, dw, dw2, dbias, dgain, sent, rhs, small)


def first_mlp_backward_kernel(
    me, grad_in, w, w2, gain_row, mixed, middle, xnb, act, slope, grad, gmix, dw_out, dbias, dgain, *refs
):
    sent, (low, gpre, tmp, dw, dw2, rhs) = refs[:2], refs[2:]
    grad[...] = grad_in[...]
    dbias[...] = jnp.zeros_like(dbias)
    dgain[...] = jnp.zeros_like(dgain)
    mlp_backward(
        w, w2, gain_row, mixed, middle, xnb, act, slope, grad, low, gpre, gmix, tmp, dw, dw_out, dw2, dbias, dgain
    )
    disperse(me[0], dw, dw2, None, None, sent, rhs, None)


def first_attention_backward_kernel(qkv, probs, gmix, gqkv):
    attention_backward(qkv, probs, gmix, gqkv)


def first_projection_backward_kernel(
    me, images, grad_in, gqkv, dw_out, dbias_in, dgain_in, w, gain_row, xna, input_grad, *refs
):
    sent, (x, grad, tmp, dw, dbias, dgain, rhs, small) = refs[:2], refs[2:]
    load_images(images, x)
    grad[...] = grad_in[...]
    dbias[...] = dbias_in[...]
    dgain[...] = dgain_in[...]
    dw[3] = dw_out[...]
    projection_backward(x, w, gain_row, xna, gqkv, grad, tmp, dw, dbias, dgain)
    for i in range(IMGS):
        input_grad[i] = grad[ROWS * i : ROWS * i + SEQ, :].astype(BF16)
    disperse(me[0], dw, None, dbias, dgain, sent, rhs, small)


def whole(count):
    return [pl.BlockSpec(memory_space=pltpu.VMEM)] * count


def scalar(count):
    return [pl.BlockSpec(memory_space=pltpu.SMEM)] * count


def params():
    return pltpu.CompilerParams(vmem_limit_bytes=VMEM_LIMIT)


def cost(flops):
    return pl.CostEstimate(flops=flops, bytes_accessed=20_000_000, transcendentals=0)


def run_first_forward(me, images, pieces):
    outs = [jax.ShapeDtypeStruct((R, D), F32)] + shapes(WEIGHTS) + shapes(STATE)
    out = pl.pallas_call(
        first_forward_kernel,
        out_shape=outs,
        in_specs=scalar(1) + whole(9),
        out_specs=whole(len(outs)),
        scratch_shapes=scratch((((R, D), F32),) + MOVE_SCRATCH),
        compiler_params=params(),
        cost_estimate=cost(33_000_000_000),
        name="first_forward",
    )(me, images, *pieces)
    return out[0], out[1:5], out[5:]


def run_second_layer(me, live, stream, cotangent, pieces):
    outs = [jax.ShapeDtypeStruct(cotangent.shape, BF16), jax.ShapeDtypeStruct((R, D), F32)]
    outs += wires(BLOCKS, True, True)
    low, full = ((R, D), BF16), ((R, D), F32)
    back = (low, low, ((3, R, D), BF16), low, full, ((BLOCKS, D, D), BF16), ((FF, D), BF16), BIAS_ROW, GAIN_ROW)
    return pl.pallas_call(
        second_layer_kernel,
        out_shape=outs,
        in_specs=scalar(2) + whole(10),
        out_specs=whole(len(outs)),
        scratch_shapes=scratch(WEIGHTS + STATE + back + MOVE_SCRATCH),
        compiler_params=params(),
        cost_estimate=cost(65_000_000_000),
        name="second_layer",
    )(me, live, stream, cotangent, *pieces)


def run_first_mlp_backward(me, grad, weights, state):
    w, w2, _, gain_row = weights
    low, full = ((R, D), BF16), ((R, D), F32)
    outs = shapes((full, low, ((D, D), BF16), BIAS_ROW, GAIN_ROW)) + wires(BLOCKS // 2, True, False)
    return pl.pallas_call(
        first_mlp_backward_kernel,
        out_shape=outs,
        in_specs=scalar(1) + whole(9),
        out_specs=whole(len(outs)),
        scratch_shapes=scratch((low, low, full, HALF_BLOCKS, ((FF, D), BF16), MOVE_SCRATCH[0])),
        compiler_params=params(),
        cost_estimate=cost(20_000_000_000),
        name="first_mlp_backward",
    )(me, grad, w, w2, gain_row, *state[3:])


def run_first_attention_backward(gmix, state):
    return pl.pallas_call(
        first_attention_backward_kernel,
        out_shape=jax.ShapeDtypeStruct((3, R, D), BF16),
        in_specs=whole(3),
        out_specs=whole(1)[0],
        compiler_params=params(),
        cost_estimate=cost(12_000_000_000),
        name="first_attention_backward",
    )(state[1], state[2], gmix)


def run_first_projection_backward(me, images, grad, gqkv, rest, weights, state):
    w, _, _, gain_row = weights
    full = ((R, D), F32)
    outs = [jax.ShapeDtypeStruct(images.shape, BF16)] + wires(BLOCKS // 2, False, True)
    return pl.pallas_call(
        first_projection_backward_kernel,
        out_shape=outs,
        in_specs=scalar(1) + whole(9),
        out_specs=whole(len(outs)),
        scratch_shapes=scratch((full, full, full, HALF_BLOCKS, BIAS_ROW, GAIN_ROW) + MOVE_SCRATCH),
        compiler_params=params(),
        cost_estimate=cost(10_000_000_000),
        name="first_projection_backward",
    )(me, images, grad, gqkv, *rest, w, gain_row, state[0])


def chunk_table():
    table = []
    for c in range(3):
        for i in range(12):
            for b in range(3):
                table.append((0, i * 9 + b * 3 + c, c, b * 12 + i))
            table.append((1, i * 3 + c, c, 36 + i))
            for b in range(4):
                table.append((2, i * 12 + b * 3 + c, c, 48 + b * 12 + i))
        for i in range(48):
            table.append((3, i * 3 + c, c, 96 + i))
    return table


def pack_kernel(qkv, out, fc1, fc2, gains, biases, slab_a, slab_b, stage_a, stage_b):
    flats, stages = (qkv, out, fc1, fc2), (stage_a, stage_b)
    for stage in stages:
        stage[SMALL:SLAB, :] = jnp.zeros((SLAB - SMALL, 128), F32)
    for which, piece, c, row in chunk_table():
        both = flats[which][:, 128 * piece : 128 * piece + 128].astype(F32)
        row += c * THIRD
        for layer in range(LAYERS):
            stages[layer][row : row + 1, :] = both[layer : layer + 1]
    for layer in range(LAYERS):
        stages[layer][SMALL : SMALL + 1, 0:SHARD_BIAS] = biases[...].astype(F32)[layer : layer + 1]
        stages[layer][SMALL + 1 : SMALL + 2, 0:SHARD_GAIN] = gains[...].astype(F32)[layer : layer + 1]
    slab_a[...] = stage_a[...].astype(BF16)
    slab_b[...] = stage_b[...].astype(BF16)


def run_pack(qkv, out, fc1, fc2, gains, biases):
    return pl.pallas_call(
        pack_kernel,
        out_shape=[jax.ShapeDtypeStruct((SLAB, 128), BF16)] * 2,
        in_specs=whole(6),
        out_specs=whole(2),
        scratch_shapes=[pltpu.VMEM((SLAB, 128), F32)] * 2,
        name="pack",
    )(qkv, out, fc1, fc2, gains, biases)


def unpack_kernel(first, second, *refs):
    flats, (gains, biases) = refs[:4], refs[4:]
    start = slab_rows(BLOCKS // 2, True, False)
    for which, piece, c, row in chunk_table():
        lanes = slice(128 * piece, 128 * piece + 128)
        at = start + c * 48 + row if which < 2 else c * 96 + row - 48
        flats[which][0:1, lanes] = first[at : at + 1, :]
        at = c * THIRD + row
        flats[which][1:2, lanes] = second[at : at + 1, :]
    for layer, slab in enumerate((first, second)):
        biases[layer : layer + 1, :] = slab[SMALL : SMALL + 1, 0:SHARD_BIAS]
        gains[layer : layer + 1, :] = slab[SMALL + 1 : SMALL + 2, 0:SHARD_GAIN]


def run_unpack(first, second, widths):
    return pl.pallas_call(
        unpack_kernel,
        out_shape=[jax.ShapeDtypeStruct((LAYERS, width), F32) for width in widths],
        in_specs=whole(2),
        out_specs=whole(6),
        name="unpack",
    )(first, second)


def swap(value, bits):
    return lax.ppermute(value, "fsdp", [(i, i ^ bits) for i in range(SLABS)])


XY_STEPS = (2, 4, 6)
Z_STEPS = (8, 16, 24)


def spread(value, steps):
    return [value] + [swap(value, bits) for bits in steps]


def gather_column(slab):
    return jnp.concatenate(spread(slab, Z_STEPS), axis=0)


def with_other_core(near):
    return near + [swap(part, 1) for part in near]


def across_cores(keep, send):
    return keep.astype(F32) + swap(send, 1).astype(F32)


def collect(total, steps):
    rows = total.shape[0] // 4
    mine = total[:rows]
    for place, bits in enumerate(steps):
        part = total[rows * (place + 1) : rows * (place + 2)]
        mine = mine + swap(part.astype(BF16), bits).astype(F32)
    return mine


def join(first, second):
    return jnp.concatenate([first.reshape(4, -1, 128), second.reshape(4, -1, 128)], axis=1).reshape(-1, 128)


def to_slabs(qkv, out, fc1, fc2, gains, biases):
    blocks = jnp.concatenate(
        [
            qkv.reshape(SLABS, 12, 3, D).transpose(0, 2, 1, 3).reshape(SLABS, 36, D),
            out.reshape(SLABS, 12, D),
            fc1.reshape(SLABS, 12, 4, D).transpose(0, 2, 1, 3).reshape(SLABS, 48, D),
            fc2.reshape(SLABS, 48, D),
        ],
        axis=1,
    )
    thirds = blocks.reshape(SLABS, THIRD, 3, 128).transpose(0, 2, 1, 3).reshape(SLABS, 3 * THIRD, 128)
    tail = jnp.zeros((SLABS, SLAB - SMALL, 128), blocks.dtype)
    tail = tail.at[:, 0, :SHARD_BIAS].set(biases.reshape(SLABS, SHARD_BIAS))
    tail = tail.at[:, 1, :SHARD_GAIN].set(gains.reshape(SLABS, SHARD_GAIN))
    return jnp.concatenate([thirds, tail], axis=1)


def from_slabs(slabs):
    blocks = slabs[:, :SMALL].reshape(SLABS, 3, THIRD, 128).transpose(0, 2, 1, 3).reshape(SLABS, THIRD, D)
    return (
        blocks[:, :36].reshape(SLABS, 3, 12, D).transpose(0, 2, 1, 3).reshape(-1),
        blocks[:, 36:48].reshape(-1),
        blocks[:, 48:96].reshape(SLABS, 4, 12, D).transpose(0, 2, 1, 3).reshape(-1),
        blocks[:, 96:].reshape(-1),
        slabs[:, SMALL + 1, :SHARD_GAIN].reshape(-1),
        slabs[:, SMALL, :SHARD_BIAS].reshape(-1),
    )


def plain_gather(flats, layer):
    return to_slabs(*(lax.all_gather(flat[layer], "fsdp", axis=0, tiled=True) for flat in flats))


def plain_pieces(slabs):
    return [
        jnp.concatenate([slabs[core + 2 * xy + 8 * z] for z in range(4)], axis=0)
        for core in range(2)
        for xy in range(4)
    ]


def plain_slabs(keep, send):
    halves = [half.reshape(4, 4, -1, 128).astype(F32) for half in (keep, send)]
    return jnp.stack([halves[d & 1][(d >> 1) & 3, d >> 3] for d in range(SLABS)])


def plain_totals(slabs):
    return [lax.psum_scatter(flat, "fsdp", scatter_dimension=0, tiled=True) for flat in from_slabs(slabs)]


def joined_slabs(mlp, attention):
    parts = []
    for c in range(3):
        parts += [attention[:, 48 * c : 48 * c + 48], mlp[:, 96 * c : 96 * c + 96]]
    return jnp.concatenate(parts + [attention[:, THIRD:]], axis=1)


def local(images, live_counts, qkv_weight, out_weight, fc1_weight, fc2_weight, norm_gains, biases, cotangent):
    flats = (qkv_weight, out_weight, fc1_weight, fc2_weight, norm_gains, biases)
    if lax.axis_size("fsdp") == SLABS:
        return local_tree(images, live_counts, flats, cotangent)
    me = jnp.zeros((1,), jnp.int32)
    pieces_b = plain_pieces(plain_gather(flats, 1))
    stream, weights, state = run_first_forward(me, images, plain_pieces(plain_gather(flats, 0)))
    activations, grad, *second = run_second_layer(me, live_counts, stream, cotangent, pieces_b)
    grad, gmix, *rest, mlp_keep, mlp_send = run_first_mlp_backward(me, grad, weights, state)
    gqkv = run_first_attention_backward(gmix, state)
    input_grad, *attention = run_first_projection_backward(me, images, grad, gqkv, rest, weights, state)
    first = joined_slabs(plain_slabs(mlp_keep, mlp_send), plain_slabs(*attention))
    results = [jnp.stack(both) for both in zip(plain_totals(first), plain_totals(plain_slabs(*second)))]
    return (activations, input_grad, *results)


def local_tree(images, live_counts, flats, cotangent):
    me = lax.axis_index("fsdp").astype(jnp.int32).reshape(1)
    slab_a, slab_b = run_pack(*flats)
    column_a, slab_b = lax.optimization_barrier((gather_column(slab_a), slab_b))
    own_a, *near_a = spread(column_a, XY_STEPS)
    near_a, column_b = lax.optimization_barrier((near_a, gather_column(slab_b)))
    stream, weights, state = run_first_forward(me, images, with_other_core([own_a] + near_a))
    near_b, stream = lax.optimization_barrier((spread(column_b, XY_STEPS), stream))
    pieces_b = with_other_core(near_b)
    activations, grad, *second = run_second_layer(me, live_counts, stream, cotangent, pieces_b)

    quarter = 4 * SLAB
    sides = across_cores(*(half[quarter : 3 * quarter] for half in second))
    sides, grad = lax.optimization_barrier((sides, grad))
    mine, corner = (across_cores(*(half[at : at + quarter] for half in second)) for at in (0, 3 * quarter))
    from_x, from_y = (swap(sides[quarter * n : quarter * n + quarter].astype(BF16), XY_STEPS[n]) for n in range(2))
    grad, gmix, *rest, mlp_keep, mlp_send = run_first_mlp_backward(me, grad, weights, state)
    from_x, from_y, corner, gmix, mlp_keep, mlp_send = lax.optimization_barrier(
        (from_x, from_y, corner, gmix, mlp_keep, mlp_send)
    )
    mlp = across_cores(mlp_keep, mlp_send)
    second = mine + from_x.astype(F32) + from_y.astype(F32) + swap(corner.astype(BF16), XY_STEPS[2]).astype(F32)
    gqkv = run_first_attention_backward(gmix, state)
    second, mlp, gqkv = lax.optimization_barrier((second, mlp, gqkv))

    second, mlp = collect(second, Z_STEPS), collect(mlp, XY_STEPS)
    input_grad, *attention = run_first_projection_backward(me, images, grad, gqkv, rest, weights, state)
    second, mlp, attention = lax.optimization_barrier((second, mlp, attention))

    attention = collect(across_cores(*attention), XY_STEPS)
    first = collect(join(mlp, attention), Z_STEPS)
    results = run_unpack(first, second, [flat.shape[1] for flat in flats])
    return (activations, input_grad, *results)


def solution(mesh):
    flat = P(None, "fsdp")
    image = P("fsdp", None, None)
    return jax.shard_map(
        local,
        mesh=mesh,
        in_specs=(image, P("fsdp")) + (flat,) * 6 + (image,),
        out_specs=(image, image) + (flat,) * 6,
        check_vma=False,
    )
```

```python
import jax
import jax.numpy as jnp
from jax import lax
from jax.experimental import pallas as pl
from jax.experimental.pallas import tpu as pltpu
from jax.sharding import PartitionSpec as P

D = 384
FF = 1536
SEQ = 197
HEAD = 64
LAYERS = 2
NORM_EPS = 1e-06
ROOT_HALF = 0.7071067811865476
INV_ROOT_TAU = 0.3989422804014327

IMGS = 3
ROWS = 208
R = IMGS * ROWS
CHUNK = 48
CHUNKS = R // CHUNK
PAIRS = 3

SLABS = 32
THIRD = 144
SMALL = 3 * THIRD
SLAB = SMALL + 16
BLOCKS = 8
SHARD_BIAS = 120
SHARD_GAIN = 24
BIAS = 6 * D + FF
GAIN = 2 * D

F32 = jnp.float32
BF16 = jnp.bfloat16
VMEM_LIMIT = 56 * 1024 * 1024


def dot_nn(a, b):
    return lax.dot_general(a, b, (((1,), (0,)), ((), ())), preferred_element_type=F32)


def dot_nt(a, b):
    return lax.dot_general(a, b, (((1,), (1,)), ((), ())), preferred_element_type=F32)


def dot_tn(a, b):
    return lax.dot_general(a, b, (((0,), (0,)), ((), ())), preferred_element_type=F32)


def chunk_rows(i):
    return pl.ds(pl.multiple_of(i * CHUNK, CHUNK), CHUNK)


def block_rows(j):
    return pl.ds(pl.multiple_of(j * D, D), D)


def image_rows(i):
    return pl.ds(pl.multiple_of(i * ROWS, 16), ROWS)


def pair_lanes(p):
    return pl.ds(pl.multiple_of(p * 128, 128), 128)


def normalize(x):
    centred = x - jnp.mean(x, axis=-1, keepdims=True)
    inv_std = lax.rsqrt(jnp.mean(centred * centred, axis=-1, keepdims=True) + NORM_EPS)
    return centred * inv_std, inv_std


def digits(index, size):
    whole = jnp.floor((index.astype(F32) + 0.5) * (1.0 / size)).astype(jnp.int32)
    return whole, index - whole * size


def order_codes(shape, axis):
    index = lax.broadcasted_iota(jnp.int32, shape, axis)
    block, rest = digits(index, 48)
    dev, row = digits(rest, 12)
    return (block * 4 + dev) * 12 + row


def slab_codes(shape, axis, low, blocks):
    index = lax.broadcasted_iota(jnp.int32, shape, axis)
    rel, rest = digits(index, 12 * blocks)
    block, row = digits(rest, 12)
    dev = jnp.bitwise_xor(rel, low)
    return (block * 4 + dev) * 12 + row


def owner_mask(size, per_owner):
    lane = lax.broadcasted_iota(jnp.int32, (1, size), 1)
    owner, place = digits(lane, per_owner)
    rows = lax.broadcasted_iota(jnp.int32, (SLABS, size), 0)
    return rows == owner, place


def place_matrix(place, size):
    rows = lax.broadcasted_iota(jnp.int32, (128, size), 0)
    return jnp.where(rows == place, 1.0, 0.0).astype(BF16)


def assemble(me, pieces, w, w2, bias_row, gain_row, rhs, small):
    low = jnp.bitwise_and(me, 3)
    order = jnp.where(
        order_codes((D, 1), 0) == slab_codes((1, D), 1, low, BLOCKS), 1.0, 0.0
    ).astype(BF16)

    for zr in range(4):
        for yr in range(2):
            g = jnp.bitwise_xor(lax.shift_right_logical(me, 2), yr + 2 * zr)
            for xr in range(2):
                for cr in range(2):
                    xy = xr + 2 * yr
                    piece, base = pieces[4 * cr + xy], zr * SLAB
                    d = jnp.bitwise_xor(me, cr + 2 * xy + 8 * zr)
                    s = xr * 2 + cr
                    for c in range(3):
                        lanes = slice(128 * c, 128 * c + 128)
                        start = base + c * THIRD
                        rhs[96 * s : 96 * s + 96, lanes] = piece[start : start + 96, :]
                        w2[pl.ds(pl.multiple_of(48 * d, 16), 48), lanes] = piece[start + 96 : start + THIRD, :]
                    tail = piece[base + SMALL : base + SLAB, :].astype(F32)
                    small[0, pl.ds(d, 1), :] = tail[0:1, :]
                    small[1, pl.ds(d, 1), :] = tail[1:2, :]
            sorted_rows = dot_nn(order, rhs[...]).astype(BF16)
            for b in range(BLOCKS):
                w[b, pl.ds(pl.multiple_of(48 * g, 16), 48), :] = sorted_rows[48 * b : 48 * b + 48]
    for slot, size, per_owner, row in ((0, BIAS, SHARD_BIAS, bias_row), (1, GAIN, SHARD_GAIN, gain_row)):
        mine, place = owner_mask(size, per_owner)
        spread = dot_nn(small[slot].astype(BF16), place_matrix(place, size))
        row[...] = jnp.sum(jnp.where(mine, spread, 0.0), axis=0, keepdims=True)


def slab_rows(blocks, with_w2, with_small):
    return 3 * (12 * blocks + 48 * with_w2) + 16 * with_small


def disperse(me, dw, dw2, bias_row, gain_row, wires, rhs, small):
    blocks = dw.shape[0]
    size = 48 * blocks
    third = slab_rows(blocks, dw2 is not None, False) // 3
    stride = slab_rows(blocks, dw2 is not None, bias_row is not None)
    low = jnp.bitwise_and(me, 3)
    order = jnp.where(
        slab_codes((size, 1), 0, low, blocks) == order_codes((1, size), 1), 1.0, 0.0
    ).astype(BF16)
    if bias_row is not None:
        for slot, width, per_owner, row in ((0, BIAS, SHARD_BIAS, bias_row), (1, GAIN, SHARD_GAIN, gain_row)):
            mine, place = owner_mask(width, per_owner)
            spread = jnp.where(mine, row[...], 0.0).astype(BF16)
            small[slot] = dot_nt(spread, place_matrix(place, width))
    head_row = lax.broadcasted_iota(jnp.int32, (16, 128), 0)

    def group(zr, carry):
        for yr in range(2):
            g = jnp.bitwise_xor(lax.shift_right_logical(me, 2), yr + 2 * zr)
            for b in range(blocks):
                rhs[48 * b : 48 * b + 48, :] = dw[b, pl.ds(pl.multiple_of(48 * g, 16), 48), :]
            slabs = dot_nn(order, rhs[0:size, :]).astype(BF16)
            for xr in range(2):
                for cr in range(2):
                    out = wires[cr]
                    xy = xr + 2 * yr
                    d = jnp.bitwise_xor(me, cr + 2 * xy + 8 * zr)
                    s = xr * 2 + cr
                    base = pl.multiple_of(xy * (4 * stride) + zr * stride, 16)
                    for c in range(3):
                        lanes = slice(128 * c, 128 * c + 128)
                        start = base + c * third
                        rows = 12 * blocks
                        out[pl.ds(start, rows), :] = slabs[rows * s : rows * s + rows, lanes]
                        if dw2 is not None:
                            out[pl.ds(start + rows, 48), :] = dw2[pl.ds(pl.multiple_of(48 * d, 16), 48), lanes]
                    if bias_row is not None:
                        tail = jnp.where(
                            head_row == 0,
                            small[0, pl.ds(d, 1), :],
                            jnp.where(head_row == 1, small[1, pl.ds(d, 1), :], 0.0),
                        )
                        out[pl.ds(base + 3 * third, 16), :] = tail.astype(BF16)
        return carry

    lax.fori_loop(0, 4, group, 0)


def forward(x, w, w2, bias_row, gain_row, xna, qkv, probs, mixed, middle, xnb, act, slope, tmp, rolled):
    def norm_a(i, carry):
        rows = chunk_rows(i)
        normal, _ = normalize(x[rows, :])
        xna[rows, :] = (normal * gain_row[:, :D] + bias_row[:, :D]).astype(BF16)
        return carry

    lax.fori_loop(0, CHUNKS, norm_a, 0, unroll=True)
    for b in range(3):
        part = dot_nn(xna[...], w[b])
        if b == 0:
            part = part + bias_row[:, D : 2 * D]
        if b == 2:
            part = part + bias_row[:, 2 * D : 3 * D]
        qkv[b] = part.astype(BF16)

    lane = lax.broadcasted_iota(jnp.int32, (1, 128), 1)
    first = lane < HEAD
    halves = (first.astype(F32).astype(BF16), 1 - first.astype(F32).astype(BF16))
    real_key = lax.broadcasted_iota(jnp.int32, (ROWS, 1), 0) < SEQ

    def image_attention(img, carry):
        rows = image_rows(img)

        def pair_attention(pair, inner):
            lanes = pair_lanes(pair)
            q, k, v = qkv[0, rows, lanes], qkv[1, rows, lanes], qkv[2, rows, lanes]
            outs = []
            for h in range(2):
                scores = dot_nt(k, q * halves[h]) * (HEAD**-0.5)
                scores = jnp.where(real_key, scores, -1e30)
                raised = jnp.exp(scores - jnp.max(scores, axis=0, keepdims=True))
                share = raised * (1.0 / jnp.sum(raised, axis=0, keepdims=True))
                share = share.astype(BF16)
                probs[(img * PAIRS + pair) * 2 + h] = share
                outs.append(dot_tn(share, v))
            mixed[rows, lanes] = jnp.where(first, outs[0], outs[1]).astype(BF16)
            return inner

        return lax.fori_loop(0, PAIRS, pair_attention, carry, unroll=True)

    lax.fori_loop(0, IMGS, image_attention, 0, unroll=1 if rolled else IMGS)
    middle[...] = x[...] + (dot_nn(mixed[...], w[3]) + bias_row[:, 3 * D : 4 * D])

    def norm_b(i, carry):
        rows = chunk_rows(i)
        normal, _ = normalize(middle[rows, :])
        xnb[rows, :] = (normal * gain_row[:, D:] + bias_row[:, 4 * D : 5 * D]).astype(BF16)
        return carry

    lax.fori_loop(0, CHUNKS, norm_b, 0, unroll=True)

    def hidden(j, carry):
        tmp[...] = dot_nn(xnb[...], w[4 + j])
        shift = bias_row[:, pl.ds(pl.multiple_of(6 * D + j * D, 128), D)]

        def gelu(i, inner):
            rows = chunk_rows(i)
            pre = tmp[rows, :] + shift
            half = 0.5 * (1.0 + lax.erf(pre * ROOT_HALF))
            act[j, rows, :] = (pre * half).astype(BF16)
            slope[j, rows, :] = (half + pre * jnp.exp(-0.5 * pre * pre) * INV_ROOT_TAU).astype(BF16)
            return inner

        return lax.fori_loop(0, CHUNKS, gelu, carry, unroll=True)

    lax.fori_loop(0, 4, hidden, 0)
    tmp[...] = middle[...] + bias_row[:, 5 * D : 6 * D]
    for j in range(4):
        tmp[...] += dot_nn(act[j], w2[D * j : D * j + D, :])


def column_total(values):
    return jnp.sum(values.astype(F32), axis=0, keepdims=True)


def norm_back(source, gain, grad, tmp, low):
    def step(i, totals):
        rows = chunk_rows(i)
        back = tmp[rows, :]
        normal, inv_std = normalize(source[rows, :])
        scaled = back * gain
        first_mean = jnp.mean(scaled, axis=-1, keepdims=True)
        cross_mean = jnp.mean(scaled * normal, axis=-1, keepdims=True)
        result = grad[rows, :] + inv_std * (scaled - first_mean - normal * cross_mean)
        grad[rows, :] = result
        result_low = result.astype(BF16)
        if low is not None:
            low[rows, :] = result_low
        return (
            totals[0] + jnp.sum(back * normal, axis=0, keepdims=True),
            totals[1] + jnp.sum(back, axis=0, keepdims=True),
            totals[2] + jnp.sum(result_low.astype(F32), axis=0, keepdims=True),
        )

    zero = jnp.zeros((1, D), F32)
    return lax.fori_loop(0, CHUNKS, step, (zero, zero, zero), unroll=True)


def mlp_backward(w, w2, gain_row, mixed, middle, xnb, act, slope, grad, low, gpre, gmix, tmp, dw, dw_out, dw2, dbias, dgain):
    low[...] = grad[...].astype(BF16)
    dbias[:, 5 * D : 6 * D] = column_total(low[...])

    def hidden(j, carry):
        dw2[block_rows(j), :] = dot_tn(act[j], low[...]).astype(BF16)
        pre = (dot_nt(low[...], w2[block_rows(j), :]) * slope[j].astype(F32)).astype(BF16)
        gpre[...] = pre
        dbias[:, pl.ds(pl.multiple_of(6 * D + j * D, 128), D)] = column_total(gpre[...])
        dw[j] = dot_tn(xnb[...], gpre[...]).astype(BF16)
        part = dot_nt(gpre[...], w[4 + j])
        tmp[...] = jnp.where(j == 0, part, tmp[...] + part)
        return carry

    lax.fori_loop(0, 4, hidden, 0)
    gain_two, shift_two, bias_out = norm_back(middle, gain_row[:, D:], grad, tmp, low)
    dgain[:, D:] = gain_two
    dbias[:, 4 * D : 5 * D] = shift_two
    dbias[:, 3 * D : 4 * D] = bias_out
    dw_out[...] = dot_tn(mixed[...], low[...]).astype(BF16)
    gmix[...] = dot_nt(low[...], w[3]).astype(BF16)


def attention_backward(qkv, probs, gmix, gqkv):
    lane = lax.broadcasted_iota(jnp.int32, (1, 128), 1)
    first = lane < HEAD
    halves = (first.astype(F32).astype(BF16), 1 - first.astype(F32).astype(BF16))

    def image_attention(img, carry):
        rows = image_rows(img)

        def pair_attention(pair, inner):
            lanes = pair_lanes(pair)
            q, k, v = qkv[0, rows, lanes], qkv[1, rows, lanes], qkv[2, rows, lanes]
            gm = gmix[rows, lanes]
            grads = ([], [], [])
            for h in range(2):
                share = probs[(img * PAIRS + pair) * 2 + h]
                grad_share = dot_nt(v, gm * halves[h])
                full = share.astype(F32)
                row_dot = jnp.sum(full * grad_share, axis=0, keepdims=True)
                grad_scores = (full * (grad_share - row_dot)).astype(BF16)
                grads[0].append(dot_tn(grad_scores, k) * (HEAD**-0.5))
                grads[1].append(dot_nn(grad_scores, q) * (HEAD**-0.5))
                grads[2].append(dot_nn(share, gm))
            for b in range(3):
                gqkv[b, rows, lanes] = jnp.where(first, grads[b][0], grads[b][1]).astype(BF16)
            return inner

        return lax.fori_loop(0, PAIRS, pair_attention, carry, unroll=True)

    lax.fori_loop(0, IMGS, image_attention, 0, unroll=True)


def projection_backward(x, w, gain_row, xna, gqkv, grad, tmp, dw, dbias, dgain):
    for b in range(3):
        dw[b] = dot_tn(xna[...], gqkv[b]).astype(BF16)
        part = dot_nt(gqkv[b], w[b])
        tmp[...] = part if b == 0 else tmp[...] + part
    dbias[:, D : 2 * D] = column_total(gqkv[0])
    dbias[:, 2 * D : 3 * D] = column_total(gqkv[2])
    gain_one, shift_one, _ = norm_back(x, gain_row[:, :D], grad, tmp, None)
    dgain[:, :D] = gain_one
    dbias[:, :D] = shift_one


def load_images(images, x):
    x[...] = jnp.zeros_like(x)
    for i in range(IMGS):
        x[ROWS * i : ROWS * i + SEQ, :] = images[i].astype(F32)


STATE = (
    ((R, D), BF16),
    ((3, R, D), BF16),
    ((IMGS * PAIRS * 2, ROWS, ROWS), BF16),
    ((R, D), BF16),
    ((R, D), F32),
    ((R, D), BF16),
    ((4, R, D), BF16),
    ((4, R, D), BF16),
)
WEIGHTS = (
    ((BLOCKS, D, D), BF16),
    ((FF, D), BF16),
    ((1, BIAS), F32),
    ((1, GAIN), F32),
)
BIAS_ROW = ((1, BIAS), F32)
GAIN_ROW = ((1, GAIN), F32)
HALF_BLOCKS = ((BLOCKS // 2, D, D), BF16)
MOVE_SCRATCH = (((D, D), BF16), ((2, SLABS, 128), F32))


def wires(*part):
    return [jax.ShapeDtypeStruct((16 * slab_rows(*part), 128), BF16)] * 2


def shapes(specs):
    return [jax.ShapeDtypeStruct(*spec) for spec in specs]


def scratch(specs):
    return [pltpu.VMEM(*spec) for spec in specs]


def first_forward_kernel(*refs):
    me, images, pieces, refs = refs[0][0], refs[1], refs[2:10], refs[10:]
    stream, weights, state = refs[0], refs[1:5], refs[5:13]
    x, rhs, small = refs[13:]
    assemble(me, pieces, *weights, rhs, small)
    load_images(images, x)
    forward(x, *weights, *state, stream, True)


def second_layer_kernel(*refs):
    me, live, stream, cotangent, pieces, refs = refs[0][0], refs[1], refs[2], refs[3], refs[4:12], refs[12:]
    activations, grad, sent, refs = refs[0], refs[1], refs[2:4], refs[4:]
    weights, state, refs = refs[:4], refs[4:12], refs[12:]
    low, gpre, gqkv, gmix, tmp, dw, dw2, dbias, dgain, rhs, small = refs
    assemble(me, pieces, *weights, rhs, small)
    forward(stream, *weights, *state, grad, False)
    for i in range(IMGS):
        alive = jnp.where(live[i] > 0, 1.0, 0.0)
        activations[i] = (grad[ROWS * i : ROWS * i + SEQ, :] * alive).astype(BF16)
    load_images(cotangent, grad)
    for i in range(IMGS):
        alive = jnp.where(live[i] > 0, 1.0, 0.0)
        grad[ROWS * i : ROWS * i + ROWS, :] = grad[ROWS * i : ROWS * i + ROWS, :] * alive
    w, w2, _, gain_row = weights
    xna, qkv, probs, mixed, middle, xnb, act, slope = state
    mlp_backward(
        w, w2, gain_row, mixed, middle, xnb, act, slope, grad, low, gpre, gmix, tmp, dw.at[4:8], dw.at[3], dw2, dbias, dgain
    )
    attention_backward(qkv, probs, gmix, gqkv)
    projection_backward(stream, w, gain_row, xna, gqkv, grad, tmp, dw, dbias, dgain)
    disperse(me, dw, dw2, dbias, dgain, sent, rhs, small)


def first_mlp_backward_kernel(
    me, grad_in, w, w2, gain_row, mixed, middle, xnb, act, slope, grad, gmix, dw_out, dbias, dgain, *refs
):
    sent, (low, gpre, tmp, dw, dw2, rhs) = refs[:2], refs[2:]
    grad[...] = grad_in[...]
    dbias[...] = jnp.zeros_like(dbias)
    dgain[...] = jnp.zeros_like(dgain)
    mlp_backward(
        w, w2, gain_row, mixed, middle, xnb, act, slope, grad, low, gpre, gmix, tmp, dw, dw_out, dw2, dbias, dgain
    )
    disperse(me[0], dw, dw2, None, None, sent, rhs, None)


def first_attention_backward_kernel(qkv, probs, gmix, gqkv):
    attention_backward(qkv, probs, gmix, gqkv)


def first_projection_backward_kernel(
    me, images, grad_in, gqkv, dw_out, dbias_in, dgain_in, w, gain_row, xna, input_grad, *refs
):
    sent, (x, grad, tmp, dw, dbias, dgain, rhs, small) = refs[:2], refs[2:]
    load_images(images, x)
    grad[...] = grad_in[...]
    dbias[...] = dbias_in[...]
    dgain[...] = dgain_in[...]
    dw[3] = dw_out[...]
    projection_backward(x, w, gain_row, xna, gqkv, grad, tmp, dw, dbias, dgain)
    for i in range(IMGS):
        input_grad[i] = grad[ROWS * i : ROWS * i + SEQ, :].astype(BF16)
    disperse(me[0], dw, None, dbias, dgain, sent, rhs, small)


def whole(count):
    return [pl.BlockSpec(memory_space=pltpu.VMEM)] * count


def scalar(count):
    return [pl.BlockSpec(memory_space=pltpu.SMEM)] * count


def params():
    return pltpu.CompilerParams(vmem_limit_bytes=VMEM_LIMIT)


def cost(flops):
    return pl.CostEstimate(flops=flops, bytes_accessed=20_000_000, transcendentals=0)


def run_first_forward(me, images, pieces):
    outs = [jax.ShapeDtypeStruct((R, D), F32)] + shapes(WEIGHTS) + shapes(STATE)
    out = pl.pallas_call(
        first_forward_kernel,
        out_shape=outs,
        in_specs=scalar(1) + whole(9),
        out_specs=whole(len(outs)),
        scratch_shapes=scratch((((R, D), F32),) + MOVE_SCRATCH),
        compiler_params=params(),
        cost_estimate=cost(33_000_000_000),
        name="first_forward",
    )(me, images, *pieces)
    return out[0], out[1:5], out[5:]


def run_second_layer(me, live, stream, cotangent, pieces):
    outs = [jax.ShapeDtypeStruct(cotangent.shape, BF16), jax.ShapeDtypeStruct((R, D), F32)]
    outs += wires(BLOCKS, True, True)
    low, full = ((R, D), BF16), ((R, D), F32)
    back = (low, low, ((3, R, D), BF16), low, full, ((BLOCKS, D, D), BF16), ((FF, D), BF16), BIAS_ROW, GAIN_ROW)
    return pl.pallas_call(
        second_layer_kernel,
        out_shape=outs,
        in_specs=scalar(2) + whole(10),
        out_specs=whole(len(outs)),
        scratch_shapes=scratch(WEIGHTS + STATE + back + MOVE_SCRATCH),
        compiler_params=params(),
        cost_estimate=cost(65_000_000_000),
        name="second_layer",
    )(me, live, stream, cotangent, *pieces)


def run_first_mlp_backward(me, grad, weights, state):
    w, w2, _, gain_row = weights
    low, full = ((R, D), BF16), ((R, D), F32)
    outs = shapes((full, low, ((D, D), BF16), BIAS_ROW, GAIN_ROW)) + wires(BLOCKS // 2, True, False)
    return pl.pallas_call(
        first_mlp_backward_kernel,
        out_shape=outs,
        in_specs=scalar(1) + whole(9),
        out_specs=whole(len(outs)),
        scratch_shapes=scratch((low, low, full, HALF_BLOCKS, ((FF, D), BF16), MOVE_SCRATCH[0])),
        compiler_params=params(),
        cost_estimate=cost(20_000_000_000),
        name="first_mlp_backward",
    )(me, grad, w, w2, gain_row, *state[3:])


def run_first_attention_backward(gmix, state):
    return pl.pallas_call(
        first_attention_backward_kernel,
        out_shape=jax.ShapeDtypeStruct((3, R, D), BF16),
        in_specs=whole(3),
        out_specs=whole(1)[0],
        compiler_params=params(),
        cost_estimate=cost(12_000_000_000),
        name="first_attention_backward",
    )(state[1], state[2], gmix)


def run_first_projection_backward(me, images, grad, gqkv, rest, weights, state):
    w, _, _, gain_row = weights
    full = ((R, D), F32)
    outs = [jax.ShapeDtypeStruct(images.shape, BF16)] + wires(BLOCKS // 2, False, True)
    return pl.pallas_call(
        first_projection_backward_kernel,
        out_shape=outs,
        in_specs=scalar(1) + whole(9),
        out_specs=whole(len(outs)),
        scratch_shapes=scratch((full, full, full, HALF_BLOCKS, BIAS_ROW, GAIN_ROW) + MOVE_SCRATCH),
        compiler_params=params(),
        cost_estimate=cost(10_000_000_000),
        name="first_projection_backward",
    )(me, images, grad, gqkv, *rest, w, gain_row, state[0])


def chunk_table():
    table = []
    for c in range(3):
        for i in range(12):
            for b in range(3):
                table.append((0, i * 9 + b * 3 + c, c, b * 12 + i))
            table.append((1, i * 3 + c, c, 36 + i))
            for b in range(4):
                table.append((2, i * 12 + b * 3 + c, c, 48 + b * 12 + i))
        for i in range(48):
            table.append((3, i * 3 + c, c, 96 + i))
    return table


def pack_kernel(qkv, out, fc1, fc2, gains, biases, slab_a, slab_b, stage_a, stage_b):
    flats, stages = (qkv, out, fc1, fc2), (stage_a, stage_b)
    for stage in stages:
        stage[SMALL:SLAB, :] = jnp.zeros((SLAB - SMALL, 128), F32)
    for which, piece, c, row in chunk_table():
        both = flats[which][:, 128 * piece : 128 * piece + 128].astype(F32)
        row += c * THIRD
        for layer in range(LAYERS):
            stages[layer][row : row + 1, :] = both[layer : layer + 1]
    for layer in range(LAYERS):
        stages[layer][SMALL : SMALL + 1, 0:SHARD_BIAS] = biases[...].astype(F32)[layer : layer + 1]
        stages[layer][SMALL + 1 : SMALL + 2, 0:SHARD_GAIN] = gains[...].astype(F32)[layer : layer + 1]
    slab_a[...] = stage_a[...].astype(BF16)
    slab_b[...] = stage_b[...].astype(BF16)


def run_pack(qkv, out, fc1, fc2, gains, biases):
    return pl.pallas_call(
        pack_kernel,
        out_shape=[jax.ShapeDtypeStruct((SLAB, 128), BF16)] * 2,
        in_specs=whole(6),
        out_specs=whole(2),
        scratch_shapes=[pltpu.VMEM((SLAB, 128), F32)] * 2,
        name="pack",
    )(qkv, out, fc1, fc2, gains, biases)


def unpack_kernel(first, second, *refs):
    flats, (gains, biases) = refs[:4], refs[4:]
    start = slab_rows(BLOCKS // 2, True, False)
    for which, piece, c, row in chunk_table():
        lanes = slice(128 * piece, 128 * piece + 128)
        at = start + c * 48 + row if which < 2 else c * 96 + row - 48
        flats[which][0:1, lanes] = first[at : at + 1, :]
        at = c * THIRD + row
        flats[which][1:2, lanes] = second[at : at + 1, :]
    for layer, slab in enumerate((first, second)):
        biases[layer : layer + 1, :] = slab[SMALL : SMALL + 1, 0:SHARD_BIAS]
        gains[layer : layer + 1, :] = slab[SMALL + 1 : SMALL + 2, 0:SHARD_GAIN]


def run_unpack(first, second, widths):
    return pl.pallas_call(
        unpack_kernel,
        out_shape=[jax.ShapeDtypeStruct((LAYERS, width), F32) for width in widths],
        in_specs=whole(2),
        out_specs=whole(6),
        name="unpack",
    )(first, second)


def swap(value, bits):
    return lax.ppermute(value, "fsdp", [(i, i ^ bits) for i in range(SLABS)])


XY_STEPS = (2, 4, 6)
Z_STEPS = (8, 16, 24)


def spread(value, steps):
    return [value] + [swap(value, bits) for bits in steps]


def gather_column(slab):
    return jnp.concatenate(spread(slab, Z_STEPS), axis=0)


def with_other_core(near):
    return near + [swap(part, 1) for part in near]


def across_cores(keep, send):
    return keep.astype(F32) + swap(send, 1).astype(F32)


def collect(total, steps):
    rows = total.shape[0] // 4
    mine = total[:rows]
    for place, bits in enumerate(steps):
        part = total[rows * (place + 1) : rows * (place + 2)]
        mine = mine + swap(part.astype(BF16), bits).astype(F32)
    return mine


def join(first, second):
    return jnp.concatenate([first.reshape(4, -1, 128), second.reshape(4, -1, 128)], axis=1).reshape(-1, 128)


def to_slabs(qkv, out, fc1, fc2, gains, biases):
    blocks = jnp.concatenate(
        [
            qkv.reshape(SLABS, 12, 3, D).transpose(0, 2, 1, 3).reshape(SLABS, 36, D),
            out.reshape(SLABS, 12, D),
            fc1.reshape(SLABS, 12, 4, D).transpose(0, 2, 1, 3).reshape(SLABS, 48, D),
            fc2.reshape(SLABS, 48, D),
        ],
        axis=1,
    )
    thirds = blocks.reshape(SLABS, THIRD, 3, 128).transpose(0, 2, 1, 3).reshape(SLABS, 3 * THIRD, 128)
    tail = jnp.zeros((SLABS, SLAB - SMALL, 128), blocks.dtype)
    tail = tail.at[:, 0, :SHARD_BIAS].set(biases.reshape(SLABS, SHARD_BIAS))
    tail = tail.at[:, 1, :SHARD_GAIN].set(gains.reshape(SLABS, SHARD_GAIN))
    return jnp.concatenate([thirds, tail], axis=1)


def from_slabs(slabs):
    blocks = slabs[:, :SMALL].reshape(SLABS, 3, THIRD, 128).transpose(0, 2, 1, 3).reshape(SLABS, THIRD, D)
    return (
        blocks[:, :36].reshape(SLABS, 3, 12, D).transpose(0, 2, 1, 3).reshape(-1),
        blocks[:, 36:48].reshape(-1),
        blocks[:, 48:96].reshape(SLABS, 4, 12, D).transpose(0, 2, 1, 3).reshape(-1),
        blocks[:, 96:].reshape(-1),
        slabs[:, SMALL + 1, :SHARD_GAIN].reshape(-1),
        slabs[:, SMALL, :SHARD_BIAS].reshape(-1),
    )


def plain_gather(flats, layer):
    return to_slabs(*(lax.all_gather(flat[layer], "fsdp", axis=0, tiled=True) for flat in flats))


def plain_pieces(slabs):
    return [
        jnp.concatenate([slabs[core + 2 * xy + 8 * z] for z in range(4)], axis=0)
        for core in range(2)
        for xy in range(4)
    ]


def plain_slabs(keep, send):
    halves = [half.reshape(4, 4, -1, 128).astype(F32) for half in (keep, send)]
    return jnp.stack([halves[d & 1][(d >> 1) & 3, d >> 3] for d in range(SLABS)])


def plain_totals(slabs):
    return [lax.psum_scatter(flat, "fsdp", scatter_dimension=0, tiled=True) for flat in from_slabs(slabs)]


def joined_slabs(mlp, attention):
    parts = []
    for c in range(3):
        parts += [attention[:, 48 * c : 48 * c + 48], mlp[:, 96 * c : 96 * c + 96]]
    return jnp.concatenate(parts + [attention[:, THIRD:]], axis=1)


def local(images, live_counts, qkv_weight, out_weight, fc1_weight, fc2_weight, norm_gains, biases, cotangent):
    flats = (qkv_weight, out_weight, fc1_weight, fc2_weight, norm_gains, biases)
    if lax.axis_size("fsdp") == SLABS:
        return local_tree(images, live_counts, flats, cotangent)
    me = jnp.zeros((1,), jnp.int32)
    pieces_b = plain_pieces(plain_gather(flats, 1))
    stream, weights, state = run_first_forward(me, images, plain_pieces(plain_gather(flats, 0)))
    activations, grad, *second = run_second_layer(me, live_counts, stream, cotangent, pieces_b)
    grad, gmix, *rest, mlp_keep, mlp_send = run_first_mlp_backward(me, grad, weights, state)
    gqkv = run_first_attention_backward(gmix, state)
    input_grad, *attention = run_first_projection_backward(me, images, grad, gqkv, rest, weights, state)
    first = joined_slabs(plain_slabs(mlp_keep, mlp_send), plain_slabs(*attention))
    results = [jnp.stack(both) for both in zip(plain_totals(first), plain_totals(plain_slabs(*second)))]
    return (activations, input_grad, *results)


def local_tree(images, live_counts, flats, cotangent):
    me = lax.axis_index("fsdp").astype(jnp.int32).reshape(1)
    slab_a, slab_b = run_pack(*flats)
    column_a, slab_b = lax.optimization_barrier((gather_column(slab_a), slab_b))
    own_a, *near_a = spread(column_a, XY_STEPS)
    near_a, column_b = lax.optimization_barrier((near_a, gather_column(slab_b)))
    stream, weights, state = run_first_forward(me, images, with_other_core([own_a] + near_a))
    near_b, stream = lax.optimization_barrier((spread(column_b, XY_STEPS), stream))
    pieces_b = with_other_core(near_b)
    activations, grad, *second = run_second_layer(me, live_counts, stream, cotangent, pieces_b)

    quarter = 4 * SLAB
    sides = across_cores(*(half[quarter : 3 * quarter] for half in second))
    sides, grad = lax.optimization_barrier((sides, grad))
    mine, corner = (across_cores(*(half[at : at + quarter] for half in second)) for at in (0, 3 * quarter))
    from_x, from_y = (swap(sides[quarter * n : quarter * n + quarter].astype(BF16), XY_STEPS[n]) for n in range(2))
    grad, gmix, *rest, mlp_keep, mlp_send = run_first_mlp_backward(me, grad, weights, state)
    from_x, from_y, corner, gmix, mlp_keep, mlp_send = lax.optimization_barrier(
        (from_x, from_y, corner, gmix, mlp_keep, mlp_send)
    )
    mlp = across_cores(mlp_keep, mlp_send)
    second = mine + from_x.astype(F32) + from_y.astype(F32) + swap(corner.astype(BF16), XY_STEPS[2]).astype(F32)
    gqkv = run_first_attention_backward(gmix, state)
    second, mlp, gqkv = lax.optimization_barrier((second, mlp, gqkv))

    second, mlp = collect(second, Z_STEPS), collect(mlp, XY_STEPS)
    input_grad, *attention = run_first_projection_backward(me, images, grad, gqkv, rest, weights, state)
    second, mlp, attention = lax.optimization_barrier((second, mlp, attention))

    attention = collect(across_cores(*attention), XY_STEPS)
    first = collect(join(mlp, attention), Z_STEPS)
    results = run_unpack(first, second, [flat.shape[1] for flat in flats])
    return (activations, input_grad, *results)


def solution(mesh):
    flat = P(None, "fsdp")
    image = P("fsdp", None, None)
    return jax.shard_map(
        local,
        mesh=mesh,
        in_specs=(image, P("fsdp")) + (flat,) * 6 + (image,),
        out_specs=(image, image) + (flat,) * 6,
        check_vma=False,
    )
```

```python
import jax
import jax.numpy as jnp
from jax import lax
from jax.experimental import pallas as pl
from jax.experimental.pallas import tpu as pltpu
from jax.sharding import PartitionSpec as P

D = 384
FF = 1536
SEQ = 197
HEAD = 64
LAYERS = 2
NORM_EPS = 1e-06
ROOT_HALF = 0.7071067811865476
INV_ROOT_TAU = 0.3989422804014327

IMGS = 3
ROWS = 208
R = IMGS * ROWS
CHUNK = 48
CHUNKS = R // CHUNK
PAIRS = 3

SLABS = 32
THIRD = 144
SMALL = 3 * THIRD
SLAB = SMALL + 16
BLOCKS = 8
SHARD_BIAS = 120
SHARD_GAIN = 24
BIAS = 6 * D + FF
GAIN = 2 * D

F32 = jnp.float32
BF16 = jnp.bfloat16
VMEM_LIMIT = 56 * 1024 * 1024


def dot_nn(a, b):
    return lax.dot_general(a, b, (((1,), (0,)), ((), ())), preferred_element_type=F32)


def dot_nt(a, b):
    return lax.dot_general(a, b, (((1,), (1,)), ((), ())), preferred_element_type=F32)


def dot_tn(a, b):
    return lax.dot_general(a, b, (((0,), (0,)), ((), ())), preferred_element_type=F32)


def chunk_rows(i):
    return pl.ds(pl.multiple_of(i * CHUNK, CHUNK), CHUNK)


def block_rows(j):
    return pl.ds(pl.multiple_of(j * D, D), D)


def image_rows(i):
    return pl.ds(pl.multiple_of(i * ROWS, 16), ROWS)


def pair_lanes(p):
    return pl.ds(pl.multiple_of(p * 128, 128), 128)


def normalize(x):
    centred = x - jnp.mean(x, axis=-1, keepdims=True)
    inv_std = lax.rsqrt(jnp.mean(centred * centred, axis=-1, keepdims=True) + NORM_EPS)
    return centred * inv_std, inv_std


def digits(index, size):
    whole = jnp.floor((index.astype(F32) + 0.5) * (1.0 / size)).astype(jnp.int32)
    return whole, index - whole * size


def order_codes(shape, axis):
    index = lax.broadcasted_iota(jnp.int32, shape, axis)
    block, rest = digits(index, 48)
    dev, row = digits(rest, 12)
    return (block * 4 + dev) * 12 + row


def slab_codes(shape, axis, low, blocks):
    index = lax.broadcasted_iota(jnp.int32, shape, axis)
    rel, rest = digits(index, 12 * blocks)
    block, row = digits(rest, 12)
    dev = jnp.bitwise_xor(rel, low)
    return (block * 4 + dev) * 12 + row


def owner_mask(size, per_owner):
    lane = lax.broadcasted_iota(jnp.int32, (1, size), 1)
    owner, place = digits(lane, per_owner)
    rows = lax.broadcasted_iota(jnp.int32, (SLABS, size), 0)
    return rows == owner, place


def place_matrix(place, size):
    rows = lax.broadcasted_iota(jnp.int32, (128, size), 0)
    return jnp.where(rows == place, 1.0, 0.0).astype(BF16)


def assemble(me, pieces, w, w2, bias_row, gain_row, rhs, small):
    low = jnp.bitwise_and(me, 3)
    order = jnp.where(
        order_codes((D, 1), 0) == slab_codes((1, D), 1, low, BLOCKS), 1.0, 0.0
    ).astype(BF16)

    for zr in range(4):
        for yr in range(2):
            g = jnp.bitwise_xor(lax.shift_right_logical(me, 2), yr + 2 * zr)
            for xr in range(2):
                for cr in range(2):
                    xy = xr + 2 * yr
                    piece, base = pieces[4 * cr + xy], zr * SLAB
                    d = jnp.bitwise_xor(me, cr + 2 * xy + 8 * zr)
                    s = xr * 2 + cr
                    for c in range(3):
                        lanes = slice(128 * c, 128 * c + 128)
                        start = base + c * THIRD
                        rhs[96 * s : 96 * s + 96, lanes] = piece[start : start + 96, :]
                        w2[pl.ds(pl.multiple_of(48 * d, 16), 48), lanes] = piece[start + 96 : start + THIRD, :]
                    tail = piece[base + SMALL : base + SLAB, :].astype(F32)
                    small[0, pl.ds(d, 1), :] = tail[0:1, :]
                    small[1, pl.ds(d, 1), :] = tail[1:2, :]
            sorted_rows = dot_nn(order, rhs[...]).astype(BF16)
            for b in range(BLOCKS):
                w[b, pl.ds(pl.multiple_of(48 * g, 16), 48), :] = sorted_rows[48 * b : 48 * b + 48]
    for slot, size, per_owner, row in ((0, BIAS, SHARD_BIAS, bias_row), (1, GAIN, SHARD_GAIN, gain_row)):
        mine, place = owner_mask(size, per_owner)
        spread = dot_nn(small[slot].astype(BF16), place_matrix(place, size))
        row[...] = jnp.sum(jnp.where(mine, spread, 0.0), axis=0, keepdims=True)


def slab_rows(blocks, with_w2, with_small):
    return 3 * (12 * blocks + 48 * with_w2) + 16 * with_small


def disperse(me, dw, dw2, bias_row, gain_row, wires, rhs, small):
    blocks = dw.shape[0]
    size = 48 * blocks
    third = slab_rows(blocks, dw2 is not None, False) // 3
    stride = slab_rows(blocks, dw2 is not None, bias_row is not None)
    low = jnp.bitwise_and(me, 3)
    order = jnp.where(
        slab_codes((size, 1), 0, low, blocks) == order_codes((1, size), 1), 1.0, 0.0
    ).astype(BF16)
    if bias_row is not None:
        for slot, width, per_owner, row in ((0, BIAS, SHARD_BIAS, bias_row), (1, GAIN, SHARD_GAIN, gain_row)):
            mine, place = owner_mask(width, per_owner)
            spread = jnp.where(mine, row[...], 0.0).astype(BF16)
            small[slot] = dot_nt(spread, place_matrix(place, width))
    head_row = lax.broadcasted_iota(jnp.int32, (16, 128), 0)

    def group(zr, carry):
        for yr in range(2):
            g = jnp.bitwise_xor(lax.shift_right_logical(me, 2), yr + 2 * zr)
            for b in range(blocks):
                rhs[48 * b : 48 * b + 48, :] = dw[b, pl.ds(pl.multiple_of(48 * g, 16), 48), :]
            slabs = dot_nn(order, rhs[0:size, :]).astype(BF16)
            for xr in range(2):
                for cr in range(2):
                    out = wires[cr]
                    xy = xr + 2 * yr
                    d = jnp.bitwise_xor(me, cr + 2 * xy + 8 * zr)
                    s = xr * 2 + cr
                    base = pl.multiple_of(xy * (4 * stride) + zr * stride, 16)
                    for c in range(3):
                        lanes = slice(128 * c, 128 * c + 128)
                        start = base + c * third
                        rows = 12 * blocks
                        out[pl.ds(start, rows), :] = slabs[rows * s : rows * s + rows, lanes]
                        if dw2 is not None:
                            out[pl.ds(start + rows, 48), :] = dw2[pl.ds(pl.multiple_of(48 * d, 16), 48), lanes]
                    if bias_row is not None:
                        tail = jnp.where(
                            head_row == 0,
                            small[0, pl.ds(d, 1), :],
                            jnp.where(head_row == 1, small[1, pl.ds(d, 1), :], 0.0),
                        )
                        out[pl.ds(base + 3 * third, 16), :] = tail.astype(BF16)
        return carry

    lax.fori_loop(0, 4, group, 0, unroll=True)


def forward(x, w, w2, bias_row, gain_row, xna, qkv, probs, mixed, middle, xnb, act, slope, tmp, rolled):
    def norm_a(i, carry):
        rows = chunk_rows(i)
        normal, _ = normalize(x[rows, :])
        xna[rows, :] = (normal * gain_row[:, :D] + bias_row[:, :D]).astype(BF16)
        return carry

    lax.fori_loop(0, CHUNKS, norm_a, 0, unroll=True)
    for b in range(3):
        part = dot_nn(xna[...], w[b])
        if b == 0:
            part = part + bias_row[:, D : 2 * D]
        if b == 2:
            part = part + bias_row[:, 2 * D : 3 * D]
        qkv[b] = part.astype(BF16)

    lane = lax.broadcasted_iota(jnp.int32, (1, 128), 1)
    first = lane < HEAD
    halves = (first.astype(F32).astype(BF16), 1 - first.astype(F32).astype(BF16))
    real_key = lax.broadcasted_iota(jnp.int32, (ROWS, 1), 0) < SEQ

    def image_attention(img, carry):
        rows = image_rows(img)

        def pair_attention(pair, inner):
            lanes = pair_lanes(pair)
            q, k, v = qkv[0, rows, lanes], qkv[1, rows, lanes], qkv[2, rows, lanes]
            outs = []
            for h in range(2):
                scores = dot_nt(k, q * halves[h]) * (HEAD**-0.5)
                scores = jnp.where(real_key, scores, -1e30)
                raised = jnp.exp(scores - jnp.max(scores, axis=0, keepdims=True))
                share = raised * (1.0 / jnp.sum(raised, axis=0, keepdims=True))
                share = share.astype(BF16)
                probs[(img * PAIRS + pair) * 2 + h] = share
                outs.append(dot_tn(share, v))
            mixed[rows, lanes] = jnp.where(first, outs[0], outs[1]).astype(BF16)
            return inner

        return lax.fori_loop(0, PAIRS, pair_attention, carry, unroll=True)

    lax.fori_loop(0, IMGS, image_attention, 0, unroll=1 if rolled else IMGS)
    middle[...] = x[...] + (dot_nn(mixed[...], w[3]) + bias_row[:, 3 * D : 4 * D])

    def norm_b(i, carry):
        rows = chunk_rows(i)
        normal, _ = normalize(middle[rows, :])
        xnb[rows, :] = (normal * gain_row[:, D:] + bias_row[:, 4 * D : 5 * D]).astype(BF16)
        return carry

    lax.fori_loop(0, CHUNKS, norm_b, 0, unroll=True)

    def hidden(j, carry):
        tmp[...] = dot_nn(xnb[...], w[4 + j])
        shift = bias_row[:, pl.ds(pl.multiple_of(6 * D + j * D, 128), D)]

        def gelu(i, inner):
            rows = chunk_rows(i)
            pre = tmp[rows, :] + shift
            half = 0.5 * (1.0 + lax.erf(pre * ROOT_HALF))
            act[j, rows, :] = (pre * half).astype(BF16)
            slope[j, rows, :] = (half + pre * jnp.exp(-0.5 * pre * pre) * INV_ROOT_TAU).astype(BF16)
            return inner

        return lax.fori_loop(0, CHUNKS, gelu, carry, unroll=True)

    lax.fori_loop(0, 4, hidden, 0, unroll=1 if rolled else 4)
    tmp[...] = middle[...] + bias_row[:, 5 * D : 6 * D]
    for j in range(4):
        tmp[...] += dot_nn(act[j], w2[D * j : D * j + D, :])


def column_total(values):
    return jnp.sum(values.astype(F32), axis=0, keepdims=True)


def norm_back(source, gain, grad, tmp, low):
    def step(i, totals):
        rows = chunk_rows(i)
        back = tmp[rows, :]
        normal, inv_std = normalize(source[rows, :])
        scaled = back * gain
        first_mean = jnp.mean(scaled, axis=-1, keepdims=True)
        cross_mean = jnp.mean(scaled * normal, axis=-1, keepdims=True)
        result = grad[rows, :] + inv_std * (scaled - first_mean - normal * cross_mean)
        grad[rows, :] = result
        result_low = result.astype(BF16)
        if low is not None:
            low[rows, :] = result_low
        return (
            totals[0] + jnp.sum(back * normal, axis=0, keepdims=True),
            totals[1] + jnp.sum(back, axis=0, keepdims=True),
            totals[2] + jnp.sum(result_low.astype(F32), axis=0, keepdims=True),
        )

    zero = jnp.zeros((1, D), F32)
    return lax.fori_loop(0, CHUNKS, step, (zero, zero, zero), unroll=True)


def mlp_backward(w, w2, gain_row, mixed, middle, xnb, act, slope, grad, low, gpre, gmix, tmp, dw, dw_out, dw2, dbias, dgain):
    low[...] = grad[...].astype(BF16)
    dbias[:, 5 * D : 6 * D] = column_total(low[...])

    def hidden(j, carry):
        dw2[block_rows(j), :] = dot_tn(act[j], low[...]).astype(BF16)
        pre = (dot_nt(low[...], w2[block_rows(j), :]) * slope[j].astype(F32)).astype(BF16)
        gpre[...] = pre
        dbias[:, pl.ds(pl.multiple_of(6 * D + j * D, 128), D)] = column_total(gpre[...])
        dw[j] = dot_tn(xnb[...], gpre[...]).astype(BF16)
        part = dot_nt(gpre[...], w[4 + j])
        tmp[...] = jnp.where(j == 0, part, tmp[...] + part)
        return carry

    lax.fori_loop(0, 4, hidden, 0, unroll=True)
    gain_two, shift_two, bias_out = norm_back(middle, gain_row[:, D:], grad, tmp, low)
    dgain[:, D:] = gain_two
    dbias[:, 4 * D : 5 * D] = shift_two
    dbias[:, 3 * D : 4 * D] = bias_out
    dw_out[...] = dot_tn(mixed[...], low[...]).astype(BF16)
    gmix[...] = dot_nt(low[...], w[3]).astype(BF16)


def attention_backward(qkv, probs, gmix, gqkv):
    lane = lax.broadcasted_iota(jnp.int32, (1, 128), 1)
    first = lane < HEAD
    halves = (first.astype(F32).astype(BF16), 1 - first.astype(F32).astype(BF16))

    def image_attention(img, carry):
        rows = image_rows(img)

        def pair_attention(pair, inner):
            lanes = pair_lanes(pair)
            q, k, v = qkv[0, rows, lanes], qkv[1, rows, lanes], qkv[2, rows, lanes]
            gm = gmix[rows, lanes]
            grads = ([], [], [])
            for h in range(2):
                share = probs[(img * PAIRS + pair) * 2 + h]
                grad_share = dot_nt(v, gm * halves[h])
                full = share.astype(F32)
                row_dot = jnp.sum(full * grad_share, axis=0, keepdims=True)
                grad_scores = (full * (grad_share - row_dot)).astype(BF16)
                grads[0].append(dot_tn(grad_scores, k) * (HEAD**-0.5))
                grads[1].append(dot_nn(grad_scores, q) * (HEAD**-0.5))
                grads[2].append(dot_nn(share, gm))
            for b in range(3):
                gqkv[b, rows, lanes] = jnp.where(first, grads[b][0], grads[b][1]).astype(BF16)
            return inner

        return lax.fori_loop(0, PAIRS, pair_attention, carry, unroll=True)

    lax.fori_loop(0, IMGS, image_attention, 0, unroll=True)


def projection_backward(x, w, gain_row, xna, gqkv, grad, tmp, dw, dbias, dgain):
    for b in range(3):
        dw[b] = dot_tn(xna[...], gqkv[b]).astype(BF16)
        part = dot_nt(gqkv[b], w[b])
        tmp[...] = part if b == 0 else tmp[...] + part
    dbias[:, D : 2 * D] = column_total(gqkv[0])
    dbias[:, 2 * D : 3 * D] = column_total(gqkv[2])
    gain_one, shift_one, _ = norm_back(x, gain_row[:, :D], grad, tmp, None)
    dgain[:, :D] = gain_one
    dbias[:, :D] = shift_one


def load_images(images, x):
    x[...] = jnp.zeros_like(x)
    for i in range(IMGS):
        x[ROWS * i : ROWS * i + SEQ, :] = images[i].astype(F32)


STATE = (
    ((R, D), BF16),
    ((3, R, D), BF16),
    ((IMGS * PAIRS * 2, ROWS, ROWS), BF16),
    ((R, D), BF16),
    ((R, D), F32),
    ((R, D), BF16),
    ((4, R, D), BF16),
    ((4, R, D), BF16),
)
WEIGHTS = (
    ((BLOCKS, D, D), BF16),
    ((FF, D), BF16),
    ((1, BIAS), F32),
    ((1, GAIN), F32),
)
BIAS_ROW = ((1, BIAS), F32)
GAIN_ROW = ((1, GAIN), F32)
HALF_BLOCKS = ((BLOCKS // 2, D, D), BF16)
MOVE_SCRATCH = (((D, D), BF16), ((2, SLABS, 128), F32))


def wires(*part):
    return [jax.ShapeDtypeStruct((16 * slab_rows(*part), 128), BF16)] * 2


def shapes(specs):
    return [jax.ShapeDtypeStruct(*spec) for spec in specs]


def scratch(specs):
    return [pltpu.VMEM(*spec) for spec in specs]


def first_forward_kernel(*refs):
    me, images, pieces, refs = refs[0][0], refs[1], refs[2:10], refs[10:]
    stream, weights, state = refs[0], refs[1:5], refs[5:13]
    x, rhs, small = refs[13:]
    assemble(me, pieces, *weights, rhs, small)
    load_images(images, x)
    forward(x, *weights, *state, stream, True)


def second_layer_kernel(*refs):
    me, live, stream, cotangent, pieces, refs = refs[0][0], refs[1], refs[2], refs[3], refs[4:12], refs[12:]
    activations, grad, sent, refs = refs[0], refs[1], refs[2:4], refs[4:]
    weights, state, refs = refs[:4], refs[4:12], refs[12:]
    low, gpre, gqkv, gmix, tmp, dw, dw2, dbias, dgain, rhs, small = refs
    assemble(me, pieces, *weights, rhs, small)
    forward(stream, *weights, *state, grad, False)
    for i in range(IMGS):
        alive = jnp.where(live[i] > 0, 1.0, 0.0)
        activations[i] = (grad[ROWS * i : ROWS * i + SEQ, :] * alive).astype(BF16)
    load_images(cotangent, grad)
    for i in range(IMGS):
        alive = jnp.where(live[i] > 0, 1.0, 0.0)
        grad[ROWS * i : ROWS * i + ROWS, :] = grad[ROWS * i : ROWS * i + ROWS, :] * alive
    w, w2, _, gain_row = weights
    xna, qkv, probs, mixed, middle, xnb, act, slope = state
    mlp_backward(
        w, w2, gain_row, mixed, middle, xnb, act, slope, grad, low, gpre, gmix, tmp, dw.at[4:8], dw.at[3], dw2, dbias, dgain
    )
    attention_backward(qkv, probs, gmix, gqkv)
    projection_backward(stream, w, gain_row, xna, gqkv, grad, tmp, dw, dbias, dgain)
    disperse(me, dw, dw2, dbias, dgain, sent, rhs, small)


def first_mlp_backward_kernel(
    me, grad_in, w, w2, gain_row, mixed, middle, xnb, act, slope, grad, gmix, dw_out, dbias, dgain, *refs
):
    sent, (low, gpre, tmp, dw, dw2, rhs) = refs[:2], refs[2:]
    grad[...] = grad_in[...]
    dbias[...] = jnp.zeros_like(dbias)
    dgain[...] = jnp.zeros_like(dgain)
    mlp_backward(
        w, w2, gain_row, mixed, middle, xnb, act, slope, grad, low, gpre, gmix, tmp, dw, dw_out, dw2, dbias, dgain
    )
    disperse(me[0], dw, dw2, None, None, sent, rhs, None)


def first_attention_backward_kernel(qkv, probs, gmix, gqkv):
    attention_backward(qkv, probs, gmix, gqkv)


def first_projection_backward_kernel(
    me, images, grad_in, gqkv, dw_out, dbias_in, dgain_in, w, gain_row, xna, input_grad, *refs
):
    sent, (x, grad, tmp, dw, dbias, dgain, rhs, small) = refs[:2], refs[2:]
    load_images(images, x)
    grad[...] = grad_in[...]
    dbias[...] = dbias_in[...]
    dgain[...] = dgain_in[...]
    dw[3] = dw_out[...]
    projection_backward(x, w, gain_row, xna, gqkv, grad, tmp, dw, dbias, dgain)
    for i in range(IMGS):
        input_grad[i] = grad[ROWS * i : ROWS * i + SEQ, :].astype(BF16)
    disperse(me[0], dw, None, dbias, dgain, sent, rhs, small)


def whole(count):
    return [pl.BlockSpec(memory_space=pltpu.VMEM)] * count


def scalar(count):
    return [pl.BlockSpec(memory_space=pltpu.SMEM)] * count


def params():
    return pltpu.CompilerParams(vmem_limit_bytes=VMEM_LIMIT)


def cost(flops):
    return pl.CostEstimate(flops=flops, bytes_accessed=20_000_000, transcendentals=0)


def run_first_forward(me, images, pieces):
    outs = [jax.ShapeDtypeStruct((R, D), F32)] + shapes(WEIGHTS) + shapes(STATE)
    out = pl.pallas_call(
        first_forward_kernel,
        out_shape=outs,
        in_specs=scalar(1) + whole(9),
        out_specs=whole(len(outs)),
        scratch_shapes=scratch((((R, D), F32),) + MOVE_SCRATCH),
        compiler_params=params(),
        cost_estimate=cost(33_000_000_000),
        name="first_forward",
    )(me, images, *pieces)
    return out[0], out[1:5], out[5:]


def run_second_layer(me, live, stream, cotangent, pieces):
    outs = [jax.ShapeDtypeStruct(cotangent.shape, BF16), jax.ShapeDtypeStruct((R, D), F32)]
    outs += wires(BLOCKS, True, True)
    low, full = ((R, D), BF16), ((R, D), F32)
    back = (low, low, ((3, R, D), BF16), low, full, ((BLOCKS, D, D), BF16), ((FF, D), BF16), BIAS_ROW, GAIN_ROW)
    return pl.pallas_call(
        second_layer_kernel,
        out_shape=outs,
        in_specs=scalar(2) + whole(10),
        out_specs=whole(len(outs)),
        scratch_shapes=scratch(WEIGHTS + STATE + back + MOVE_SCRATCH),
        compiler_params=params(),
        cost_estimate=cost(65_000_000_000),
        name="second_layer",
    )(me, live, stream, cotangent, *pieces)


def run_first_mlp_backward(me, grad, weights, state):
    w, w2, _, gain_row = weights
    low, full = ((R, D), BF16), ((R, D), F32)
    outs = shapes((full, low, ((D, D), BF16), BIAS_ROW, GAIN_ROW)) + wires(BLOCKS // 2, True, False)
    return pl.pallas_call(
        first_mlp_backward_kernel,
        out_shape=outs,
        in_specs=scalar(1) + whole(9),
        out_specs=whole(len(outs)),
        scratch_shapes=scratch((low, low, full, HALF_BLOCKS, ((FF, D), BF16), MOVE_SCRATCH[0])),
        compiler_params=params(),
        cost_estimate=cost(20_000_000_000),
        name="first_mlp_backward",
    )(me, grad, w, w2, gain_row, *state[3:])


def run_first_attention_backward(gmix, state):
    return pl.pallas_call(
        first_attention_backward_kernel,
        out_shape=jax.ShapeDtypeStruct((3, R, D), BF16),
        in_specs=whole(3),
        out_specs=whole(1)[0],
        compiler_params=params(),
        cost_estimate=cost(12_000_000_000),
        name="first_attention_backward",
    )(state[1], state[2], gmix)


def run_first_projection_backward(me, images, grad, gqkv, rest, weights, state):
    w, _, _, gain_row = weights
    full = ((R, D), F32)
    outs = [jax.ShapeDtypeStruct(images.shape, BF16)] + wires(BLOCKS // 2, False, True)
    return pl.pallas_call(
        first_projection_backward_kernel,
        out_shape=outs,
        in_specs=scalar(1) + whole(9),
        out_specs=whole(len(outs)),
        scratch_shapes=scratch((full, full, full, HALF_BLOCKS, BIAS_ROW, GAIN_ROW) + MOVE_SCRATCH),
        compiler_params=params(),
        cost_estimate=cost(10_000_000_000),
        name="first_projection_backward",
    )(me, images, grad, gqkv, *rest, w, gain_row, state[0])


def chunk_table():
    table = []
    for c in range(3):
        for i in range(12):
            for b in range(3):
                table.append((0, i * 9 + b * 3 + c, c, b * 12 + i))
            table.append((1, i * 3 + c, c, 36 + i))
            for b in range(4):
                table.append((2, i * 12 + b * 3 + c, c, 48 + b * 12 + i))
        for i in range(48):
            table.append((3, i * 3 + c, c, 96 + i))
    return table


def pack_kernel(qkv, out, fc1, fc2, gains, biases, slab_a, slab_b, stage_a, stage_b):
    flats, stages = (qkv, out, fc1, fc2), (stage_a, stage_b)
    for stage in stages:
        stage[SMALL:SLAB, :] = jnp.zeros((SLAB - SMALL, 128), F32)
    for which, piece, c, row in chunk_table():
        both = flats[which][:, 128 * piece : 128 * piece + 128].astype(F32)
        row += c * THIRD
        for layer in range(LAYERS):
            stages[layer][row : row + 1, :] = both[layer : layer + 1]
    for layer in range(LAYERS):
        stages[layer][SMALL : SMALL + 1, 0:SHARD_BIAS] = biases[...].astype(F32)[layer : layer + 1]
        stages[layer][SMALL + 1 : SMALL + 2, 0:SHARD_GAIN] = gains[...].astype(F32)[layer : layer + 1]
    slab_a[...] = stage_a[...].astype(BF16)
    slab_b[...] = stage_b[...].astype(BF16)


def run_pack(qkv, out, fc1, fc2, gains, biases):
    return pl.pallas_call(
        pack_kernel,
        out_shape=[jax.ShapeDtypeStruct((SLAB, 128), BF16)] * 2,
        in_specs=whole(6),
        out_specs=whole(2),
        scratch_shapes=[pltpu.VMEM((SLAB, 128), F32)] * 2,
        name="pack",
    )(qkv, out, fc1, fc2, gains, biases)


def unpack_kernel(first, second, *refs):
    flats, (gains, biases) = refs[:4], refs[4:]
    start = slab_rows(BLOCKS // 2, True, False)
    for which, piece, c, row in chunk_table():
        lanes = slice(128 * piece, 128 * piece + 128)
        at = start + c * 48 + row if which < 2 else c * 96 + row - 48
        flats[which][0:1, lanes] = first[at : at + 1, :]
        at = c * THIRD + row
        flats[which][1:2, lanes] = second[at : at + 1, :]
    for layer, slab in enumerate((first, second)):
        biases[layer : layer + 1, :] = slab[SMALL : SMALL + 1, 0:SHARD_BIAS]
        gains[layer : layer + 1, :] = slab[SMALL + 1 : SMALL + 2, 0:SHARD_GAIN]


def run_unpack(first, second, widths):
    return pl.pallas_call(
        unpack_kernel,
        out_shape=[jax.ShapeDtypeStruct((LAYERS, width), F32) for width in widths],
        in_specs=whole(2),
        out_specs=whole(6),
        name="unpack",
    )(first, second)


def swap(value, bits):
    return lax.ppermute(value, "fsdp", [(i, i ^ bits) for i in range(SLABS)])


XY_STEPS = (2, 4, 6)
Z_STEPS = (8, 16, 24)


def spread(value, steps):
    return [value] + [swap(value, bits) for bits in steps]


def gather_column(slab):
    return jnp.concatenate(spread(slab, Z_STEPS), axis=0)


def with_other_core(near):
    return near + [swap(part, 1) for part in near]


def across_cores(keep, send):
    return keep.astype(F32) + swap(send, 1).astype(F32)


def collect(total, steps):
    rows = total.shape[0] // 4
    mine = total[:rows]
    for place, bits in enumerate(steps):
        part = total[rows * (place + 1) : rows * (place + 2)]
        mine = mine + swap(part.astype(BF16), bits).astype(F32)
    return mine


def join(first, second):
    return jnp.concatenate([first.reshape(4, -1, 128), second.reshape(4, -1, 128)], axis=1).reshape(-1, 128)


def to_slabs(qkv, out, fc1, fc2, gains, biases):
    blocks = jnp.concatenate(
        [
            qkv.reshape(SLABS, 12, 3, D).transpose(0, 2, 1, 3).reshape(SLABS, 36, D),
            out.reshape(SLABS, 12, D),
            fc1.reshape(SLABS, 12, 4, D).transpose(0, 2, 1, 3).reshape(SLABS, 48, D),
            fc2.reshape(SLABS, 48, D),
        ],
        axis=1,
    )
    thirds = blocks.reshape(SLABS, THIRD, 3, 128).transpose(0, 2, 1, 3).reshape(SLABS, 3 * THIRD, 128)
    tail = jnp.zeros((SLABS, SLAB - SMALL, 128), blocks.dtype)
    tail = tail.at[:, 0, :SHARD_BIAS].set(biases.reshape(SLABS, SHARD_BIAS))
    tail = tail.at[:, 1, :SHARD_GAIN].set(gains.reshape(SLABS, SHARD_GAIN))
    return jnp.concatenate([thirds, tail], axis=1)


def from_slabs(slabs):
    blocks = slabs[:, :SMALL].reshape(SLABS, 3, THIRD, 128).transpose(0, 2, 1, 3).reshape(SLABS, THIRD, D)
    return (
        blocks[:, :36].reshape(SLABS, 3, 12, D).transpose(0, 2, 1, 3).reshape(-1),
        blocks[:, 36:48].reshape(-1),
        blocks[:, 48:96].reshape(SLABS, 4, 12, D).transpose(0, 2, 1, 3).reshape(-1),
        blocks[:, 96:].reshape(-1),
        slabs[:, SMALL + 1, :SHARD_GAIN].reshape(-1),
        slabs[:, SMALL, :SHARD_BIAS].reshape(-1),
    )


def plain_gather(flats, layer):
    return to_slabs(*(lax.all_gather(flat[layer], "fsdp", axis=0, tiled=True) for flat in flats))


def plain_pieces(slabs):
    return [
        jnp.concatenate([slabs[core + 2 * xy + 8 * z] for z in range(4)], axis=0)
        for core in range(2)
        for xy in range(4)
    ]


def plain_slabs(keep, send):
    halves = [half.reshape(4, 4, -1, 128).astype(F32) for half in (keep, send)]
    return jnp.stack([halves[d & 1][(d >> 1) & 3, d >> 3] for d in range(SLABS)])


def plain_totals(slabs):
    return [lax.psum_scatter(flat, "fsdp", scatter_dimension=0, tiled=True) for flat in from_slabs(slabs)]


def joined_slabs(mlp, attention):
    parts = []
    for c in range(3):
        parts += [attention[:, 48 * c : 48 * c + 48], mlp[:, 96 * c : 96 * c + 96]]
    return jnp.concatenate(parts + [attention[:, THIRD:]], axis=1)


def local(images, live_counts, qkv_weight, out_weight, fc1_weight, fc2_weight, norm_gains, biases, cotangent):
    flats = (qkv_weight, out_weight, fc1_weight, fc2_weight, norm_gains, biases)
    if lax.axis_size("fsdp") == SLABS:
        return local_tree(images, live_counts, flats, cotangent)
    me = jnp.zeros((1,), jnp.int32)
    pieces_b = plain_pieces(plain_gather(flats, 1))
    stream, weights, state = run_first_forward(me, images, plain_pieces(plain_gather(flats, 0)))
    activations, grad, *second = run_second_layer(me, live_counts, stream, cotangent, pieces_b)
    grad, gmix, *rest, mlp_keep, mlp_send = run_first_mlp_backward(me, grad, weights, state)
    gqkv = run_first_attention_backward(gmix, state)
    input_grad, *attention = run_first_projection_backward(me, images, grad, gqkv, rest, weights, state)
    first = joined_slabs(plain_slabs(mlp_keep, mlp_send), plain_slabs(*attention))
    results = [jnp.stack(both) for both in zip(plain_totals(first), plain_totals(plain_slabs(*second)))]
    return (activations, input_grad, *results)


def local_tree(images, live_counts, flats, cotangent):
    me = lax.axis_index("fsdp").astype(jnp.int32).reshape(1)
    slab_a, slab_b = run_pack(*flats)
    column_a, slab_b = lax.optimization_barrier((gather_column(slab_a), slab_b))
    own_a, *near_a = spread(column_a, XY_STEPS)
    near_a, column_b = lax.optimization_barrier((near_a, gather_column(slab_b)))
    stream, weights, state = run_first_forward(me, images, with_other_core([own_a] + near_a))
    near_b, stream = lax.optimization_barrier((spread(column_b, XY_STEPS), stream))
    pieces_b = with_other_core(near_b)
    activations, grad, *second = run_second_layer(me, live_counts, stream, cotangent, pieces_b)

    quarter = 4 * SLAB
    sides = across_cores(*(half[quarter : 3 * quarter] for half in second))
    sides, grad = lax.optimization_barrier((sides, grad))
    mine, corner = (across_cores(*(half[at : at + quarter] for half in second)) for at in (0, 3 * quarter))
    from_x, from_y = (swap(sides[quarter * n : quarter * n + quarter].astype(BF16), XY_STEPS[n]) for n in range(2))
    grad, gmix, *rest, mlp_keep, mlp_send = run_first_mlp_backward(me, grad, weights, state)
    from_x, from_y, corner, gmix, mlp_keep, mlp_send = lax.optimization_barrier(
        (from_x, from_y, corner, gmix, mlp_keep, mlp_send)
    )
    mlp = across_cores(mlp_keep, mlp_send)
    second = mine + from_x.astype(F32) + from_y.astype(F32) + swap(corner.astype(BF16), XY_STEPS[2]).astype(F32)
    gqkv = run_first_attention_backward(gmix, state)
    second, mlp, gqkv = lax.optimization_barrier((second, mlp, gqkv))

    second, mlp = collect(second, Z_STEPS), collect(mlp, XY_STEPS)
    input_grad, *attention = run_first_projection_backward(me, images, grad, gqkv, rest, weights, state)
    second, mlp, attention = lax.optimization_barrier((second, mlp, attention))

    attention = collect(across_cores(*attention), XY_STEPS)
    first = collect(join(mlp, attention), Z_STEPS)
    results = run_unpack(first, second, [flat.shape[1] for flat in flats])
    return (activations, input_grad, *results)


def solution(mesh):
    flat = P(None, "fsdp")
    image = P("fsdp", None, None)
    return jax.shard_map(
        local,
        mesh=mesh,
        in_specs=(image, P("fsdp")) + (flat,) * 6 + (image,),
        out_specs=(image, image) + (flat,) * 6,
        check_vma=False,
    )
```
